128 devices in a mesh: grp: 8 (over x, core), blk: 16 (over y, z).
Axes of the slice: x: 4, y: 4, z: 4, core: 2. Of those that a mesh axis runs over, the one named last changes fastest.
Arguments:
- embeddings: bfloat16 [65536, 768], P(('grp', 'blk'))
- labels: int32 [65536], P(('grp', 'blk')), may hold values from 0 to 511, as said below
- cluster_slot: int32 [512], replicated, may hold values from 0 to 511, as said below
Outputs:
- max_similarity: float32 [65536], P(('grp', 'blk'))
- duplicate_mass: float32 [65536], P(('grp', 'blk'))
The draws below stay inside these ranges and needn't reach their ends.
Inputs may be any that keep to these rules, and one draw needn't show every extreme that they name: `labels`: at most 128 of one device's 512 documents lie in clusters of one group, and on every device some group holds exactly 128 of them. `cluster_slot`: A permutation of the clusters' slots.
All inputs are finite; a program needn't handle non-finite values.
Results may differ from the reference program's by a relative error of at most 0.00053.
Values may be sent and summed in bfloat16 or wider, within the bound.
No kernel may reach another device: no remote copies, remote signals or barrier semaphores. Data moves between devices by JAX's collectives and lax.ppermute only.
A program may use at most 128 MiB of HBM per device.

```python
import math
import jax
import jax.numpy as jnp
from jax import lax

D = 768
CL_GRP = 64
ROWS_DEV = 512
CAP = 128
DOCS = 65536
CLUSTERS = 512
N_GRP = 8


def routing(key):
    device_keys = jax.random.split(jax.random.fold_in(key, 11), DOCS // ROWS_DEV)
    group_count = CLUSTERS // CL_GRP

    def one_device(device_key):
        first_key, second_key, third_key = jax.random.split(device_key, 3)
        busy_group = jax.random.randint(first_key, (), 0, group_count)
        slot_index = jnp.arange(group_count * CAP, dtype=jnp.int32)
        group_of = slot_index // CAP
        score_ints = jax.random.permutation(second_key, group_count * CAP).astype(jnp.int32)
        score_ints = jnp.where(group_of == busy_group, slot_index - group_count * CAP, score_ints)
        order = jnp.argsort(score_ints)[:ROWS_DEV]
        chosen = group_of[order]
        return jax.random.permutation(third_key, chosen)
    groups_drawn = jax.vmap(one_device)(device_keys).reshape(DOCS)
    factors = jax.random.randint(jax.random.fold_in(key, 12), (3, DOCS), 0, CL_GRP)
    local_cluster = factors[0] * factors[1] * factors[2] // (CL_GRP * CL_GRP)
    slot_ids = groups_drawn * CL_GRP + local_cluster
    permuted = jax.random.permutation(jax.random.fold_in(key, 13), CLUSTERS).astype(jnp.int32)
    inverse = jnp.argsort(permuted).astype(jnp.int32)
    return (inverse[slot_ids], permuted)


def draw_labels(key, part):
    labels_drawn, permuted = routing(key)
    return labels_drawn.astype(jnp.int32)


def draw_cluster_slot(key, part):
    labels_drawn, permuted = routing(key)
    return permuted.astype(jnp.int32)


def draw_embeddings(key, part):
    labels_drawn, permuted = routing(key)
    key = jax.random.fold_in(key, 5)
    subkeys = jax.random.split(key, 6)
    centers = jax.random.normal(subkeys[0], (CLUSTERS, D), dtype=jnp.float32)
    strength = jnp.exp(jax.random.uniform(subkeys[1], (CLUSTERS, 1), minval=math.log(0.3), maxval=math.log(3.0)))
    column_scale = jnp.exp(jax.random.uniform(subkeys[5], (1, D), minval=0.0, maxval=math.log(1.2)))
    noise = jax.random.normal(subkeys[2], (DOCS, D), dtype=jnp.float32)
    row_scale = jnp.exp(jax.random.uniform(subkeys[3], (DOCS, 1), minval=0.0, maxval=math.log(10.0)))
    values = (centers[labels_drawn] * strength[labels_drawn] + noise) * row_scale * column_scale * 0.05
    return values.astype(jnp.bfloat16)


def setup_inputs(seed: int = 0) -> dict:
    seeds = jax.random.split(jax.random.key(seed), 4)
    embeddings = draw_embeddings(jax.random.fold_in(seeds[3], 71), 0)
    labels = draw_labels(jax.random.fold_in(seeds[3], 71), 0)
    cluster_slot = draw_cluster_slot(jax.random.fold_in(seeds[3], 71), 0)
    return dict(embeddings=embeddings, labels=labels, cluster_slot=cluster_slot)


epsilon = 1e-06
sharpness = 8.0

def reference(embeddings, labels, cluster_slot):
    widened = embeddings.astype(jnp.float32)
    units = (widened * lax.rsqrt(lax.optimization_barrier(jnp.sum(widened * widened, axis=1, keepdims=True)) + epsilon)).astype(jnp.bfloat16)
    slot_ids = cluster_slot[labels].astype(jnp.int32)
    owner_group = slot_ids // CL_GRP
    doc_ids = jnp.arange(DOCS, dtype=jnp.int32)
    holding = DOCS // ROWS_DEV * (ROWS_DEV // 4)
    block_rows = min(1024, holding)

    def one_group(group_index, running):
        best_all, mass_all = running
        order_key = jnp.where(owner_group == group_index, doc_ids, doc_ids + DOCS)
        members = jnp.argsort(order_key)[:holding].astype(jnp.int32)
        inside = owner_group[members] == group_index
        member_units = units[members]
        member_slots = jnp.where(inside, slot_ids[members], -1)

        def one_block(block_index):
            lower = (block_index * block_rows).astype(jnp.int32)
            queries = lax.dynamic_slice_in_dim(member_units, lower, block_rows, 0)
            query_slots = lax.dynamic_slice_in_dim(member_slots, lower, block_rows, 0)
            query_ids = lax.dynamic_slice_in_dim(members, lower, block_rows, 0)
            scores = jnp.dot(queries, member_units.T, preferred_element_type=jnp.float32)
            matched = (query_slots[:, None] == member_slots[None, :]) & (member_slots[None, :] >= 0)
            matched = matched & (query_ids[:, None] != members[None, :])
            best_sim = lax.optimization_barrier(jnp.max(jnp.where(matched, scores, jnp.float32(-1.0)), axis=1))
            dup_mass = lax.optimization_barrier(jnp.sum(jnp.where(matched, jnp.exp(sharpness * (scores - 1.0)), jnp.float32(0.0)), axis=1))
            return (best_sim, dup_mass)
        best_sim, dup_mass = lax.map(one_block, jnp.arange(holding // block_rows, dtype=jnp.int32))
        best_sim = best_sim.reshape(-1)
        dup_mass = dup_mass.reshape(-1)
        best_all = best_all.at[members].set(jnp.where(inside, best_sim, best_all[members]))
        mass_all = mass_all.at[members].set(jnp.where(inside, dup_mass, mass_all[members]))
        return (best_all, mass_all)
    start_best = jnp.full((DOCS,), -1.0, dtype=jnp.float32)
    start_mass = jnp.zeros((DOCS,), dtype=jnp.float32)
    best_all, mass_all = lax.fori_loop(0, N_GRP, one_group, (start_best, start_mass))
    return (best_all, jnp.log1p(mass_all))
```

```python
import jax
import jax.numpy as jnp
from jax import lax
from jax.experimental import pallas as pl
from jax.experimental.pallas import tpu as pltpu
from jax.sharding import PartitionSpec as P

epsilon = 1e-06
sharpness = 8.0
sentinel = 1 << 30

ROWS = 512
FEAT = 768
WIDE = 896
GROUPS = 8
MEMBERS = 16
FIRST = 64
SPREAD = 4
PACKED = 128
BLOCK = ROWS + PACKED
OFFSET = 16.0
LOG2E = 1.4426950408889634
AXES = ("grp", "blk")
VMEM_LIMIT = 56 * 1024 * 1024

SPOTS = ((0, 0), (1, 0), (0, 1), (0, 3), (2, 0), (0, 2))
BOTH = ((1, 0), (2, 0), (1, 3), (1, 2), (1, 5), (2, 4))
ONE = ((0, 0), (3, 2), (4, 0), (4, 5))
ROW_BLOCKS = (1, 2)


def iota(shape, axis):
    return lax.broadcasted_iota(jnp.int32, shape, axis)


def matmul(a, b, dims, exact=False):
    return lax.dot_general(
        a,
        b,
        (dims, ((), ())),
        precision=lax.Precision.HIGHEST if exact else None,
        preferred_element_type=jnp.float32,
    )


NN = ((1,), (0,))
NT = ((1,), (1,))


def prelude_kernel(labels, slots, rows, straight, spread, places):
    lab = labels[...]
    table = slots[...]
    by_cluster = (iota((ROWS, ROWS), 0) == lab).astype(jnp.bfloat16)
    sub = iota((8, ROWS), 0)
    parts = jnp.where(sub == 0, table >> 6, jnp.where(sub == 1, table & 63, 0)).astype(jnp.bfloat16)
    found = matmul(parts, by_cluster, NN)
    group = found[0:1].astype(jnp.int32)
    local = found[1:2].astype(jnp.int32)
    in_group = sub == group
    before = (iota((ROWS, ROWS), 0) < iota((ROWS, ROWS), 1)).astype(jnp.bfloat16)
    counts = matmul(in_group.astype(jnp.bfloat16), before, NN)
    rank = jnp.sum(jnp.where(in_group, counts, 0.0), axis=0, keepdims=True).astype(jnp.int32)
    places[...] = jnp.where(sub == 0, group, jnp.where(sub == 1, rank, 0))

    wide = rows[...].astype(jnp.float32)
    norm = lax.rsqrt(jnp.sum(wide * wide, axis=1, keepdims=True) + epsilon)
    units = (wide * norm).astype(jnp.bfloat16)
    lanes = iota((128, ROWS), 0)
    marks = jnp.where(lanes == local, 4.0, 0.0).astype(jnp.bfloat16)

    target = jnp.where(rank < FIRST, group * FIRST + rank, -1)
    for t in range(ROWS // 128):
        pick = (lanes + 128 * t == target).astype(jnp.bfloat16)
        here = pl.ds(128 * t, 128)
        straight[here, :FEAT] = matmul(pick, units, NN).astype(jnp.bfloat16)
        straight[here, FEAT:] = matmul(pick, marks, NT).astype(jnp.bfloat16)
    member = group * MEMBERS + (rank & (MEMBERS - 1))
    turn = rank >> 4
    totals = matmul(
        jnp.ones((128, ROWS), jnp.bfloat16), (lanes - 64 == group).astype(jnp.bfloat16), NT
    )
    for j in range(SPREAD):
        pick = (lanes == jnp.where(turn == FIRST // MEMBERS + j, member, -1)).astype(jnp.bfloat16)
        spread[:, j * WIDE : j * WIDE + FEAT] = matmul(pick, units, NN).astype(jnp.bfloat16)
        more = matmul(pick, marks, NT)
        if j == 0:
            more = more + totals
        spread[:, j * WIDE + FEAT : (j + 1) * WIDE] = more.astype(jnp.bfloat16)


def pack_kernel(arrived, packed, over):
    lane = iota((128, 128), 1)
    sub = iota((128, 128), 0)
    ones = jnp.ones((8, 128), jnp.bfloat16)
    before = (iota((ROWS, ROWS), 0) < iota((ROWS, ROWS), 1)).astype(jnp.bfloat16)
    more = [arrived[:, j * WIDE + FEAT : (j + 1) * WIDE] for j in range(SPREAD)]
    totals = jnp.where(lane >= 64, more[0].astype(jnp.float32), 0.0)
    turns = jnp.zeros((128, 128), jnp.float32)
    for m in range(SPREAD):
        turns = turns + (totals > (FIRST + MEMBERS * m)).astype(jnp.float32)
    most = jnp.max(jnp.sum(turns, axis=0, keepdims=True), axis=1, keepdims=True)
    over[...] = jnp.broadcast_to((most > PACKED).astype(jnp.int32), (8, 128))
    marks = [jnp.where(lane < 64, m, jnp.zeros_like(m)) for m in more]
    held = jnp.concatenate([matmul(ones, m, NT) for m in marks], axis=1) > 0.0
    position = matmul(held.astype(jnp.bfloat16), before, NN)
    position = jnp.where(held, position, -1.0)[0:1].astype(jnp.int32)
    rows = jnp.zeros((PACKED, FEAT), jnp.float32)
    tail = jnp.zeros((PACKED, 128), jnp.float32)
    for j in range(SPREAD):
        pick = (sub == position[:, 128 * j : 128 * (j + 1)]).astype(jnp.bfloat16)
        rows = rows + matmul(pick, arrived[:, j * WIDE : j * WIDE + FEAT], NN)
        names = jnp.where(sub == 64, lane + 1, jnp.where(sub == 65, j, 0)).astype(jnp.bfloat16)
        tail = tail + matmul(pick, marks[j], NN) + matmul(pick, names, NT)
    packed[:, :FEAT] = rows.astype(jnp.bfloat16)
    packed[:, FEAT:] = tail.astype(jnp.bfloat16)


def column_fold(x, op):
    while x.shape[0] > 8:
        half = x.shape[0] // 2
        x = op(x[:half], x[half:])
    return x


def row_fold(x, op):
    total = x[:, :128]
    for t in range(1, x.shape[1] // 128):
        total = op(total, x[:, 128 * t : 128 * (t + 1)])
    return total


def pair_kernel(*refs):
    big = refs[:6]
    small = refs[6:12]
    out = refs[12]
    clean, col_best, col_mass, row_best, row_mass, lines = refs[13:]

    lane = iota((128, 128), 1)
    for e in range(6):
        clean[e, :, :FEAT] = small[e][:, :FEAT]
        tail = small[e][:, FEAT:]
        clean[e, :, FEAT:] = jnp.where(lane < 64, tail, jnp.zeros_like(tail))
    col_best[...] = jnp.zeros_like(col_best)
    col_mass[...] = jnp.zeros_like(col_mass)
    row_best[...] = jnp.zeros_like(row_best)
    row_mass[...] = jnp.zeros_like(row_mass)

    def tile(x, y, c, first, width, r, start, diagonal):
        product = matmul(x, y, NT)
        if diagonal is not None:
            shape = (128, width)
            product = jnp.where(iota(shape, 0) + diagonal == iota(shape, 1), 0.0, product)
        soft = jnp.exp2((product - (OFFSET + 1.0)) * (sharpness * LOG2E))
        here = slice(first, first + width)
        col_best[c, :, here] = jnp.maximum(col_best[c, :, here], column_fold(product, jnp.maximum))
        col_mass[c, :, here] = col_mass[c, :, here] + column_fold(soft, jnp.add)
        if r is not None:
            there = pl.ds(start, 128)
            row_best[r, there, :] = jnp.maximum(row_best[r, there, :], row_fold(product, jnp.maximum))
            row_mass[r, there, :] = row_mass[r, there, :] + row_fold(soft, jnp.add)

    def pair(rows, cols, r):
        own = rows == cols

        def chunk(t, carry):
            start = pl.multiple_of(t * 128, 128)
            x = big[rows][pl.ds(start, 128), :]
            tile(x, big[cols][...], cols, 0, ROWS, r, start, start if own else None)
            tile(x, clean[cols], cols, ROWS, PACKED, r, start, None)
            return carry

        lax.fori_loop(0, ROWS // 128, chunk, 0)
        x = clean[rows]
        tile(x, big[cols][...], cols, 0, ROWS, r, ROWS, None)
        tile(x, clean[cols], cols, ROWS, PACKED, r, ROWS, 0 if own else None)

    for rows, cols in ONE:
        pair(rows, cols, None)
    for rows, cols in BOTH:
        pair(rows, cols, ROW_BLOCKS.index(rows))

    lines[...] = jnp.zeros_like(lines)
    member = lax.axis_index("blk")
    odd = lax.axis_index("grp") & 1
    sub = iota((128, 128), 0)
    back = jnp.zeros((128, 128), jnp.float32)
    for e in range(6):
        best = jnp.max(col_best[e], axis=0, keepdims=True)
        mass = jnp.sum(col_mass[e], axis=0, keepdims=True)
        if e in ROW_BLOCKS:
            r = ROW_BLOCKS.index(e)
            tops, sums = [], []
            for t in range(BLOCK // 128):
                here = pl.ds(128 * t, 128)
                tops.append(jnp.max(row_best[r, here, :].T, axis=0, keepdims=True))
                sums.append(jnp.sum(row_mass[r, here, :].T, axis=0, keepdims=True))
            best = jnp.maximum(best, jnp.concatenate(tops, axis=1))
            mass = mass + jnp.concatenate(sums, axis=1)
        best = jnp.where(best > 0.5 * OFFSET, jnp.maximum(best - OFFSET, -1.0), -1.0)
        dy, dz = SPOTS[e]
        y = ((member >> 2) + jnp.where(odd == 1, 4 - dy, dy)) & 3
        z = ((member & 3) + jnp.where(odd == 1, 4 - dz, dz)) & 3
        spot = y * 4 + z
        for g in range(GROUPS):
            line = pl.ds(g * MEMBERS + spot, 1)
            part = slice(g * FIRST, (g + 1) * FIRST)
            lines[line, :] = jnp.concatenate([best[:, part], mass[:, part]], axis=1)
        names = small[e][:, FEAT:]
        pick = jnp.where((iota((8, 128), 0) == 0) & (iota((8, 128), 1) == 64), 1.0, 0.0)
        pick = pick + jnp.where((iota((8, 128), 0) == 1) & (iota((8, 128), 1) == 65), 1.0, 0.0)
        named = matmul(pick.astype(jnp.bfloat16), names, NT)
        source = named[0:1].astype(jnp.int32) - 1
        turn = named[1:2].astype(jnp.int32)
        spots = sub - 8 * e
        values = jnp.where(
            (spots >= 0) & (spots < 8) & ((spots >> 1) == turn),
            jnp.where((spots & 1) == 0, best[:, ROWS:], mass[:, ROWS:]),
            0.0,
        )
        to = (sub == source).astype(jnp.float32)
        back = back + matmul(to, values, NT, exact=True)
    out[:, 128:] = back
    out[:, :128] = lines[...]


def finish_kernel(arrived, places, result, lines):
    lines[...] = arrived[:, 0:128]
    member = lax.axis_index("blk")
    group = places[0:1, :]
    rank = places[1:2, :]
    lane = iota((1, 128), 1)
    y, z = member >> 2, member & 3
    tables = []
    for g in range(GROUPS):
        best = mass = None
        for dy, dz in SPOTS:
            if g & 1:
                dy, dz = -dy, -dz
            line = g * MEMBERS + ((y + ((-dy) & 3)) & 3) * 4 + ((z + ((-dz) & 3)) & 3)
            row = lines[pl.ds(line, 1), :]
            best = row if best is None else jnp.maximum(best, row)
            mass = row if mass is None else mass + row
        tables.append(jnp.where(lane < FIRST, best, mass))
    table = jnp.concatenate(tables, axis=0)
    chosen = (iota((8, ROWS), 0) == group).astype(jnp.float32)
    values = matmul(table.T, chosen, NN, exact=True)
    sub = iota((128, ROWS), 0)
    first_best = jnp.sum(jnp.where(sub == rank, values, 0.0), axis=0, keepdims=True)
    first_mass = jnp.sum(jnp.where(sub == rank + FIRST, values, 0.0), axis=0, keepdims=True)

    shape = (128, 128)
    at, col = iota(shape, 0), iota(shape, 1)
    base, ay, az = at >> 4, (at >> 2) & 3, at & 3
    turned = (base & 1) == 1
    best = mass = None
    late = arrived[:, 128:256]
    for e, (dy, dz) in enumerate(SPOTS):
        by = (ay + jnp.where(turned, dy, (-dy) & 3)) & 3
        bz = (az + jnp.where(turned, dz, (-dz) & 3)) & 3
        move = (col == base * MEMBERS + by * 4 + bz).astype(jnp.float32)
        moved = matmul(move, late, NN, exact=True)
        if e:
            moved = pltpu.roll(moved, 128 - 8 * e, 1)
        best = moved if best is None else jnp.maximum(best, moved)
        mass = moved if mass is None else mass + moved
    merged = jnp.where((col & 1) == 0, best, mass)
    holder = (sub == group * MEMBERS + (rank & (MEMBERS - 1))).astype(jnp.float32)
    picked = matmul(merged.T, holder, NN, exact=True)
    turn = (rank >> 4) - FIRST // MEMBERS
    late_best = jnp.sum(jnp.where(sub == 2 * turn, picked, 0.0), axis=0, keepdims=True)
    late_mass = jnp.sum(jnp.where(sub == 2 * turn + 1, picked, 0.0), axis=0, keepdims=True)
    best = jnp.where(rank < FIRST, first_best, late_best)
    mass = jnp.where(rank < FIRST, first_mass, late_mass)
    result[0:1, :] = best
    result[1:2, :] = jnp.log1p(mass)


def call(kernel, out_shape, scratch=(), flops=0, name=None):
    return pl.pallas_call(
        kernel,
        out_shape=out_shape,
        scratch_shapes=scratch,
        compiler_params=pltpu.CompilerParams(vmem_limit_bytes=VMEM_LIMIT),
        cost_estimate=pl.CostEstimate(flops=flops, bytes_accessed=8_000_000, transcendentals=0),
        name=name,
    )


def hop(dy, dz):
    pairs = []
    for g in range(GROUPS):
        turn = -1 if g & 1 else 1
        for y in range(4):
            for z in range(4):
                source = ((y + turn * dy) % 4) * 4 + (z + turn * dz) % 4
                pairs.append((g * MEMBERS + source, g * MEMBERS + y * 4 + z))
    return pairs


def from_spot(x, dy, dz):
    return lax.ppermute(x, AXES, hop(dy, dz))


def gather_spots(x):
    one = from_spot(x, 1, 0)
    two = from_spot(x, 0, 1)
    three = from_spot(x, 0, 3)
    return (x, one, two, three, from_spot(one, 1, 0), from_spot(two, 0, 1))


def fast(embeddings, labels, cluster_slot):
    f32, bf16, i32 = jnp.float32, jnp.bfloat16, jnp.int32
    straight, spread, places = call(
        prelude_kernel,
        (
            jax.ShapeDtypeStruct((ROWS, WIDE), bf16),
            jax.ShapeDtypeStruct((128, SPREAD * WIDE), bf16),
            jax.ShapeDtypeStruct((8, ROWS), i32),
        ),
        flops=3 * ROWS * ROWS * WIDE,
        name="prelude",
    )(labels.reshape(1, ROWS), cluster_slot.reshape(1, ROWS), embeddings)
    big = lax.all_to_all(straight, "grp", split_axis=0, concat_axis=0, tiled=True)
    late = lax.all_to_all(spread, AXES, split_axis=0, concat_axis=0, tiled=True)
    big = gather_spots(big)
    packed, over = call(
        pack_kernel,
        (jax.ShapeDtypeStruct((PACKED, WIDE), bf16), jax.ShapeDtypeStruct((8, 128), i32)),
        flops=2 * ROWS * PACKED * WIDE,
        name="pack",
    )(late)
    small = gather_spots(packed)
    message = call(
        pair_kernel,
        jax.ShapeDtypeStruct((128, 256), f32),
        scratch=(
            pltpu.VMEM((6, PACKED, WIDE), bf16),
            pltpu.VMEM((6, 8, BLOCK), f32),
            pltpu.VMEM((6, 8, BLOCK), f32),
            pltpu.VMEM((2, BLOCK, 128), f32),
            pltpu.VMEM((2, BLOCK, 128), f32),
            pltpu.VMEM((128, 128), f32),
        ),
        flops=20 * BLOCK * BLOCK * WIDE,
        name="pairs",
    )(*big, *small)
    answer = lax.all_to_all(message, AXES, split_axis=0, concat_axis=0, tiled=True)
    result = call(
        finish_kernel,
        jax.ShapeDtypeStruct((2, ROWS), f32),
        scratch=(pltpu.VMEM((128, 128), f32),),
        flops=ROWS * ROWS * 128,
        name="finish",
    )(answer, places)
    return (result[0], result[1]), over[0, 0]


def shortened(shard):

    def short(part):
        return part.astype(jnp.bfloat16) if part.dtype == jnp.float32 else part

    return jax.tree.map(short, shard)


def scores_of(queries, key_rows):
    return jnp.einsum("qd,kd->qk", queries, key_rows, preferred_element_type=jnp.float32)


def partners(query_slots, key_slots):
    return (query_slots[:, None] == key_slots[None, :]) & (key_slots[None, :] >= 0)


def reduce_pairs(scores, matched, along):
    best_sim = jnp.max(jnp.where(matched, scores, jnp.float32(-1.0)), axis=along)
    dup_mass = jnp.sum(
        jnp.where(matched, jnp.exp(sharpness * (scores - 1.0)), jnp.float32(0.0)), axis=along
    )
    return (best_sim, dup_mass)


def tile_stats(queries, query_slots, query_ids, key_rows, key_slots, key_ids):
    width = queries.shape[1]
    member_count = queries.shape[0]
    key_count = key_rows.shape[0]
    span = member_count * max(1, 1024 // member_count)
    key_tiles = key_count // span
    k_rows = key_rows.reshape(key_tiles, span, width)
    k_slot = key_slots.reshape(key_tiles, span)
    k_ident = key_ids.reshape(key_tiles, span)

    def one_block(block_index):
        scores = scores_of(queries, k_rows[block_index])
        matched = partners(query_slots, k_slot[block_index])
        matched = matched & (query_ids[:, None] != k_ident[block_index][None, :])
        row_best, row_mass = reduce_pairs(scores, matched, 1)
        col_best = jnp.full((span,), -1.0, dtype=jnp.float32)
        col_mass = jnp.zeros((span,), dtype=jnp.float32)
        return (row_best, row_mass, col_best, col_mass)

    row_best, row_mass, col_best, col_mass = lax.map(
        one_block, jnp.arange(key_tiles, dtype=jnp.int32)
    )
    return (
        jnp.max(row_best, axis=0),
        jnp.sum(row_mass, axis=0),
        col_best.reshape(-1),
        col_mass.reshape(-1),
    )


def similarities(members, member_slots):
    member_count = members.shape[0]
    local_ids = jnp.arange(member_count, dtype=jnp.int32)
    own_ids = lax.axis_index("blk") * member_count + local_ids
    start_best = jnp.full((member_count,), -1.0, dtype=jnp.float32)
    start_mass = jnp.zeros((member_count,), dtype=jnp.float32)
    key_rows = lax.all_gather(members, "blk", axis=0, tiled=True)
    key_slots = lax.all_gather(shortened(member_slots), "blk", axis=0, tiled=True)
    key_ids = jnp.arange(key_rows.shape[0], dtype=jnp.int32)
    row_best, row_mass, unused_best, unused_mass = tile_stats(
        members, member_slots, own_ids, key_rows, key_slots, key_ids
    )
    return (jnp.maximum((start_best, start_mass)[0], row_best), row_mass)


def general(embeddings, labels, cluster_slot):
    groups = lax.axis_size("grp")
    row_count, feature_count = embeddings.shape
    cluster_count = cluster_slot.shape[0]
    capacity = row_count // 4
    widened = embeddings.astype(jnp.float32)
    units = (
        widened * lax.rsqrt(jnp.sum(widened * widened, axis=1, keepdims=True) + epsilon)
    ).astype(jnp.bfloat16)
    cluster_ids = jnp.arange(cluster_count, dtype=jnp.int32)
    slot_ids = jnp.sum(
        jnp.where(labels[:, None] == cluster_ids[None, :], cluster_slot[None, :], 0), axis=1
    )
    owner_group = slot_ids // (cluster_count // groups)
    owner_onehot = (owner_group[:, None] == jnp.arange(groups, dtype=jnp.int32)[None, :]).astype(
        jnp.int32
    )
    earlier = jnp.cumsum(owner_onehot, axis=0) - owner_onehot
    rank_within = jnp.sum(earlier * owner_onehot, axis=1)
    send_place = owner_group * capacity + rank_within
    outgoing = jnp.zeros((groups * capacity, feature_count), jnp.bfloat16).at[send_place].set(units)
    outgoing_slots = jnp.full((groups * capacity,), -1, jnp.int32).at[send_place].set(slot_ids)
    arrived, arrived_slots = (
        lax.all_to_all(outgoing, "grp", split_axis=0, concat_axis=0, tiled=True),
        lax.all_to_all(outgoing_slots, "grp", split_axis=0, concat_axis=0, tiled=True),
    )
    sort_keys = jnp.where(arrived_slots >= 0, arrived_slots, sentinel)
    order = jnp.argsort(sort_keys, stable=True)
    members = arrived[order]
    member_slots = arrived_slots[order]
    best_sorted, mass_sorted = similarities(members, member_slots)
    best_all = jnp.zeros_like(best_sorted).at[order].set(best_sorted)
    mass_all = jnp.zeros_like(mass_sorted).at[order].set(mass_sorted)
    best_back, mass_back = (
        lax.all_to_all(best_all, "grp", split_axis=0, concat_axis=0, tiled=True),
        lax.all_to_all(mass_all, "grp", split_axis=0, concat_axis=0, tiled=True),
    )
    return (best_back[send_place], jnp.log1p(mass_back[send_place]))


def body(embeddings, labels, cluster_slot):
    result, over = fast(embeddings, labels, cluster_slot)
    return lax.cond(
        over > 0, lambda: general(embeddings, labels, cluster_slot), lambda: result
    )


def solution(mesh):
    placed = (P(AXES, None), P(AXES), P())
    return jax.shard_map(
        body,
        mesh=mesh,
        in_specs=placed,
        out_specs=(P(AXES), P(AXES)),
        check_vma=False,
    )
```

```python
import jax
import jax.numpy as jnp
from jax import lax
from jax.experimental import pallas as pl
from jax.experimental.pallas import tpu as pltpu
from jax.sharding import PartitionSpec as P

epsilon = 1e-06
sharpness = 8.0

ROWS = 512
FEAT = 768
HALF = 512
WIDE = 896
GROUPS = 8
MEMBERS = 16
FIRST = 64
SPREAD = 4
PACKED = 128
BLOCK = ROWS + PACKED
OFFSET = 16.0
LOG2E = 1.4426950408889634
AXES = ("grp", "blk")
VMEM_LIMIT = 56 * 1024 * 1024

SPOTS = ((0, 0), (1, 0), (0, 1), (0, 3), (2, 0), (0, 2))
ROW_BLOCKS = (1, 2)
COL_ORDER = (3, 2, 5, 0, 4)
ROW_ORDER = (3, 1, 4, 2, 0)


def iota(shape, axis):
    return lax.broadcasted_iota(jnp.int32, shape, axis)


def matmul(a, b, dims, exact=False):
    return lax.dot_general(
        a,
        b,
        (dims, ((), ())),
        precision=lax.Precision.HIGHEST if exact else None,
        preferred_element_type=jnp.float32,
    )


NN = ((1,), (0,))
NT = ((1,), (1,))


def prelude_kernel(labels, slots, rows, straight, spread, places):
    lab = labels[...]
    table = slots[...]
    by_cluster = (iota((ROWS, ROWS), 0) == lab).astype(jnp.bfloat16)
    sub = iota((8, ROWS), 0)
    parts = jnp.where(sub == 0, table >> 6, jnp.where(sub == 1, table & 63, 0)).astype(jnp.bfloat16)
    found = matmul(parts, by_cluster, NN)
    group = found[0:1].astype(jnp.int32)
    local = found[1:2].astype(jnp.int32)
    in_group = sub == group
    before = (iota((ROWS, ROWS), 0) < iota((ROWS, ROWS), 1)).astype(jnp.bfloat16)
    counts = matmul(in_group.astype(jnp.bfloat16), before, NN)
    rank = jnp.sum(jnp.where(in_group, counts, 0.0), axis=0, keepdims=True).astype(jnp.int32)
    places[...] = jnp.where(sub == 0, group, jnp.where(sub == 1, rank, 0))

    wide = rows[...].astype(jnp.float32)
    norm = lax.rsqrt(jnp.sum(wide * wide, axis=1, keepdims=True) + epsilon)
    units = (wide * norm).astype(jnp.bfloat16)
    lanes = iota((128, ROWS), 0)
    marks = jnp.where(lanes == local, 4.0, 0.0).astype(jnp.bfloat16)

    target = jnp.where(rank < FIRST, group * FIRST + rank, -1)
    for t in range(ROWS // 128):
        pick = (lanes + 128 * t == target).astype(jnp.bfloat16)
        here = pl.ds(128 * t, 128)
        straight[here, :FEAT] = matmul(pick, units, NN).astype(jnp.bfloat16)
        straight[here, FEAT:] = matmul(pick, marks, NT).astype(jnp.bfloat16)
    member = group * MEMBERS + (rank & (MEMBERS - 1))
    goal = jnp.where(rank < FIRST, -8, member * 8 + 2 * ((rank >> 4) - FIRST // MEMBERS))
    totals = matmul(
        jnp.ones((128, ROWS), jnp.bfloat16), (lanes - 64 == group).astype(jnp.bfloat16), NT
    )
    first = (iota((128, 128), 0) & 7) == 1
    for t in range(8):
        here = pl.ds(128 * t, 128)
        left = (lanes + 128 * t == goal).astype(jnp.bfloat16)
        right = (lanes + 128 * t == goal + 1).astype(jnp.bfloat16)
        spread[here, :256] = (
            matmul(left, units[:, :256], NN) + matmul(right, units[:, HALF:], NN)
        ).astype(jnp.bfloat16)
        spread[here, 256:384] = (
            matmul(left, units[:, 256:384], NN)
            + matmul(right, marks, NT)
            + jnp.where(first, totals, 0.0)
        ).astype(jnp.bfloat16)
        spread[here, 384:] = matmul(left, units[:, 384:HALF], NN).astype(jnp.bfloat16)


def pack_kernel(arrived, packed, over):
    shape = (128, 128)
    lane, sub = iota(shape, 1), iota(shape, 0)
    count = 8 * 128
    totals = jnp.zeros(shape, jnp.float32)
    for t in range(8):
        tail = arrived[pl.ds(128 * t, 128), 256:384].astype(jnp.float32)
        tail = jnp.where(((sub & 7) == 1) & (lane >= 64), tail, 0.0)
        for m in range(SPREAD):
            totals = totals + (tail > (FIRST + MEMBERS * m)).astype(jnp.float32)
    most = jnp.max(jnp.sum(totals, axis=0, keepdims=True), axis=1, keepdims=True)
    over[...] = jnp.broadcast_to((most > PACKED).astype(jnp.int32), (8, 128))
    tails = arrived[:, 256:384]
    tails = jnp.where(
        ((iota((count, 128), 0) & 1) == 1) & (iota((count, 128), 1) < 64), tails, jnp.zeros_like(tails)
    )
    held = matmul(jnp.ones((8, 128), jnp.bfloat16), tails, NT) > 0.0
    before = (iota((count, count), 0) < iota((count, count), 1)).astype(jnp.bfloat16)
    position = matmul(held.astype(jnp.bfloat16), before, NN)
    position = jnp.where(held, position, -1.0)[0:1].astype(jnp.int32)
    right = (iota((128, count), 0) == position).astype(jnp.bfloat16)
    position = jnp.concatenate([position[:, 1:], position[:, :1]], axis=1)
    left = (iota((128, count), 0) == position).astype(jnp.bfloat16)
    at = iota((128, count), 1)
    line = iota((128, count), 0)
    names = jnp.where(line == 64, (at >> 3) + 1, jnp.where(line == 65, (at >> 1) & 3, 0))
    packed[:, :HALF] = matmul(left, arrived[...], NN).astype(jnp.bfloat16)
    packed[:, HALF:FEAT] = matmul(right, arrived[:, :256], NN).astype(jnp.bfloat16)
    packed[:, FEAT:] = (
        matmul(right, tails, NN) + matmul(right, names.astype(jnp.bfloat16), NT)
    ).astype(jnp.bfloat16)


def column_fold(x, op):
    while x.shape[0] > 8:
        half = x.shape[0] // 2
        x = op(x[:half], x[half:])
    return x


def row_fold(x, op):
    total = x[:, :128]
    for t in range(1, x.shape[1] // 128):
        total = op(total, x[:, 128 * t : 128 * (t + 1)])
    return total


def clear(*refs):
    for ref in refs:
        ref[...] = jnp.zeros_like(ref)


def tile(x, y, cols, rows, state, diagonal=False):
    col_best, col_mass, row_best, row_mass = state
    product = matmul(x, y, NT)
    if diagonal:
        shape = product.shape
        product = jnp.where(iota(shape, 0) == iota(shape, 1), 0.0, product)
    soft = jnp.exp2((product - (OFFSET + 1.0)) * (sharpness * LOG2E))
    for first, size, c, start in cols:
        part = slice(first, first + size)
        here = slice(start, start + size)
        col_best[c, :, here] = jnp.maximum(
            col_best[c, :, here], column_fold(product[:, part], jnp.maximum)
        )
        col_mass[c, :, here] = col_mass[c, :, here] + column_fold(soft[:, part], jnp.add)
    for first, size, r, start in rows:
        part = slice(first, first + size)
        here = slice(start, start + size)
        row_best[r, here, :] = jnp.maximum(
            row_best[r, here, :], row_fold(product[part], jnp.maximum)
        )
        row_mass[r, here, :] = row_mass[r, here, :] + row_fold(soft[part], jnp.add)


def square(rows, cols, c, r, state, own=False):
    for i in range(0, ROWS, 256):
        for j in range(0, ROWS, 256):
            tile(
                rows[i : i + 256, :],
                cols[j : j + 256, :],
                [(0, 256, c, j)],
                [] if r is None else [(0, 256, r, i)],
                state,
                own and i == j,
            )


def settle(e, size, state):
    col_best, col_mass, row_best, row_mass = state
    best = jnp.max(col_best[e], axis=0, keepdims=True)
    mass = jnp.sum(col_mass[e], axis=0, keepdims=True)
    if e in ROW_BLOCKS:
        r = ROW_BLOCKS.index(e)
        tops, sums = [], []
        for t in range(0, size, 128):
            tops.append(jnp.max(row_best[r, t : t + 128, :].T, axis=0, keepdims=True))
            sums.append(jnp.sum(row_mass[r, t : t + 128, :].T, axis=0, keepdims=True))
        best = jnp.maximum(best, jnp.concatenate(tops, axis=1))
        mass = mass + jnp.concatenate(sums, axis=1)
    return best, mass


def similarity(best):
    return jnp.where(best > 0.5 * OFFSET, jnp.maximum(best - OFFSET, -1.0), -1.0)


def early_kernel(b0, b1, b2, b3, best_out, mass_out, *state):
    clear(best_out, mass_out, *state)
    square(b0, b0, 0, None, state, True)
    square(b1, b0, 0, 0, state)
    square(b2, b0, 0, 1, state)
    square(b1, b3, 3, 0, state)
    square(b1, b2, 2, 0, state)
    square(b3, b2, 2, None, state)
    for e in range(4):
        best_out[e : e + 1, :], mass_out[e : e + 1, :] = settle(e, ROWS, state)


def packed_kernel(*refs):
    big = refs[:6]
    small = refs[6:12]
    back_out, best_out, mass_out = refs[12:15]
    as_cols, as_rows = refs[15:17]
    state = refs[17:]
    clear(best_out, mass_out, *state)
    lane = iota((PACKED, 128), 1)
    for stack, order in ((as_cols, COL_ORDER), (as_rows, ROW_ORDER)):
        for place, e in enumerate(order):
            here = slice(place * PACKED, (place + 1) * PACKED)
            stack[here, :FEAT] = small[e][:, :FEAT]
            tail = small[e][:, FEAT:]
            stack[here, FEAT:] = jnp.where(lane < 64, tail, jnp.zeros_like(tail))

    def piece(stack, first, count):
        return stack[first * PACKED : (first + count) * PACKED, :]

    for r, first, count in ((1, 0, 2), (1, 2, 2), (2, 3, 2), (4, 2, 2), (3, 1, 1), (0, 3, 1)):
        cols = [(i * PACKED, PACKED, COL_ORDER[first + i], ROWS) for i in range(count)]
        y = piece(as_cols, first, count)
        for start in (0, 256):
            rows = [(0, 256, ROW_BLOCKS.index(r), start)] if r in ROW_BLOCKS else []
            tile(big[r][start : start + 256, :], y, cols, rows, state)
        rows = [(0, PACKED, ROW_BLOCKS.index(r), ROWS)] if r in ROW_BLOCKS else []
        tile(piece(as_rows, ROW_ORDER.index(r), 1), y, cols, rows, state, r == 0)
    for c, first, count in ((0, 1, 2), (0, 3, 2), (2, 0, 2), (5, 1, 2), (3, 1, 1), (4, 3, 1)):
        x = piece(as_rows, first, count)
        rows = [
            (i * PACKED, PACKED, ROW_BLOCKS.index(ROW_ORDER[first + i]), ROWS)
            for i in range(count)
            if ROW_ORDER[first + i] in ROW_BLOCKS
        ]
        for start in (0, 256):
            tile(x, big[c][start : start + 256, :], [(0, 256, c, start)], rows, state)

    sub = iota((128, 128), 0)
    spot = iota((8, 128), 0)
    pick = jnp.where((spot < 2) & (iota((8, 128), 1) == 64 + spot), 1.0, 0.0).astype(jnp.bfloat16)
    back = jnp.zeros((128, 128), jnp.float32)
    for e in range(6):
        best, mass = settle(e, BLOCK, state)
        best_out[e : e + 1, :] = best[:, :ROWS]
        mass_out[e : e + 1, :] = mass[:, :ROWS]
        named = matmul(pick, small[e][:, FEAT:], NT)
        source = named[0:1].astype(jnp.int32) - 1
        turn = named[1:2].astype(jnp.int32)
        spots = sub - 8 * e
        values = jnp.where(
            (spots >= 0) & (spots < 8) & ((spots >> 1) == turn),
            jnp.where((spots & 1) == 0, similarity(best[:, ROWS:]), mass[:, ROWS:]),
            0.0,
        )
        to = (sub == source).astype(jnp.float32)
        back = back + matmul(to, values, NT, exact=True)
    back_out[...] = back


def late_kernel(b0, b1, b2, b4, b5, best1, mass1, best2, mass2, back, out, *state):
    state, lines = state[:4], state[4]
    clear(lines, *state)
    square(b4, b0, 0, None, state)
    square(b4, b5, 5, None, state)
    square(b1, b5, 5, 0, state)
    square(b2, b4, 4, 1, state)
    member = lax.axis_index("blk")
    odd = lax.axis_index("grp") & 1
    for e in range(6):
        here = slice(e, e + 1)
        best, mass = settle(e, ROWS, state)
        best = similarity(jnp.maximum(best, jnp.maximum(best1[here, :], best2[here, :])))
        mass = mass + (mass1[here, :] + mass2[here, :])
        dy, dz = SPOTS[e]
        y = ((member >> 2) + jnp.where(odd == 1, 4 - dy, dy)) & 3
        z = ((member & 3) + jnp.where(odd == 1, 4 - dz, dz)) & 3
        spot = y * 4 + z
        for g in range(GROUPS):
            line = pl.ds(g * MEMBERS + spot, 1)
            part = slice(g * FIRST, (g + 1) * FIRST)
            lines[line, :] = jnp.concatenate([best[:, part], mass[:, part]], axis=1)
    out[:, :128] = lines[...]
    out[:, 128:] = back[...]


def finish_kernel(arrived, places, result, lines):
    lines[...] = arrived[:, 0:128]
    member = lax.axis_index("blk")
    group = places[0:1, :]
    rank = places[1:2, :]
    lane = iota((1, 128), 1)
    y, z = member >> 2, member & 3
    tables = []
    for g in range(GROUPS):
        best = mass = None
        for dy, dz in SPOTS:
            if g & 1:
                dy, dz = -dy, -dz
            line = g * MEMBERS + ((y + ((-dy) & 3)) & 3) * 4 + ((z + ((-dz) & 3)) & 3)
            row = lines[pl.ds(line, 1), :]
            best = row if best is None else jnp.maximum(best, row)
            mass = row if mass is None else mass + row
        tables.append(jnp.where(lane < FIRST, best, mass))
    table = jnp.concatenate(tables, axis=0)
    chosen = (iota((8, ROWS), 0) == group).astype(jnp.float32)
    values = matmul(table.T, chosen, NN, exact=True)
    sub = iota((128, ROWS), 0)
    first_best = jnp.sum(jnp.where(sub == rank, values, 0.0), axis=0, keepdims=True)
    first_mass = jnp.sum(jnp.where(sub == rank + FIRST, values, 0.0), axis=0, keepdims=True)

    shape = (128, 128)
    at, col = iota(shape, 0), iota(shape, 1)
    base, ay, az = at >> 4, (at >> 2) & 3, at & 3
    turned = (base & 1) == 1
    best = mass = None
    late = arrived[:, 128:256]
    for e, (dy, dz) in enumerate(SPOTS):
        by = (ay + jnp.where(turned, dy, (-dy) & 3)) & 3
        bz = (az + jnp.where(turned, dz, (-dz) & 3)) & 3
        move = (col == base * MEMBERS + by * 4 + bz).astype(jnp.float32)
        moved = matmul(move, late, NN, exact=True)
        if e:
            moved = pltpu.roll(moved, 128 - 8 * e, 1)
        best = moved if best is None else jnp.maximum(best, moved)
        mass = moved if mass is None else mass + moved
    merged = jnp.where((col & 1) == 0, best, mass)
    holder = (sub == group * MEMBERS + (rank & (MEMBERS - 1))).astype(jnp.float32)
    picked = matmul(merged.T, holder, NN, exact=True)
    turn = (rank >> 4) - FIRST // MEMBERS
    late_best = jnp.sum(jnp.where(sub == 2 * turn, picked, 0.0), axis=0, keepdims=True)
    late_mass = jnp.sum(jnp.where(sub == 2 * turn + 1, picked, 0.0), axis=0, keepdims=True)
    best = jnp.where(rank < FIRST, first_best, late_best)
    mass = jnp.where(rank < FIRST, first_mass, late_mass)
    result[0:1, :] = best
    result[1:2, :] = jnp.log1p(mass)


def call(kernel, out_shape, scratch=(), flops=0, name=None):
    return pl.pallas_call(
        kernel,
        out_shape=out_shape,
        scratch_shapes=scratch,
        compiler_params=pltpu.CompilerParams(vmem_limit_bytes=VMEM_LIMIT),
        cost_estimate=pl.CostEstimate(flops=flops, bytes_accessed=8_000_000, transcendentals=0),
        name=name,
    )


def hop(dy, dz):
    pairs = []
    for g in range(GROUPS):
        turn = -1 if g & 1 else 1
        for y in range(4):
            for z in range(4):
                source = ((y + turn * dy) % 4) * 4 + (z + turn * dz) % 4
                pairs.append((g * MEMBERS + source, g * MEMBERS + y * 4 + z))
    return pairs


def from_spot(x, dy, dz):
    return lax.ppermute(x, AXES, hop(dy, dz))


def fast(embeddings, labels, cluster_slot):
    f32, bf16, i32 = jnp.float32, jnp.bfloat16, jnp.int32
    shape = jax.ShapeDtypeStruct
    straight, spread, places = call(
        prelude_kernel,
        (shape((ROWS, WIDE), bf16), shape((1024, HALF), bf16), shape((8, ROWS), i32)),
        flops=4_000_000_000,
        name="prelude",
    )(labels.reshape(1, ROWS), cluster_slot.reshape(1, ROWS), embeddings)
    b0 = lax.all_to_all(straight, "grp", split_axis=0, concat_axis=0, tiled=True)
    b1 = from_spot(b0, 1, 0)
    b2 = from_spot(b0, 0, 1)
    b3 = from_spot(b0, 0, 3)
    arrived = lax.all_to_all(spread, AXES, split_axis=0, concat_axis=0, tiled=True)
    b4 = from_spot(b1, 1, 0)
    b5 = from_spot(b2, 0, 1)
    packed, over = call(
        pack_kernel,
        (shape((PACKED, WIDE), bf16), shape((8, 128), i32)),
        flops=3_000_000_000,
        name="pack",
    )(arrived)
    small = [packed] + [from_spot(packed, *spot) for spot in SPOTS[1:]]

    def state(size):
        return (
            pltpu.VMEM((6, 8, size), f32),
            pltpu.VMEM((6, 8, size), f32),
            pltpu.VMEM((2, size, 128), f32),
            pltpu.VMEM((2, size, 128), f32),
        )

    best1, mass1 = call(
        early_kernel,
        (shape((8, ROWS), f32), shape((8, ROWS), f32)),
        scratch=state(ROWS),
        flops=6_000_000_000,
        name="early",
    )(b0, b1, b2, b3)
    back, best2, mass2 = call(
        packed_kernel,
        (shape((128, 128), f32), shape((8, ROWS), f32), shape((8, ROWS), f32)),
        scratch=(pltpu.VMEM((5 * PACKED, WIDE), bf16), pltpu.VMEM((5 * PACKED, WIDE), bf16))
        + state(BLOCK),
        flops=6_000_000_000,
        name="packed",
    )(b0, b1, b2, b3, b4, b5, *small)
    message = call(
        late_kernel,
        shape((128, 256), f32),
        scratch=state(ROWS) + (pltpu.VMEM((128, 128), f32),),
        flops=4_000_000_000,
        name="late",
    )(b0, b1, b2, b4, b5, best1, mass1, best2, mass2, back)
    answer = lax.all_to_all(message, AXES, split_axis=0, concat_axis=0, tiled=True)
    result = call(
        finish_kernel,
        shape((2, ROWS), f32),
        scratch=(pltpu.VMEM((128, 128), f32),),
        flops=ROWS * ROWS * 128,
        name="finish",
    )(answer, places)
    return (result[0], result[1]), over[0, 0]


def general(embeddings, labels, cluster_slot):
    groups = lax.axis_size("grp")
    members = lax.axis_size("blk")
    row_count, feature_count = embeddings.shape
    capacity = row_count // 4
    held = groups * capacity
    widened = embeddings.astype(jnp.float32)
    units = (
        widened * lax.rsqrt(jnp.sum(widened * widened, axis=1, keepdims=True) + epsilon)
    ).astype(jnp.bfloat16)
    slot_ids = cluster_slot[labels]
    owner_group = slot_ids // (cluster_slot.shape[0] // groups)
    owner_onehot = (owner_group[:, None] == jnp.arange(groups, dtype=jnp.int32)[None, :]).astype(
        jnp.int32
    )
    earlier = jnp.cumsum(owner_onehot, axis=0) - owner_onehot
    send_place = owner_group * capacity + jnp.sum(earlier * owner_onehot, axis=1)
    outgoing = jnp.zeros((held, feature_count), jnp.bfloat16).at[send_place].set(units)
    outgoing_slots = jnp.full((held,), -1, jnp.int32).at[send_place].set(slot_ids)
    rows = lax.all_to_all(outgoing, "grp", split_axis=0, concat_axis=0, tiled=True)
    slots = lax.all_to_all(outgoing_slots, "grp", split_axis=0, concat_axis=0, tiled=True)
    ring = [(i, (i + 1) % members) for i in range(members)]
    local = jnp.arange(held, dtype=jnp.int32)
    place = lax.axis_index("blk")
    own_ids = place * held + local

    def step(turn, carry):
        key_rows, key_slots, best, mass = carry
        scores = jnp.einsum("qd,kd->qk", rows, key_rows, preferred_element_type=jnp.float32)
        matched = (slots[:, None] == key_slots[None, :]) & (key_slots[None, :] >= 0)
        owner = (place - turn) & (members - 1)
        matched = matched & (own_ids[:, None] != (owner * held + local)[None, :])
        best = jnp.maximum(best, jnp.max(jnp.where(matched, scores, -1.0), axis=1))
        mass = mass + jnp.sum(
            jnp.where(matched, jnp.exp(sharpness * (scores - 1.0)), 0.0), axis=1
        )
        key_rows = lax.ppermute(key_rows, "blk", ring)
        key_slots = lax.ppermute(key_slots, "blk", ring)
        return key_rows, key_slots, best, mass

    start = (
        rows,
        slots,
        jnp.full((held,), -1.0, jnp.float32),
        jnp.zeros((held,), jnp.float32),
    )
    _, _, best, mass = lax.fori_loop(0, members, step, start)
    best = lax.all_to_all(best, "grp", split_axis=0, concat_axis=0, tiled=True)
    mass = lax.all_to_all(mass, "grp", split_axis=0, concat_axis=0, tiled=True)
    return (best[send_place], jnp.log1p(mass[send_place]))


def body(embeddings, labels, cluster_slot):
    result, over = fast(embeddings, labels, cluster_slot)
    return lax.cond(
        over > 0, lambda: general(embeddings, labels, cluster_slot), lambda: result
    )


def solution(mesh):
    placed = (P(AXES, None), P(AXES), P())
    return jax.shard_map(
        body,
        mesh=mesh,
        in_specs=placed,
        out_specs=(P(AXES), P(AXES)),
        check_vma=False,
    )
```

```python
import jax
import jax.numpy as jnp
from jax import lax
from jax.experimental import pallas as pl
from jax.experimental.pallas import tpu as pltpu
from jax.sharding import PartitionSpec as P

epsilon = 1e-06
sharpness = 8.0

ROWS = 512
FEAT = 768
WIDE = 896
GROUPS = 8
MEMBERS = 16
DEVICES = GROUPS * MEMBERS
SHARE = 8
HELD = DEVICES * SHARE
BLOCK = 640
SENT = BLOCK + 16
OFFSET = 16.0
LOG2E = 1.4426950408889634
AXES = ("grp", "blk")
VMEM_LIMIT = 56 * 1024 * 1024

SPOTS = ((0, 0), (1, 0), (0, 1), (0, 3), (2, 0), (0, 2))
ROW_BLOCKS = (1, 2)


def iota(shape, axis):
    return lax.broadcasted_iota(jnp.int32, shape, axis)


def matmul(a, b, dims, exact=False):
    return lax.dot_general(
        a,
        b,
        (dims, ((), ())),
        precision=lax.Precision.HIGHEST if exact else None,
        preferred_element_type=jnp.float32,
    )


NN = ((1,), (0,))
NT = ((1,), (1,))


def prelude_kernel(labels, slots, rows, spread, places):
    lab = labels[...]
    table = slots[...]
    by_cluster = (iota((ROWS, ROWS), 0) == lab).astype(jnp.bfloat16)
    sub = iota((8, ROWS), 0)
    parts = jnp.where(sub == 0, table >> 6, jnp.where(sub == 1, table & 63, 0)).astype(jnp.bfloat16)
    found = matmul(parts, by_cluster, NN)
    group = found[0:1].astype(jnp.int32)
    local = found[1:2].astype(jnp.int32)
    in_group = sub == group
    before = (iota((ROWS, ROWS), 0) < iota((ROWS, ROWS), 1)).astype(jnp.bfloat16)
    counts = matmul(in_group.astype(jnp.bfloat16), before, NN)
    rank = jnp.sum(jnp.where(in_group, counts, 0.0), axis=0, keepdims=True).astype(jnp.int32)
    holder = group * MEMBERS + ((rank + lax.axis_index("blk")) & (MEMBERS - 1))
    turn = rank >> 4
    places[...] = jnp.where(sub == 0, holder, turn)

    wide = rows[...].astype(jnp.float32)
    norm = lax.rsqrt(jnp.sum(wide * wide, axis=1, keepdims=True) + epsilon)
    units = (wide * norm).astype(jnp.bfloat16)
    lanes = iota((128, ROWS), 0)
    marks = jnp.where(lanes == local, 4.0, 0.0).astype(jnp.bfloat16)
    goal = holder * SHARE + turn
    totals = matmul(
        jnp.ones((128, ROWS), jnp.bfloat16), (lanes - 64 == group).astype(jnp.bfloat16), NT
    )
    totals = jnp.where((iota((128, 128), 0) & (SHARE - 1)) == 0, totals, 0.0)
    for t in range(HELD // 128):
        here = pl.ds(128 * t, 128)
        pick = (lanes + 128 * t == goal).astype(jnp.bfloat16)
        spread[here, :FEAT] = matmul(pick, units, NN).astype(jnp.bfloat16)
        spread[here, FEAT:] = (matmul(pick, marks, NT) + totals).astype(jnp.bfloat16)


def pack_kernel(arrived, packed, over):
    tails = arrived[:, FEAT:]
    own = iota((HELD, 128), 1) < 64
    counted = jnp.where(own, jnp.zeros_like(tails), tails)
    marks = jnp.where(own, tails, jnp.zeros_like(tails))
    one = ((iota((128, HELD), 0) * SHARE) == iota((128, HELD), 1)).astype(jnp.bfloat16)
    counts = matmul(one, counted, NN).astype(jnp.int32)
    turned = iota((128, 128), 0) & (MEMBERS - 1)
    most = jnp.zeros((1, 128), jnp.int32)
    for k in range(MEMBERS):
        gets = (counts + (MEMBERS - 1) - ((k - turned) & (MEMBERS - 1))) >> 4
        most = jnp.maximum(most, jnp.sum(gets, axis=0, keepdims=True))
    over[...] = jnp.broadcast_to((most > BLOCK).astype(jnp.int32), (8, 128))

    held = matmul(jnp.ones((8, 128), jnp.bfloat16), marks, NT) > 0.0
    before = (iota((HELD, HELD), 0) < iota((HELD, HELD), 1)).astype(jnp.bfloat16)
    position = matmul(held.astype(jnp.bfloat16), before, NN)
    position = jnp.where(held, position, -1.0)[0:1].astype(jnp.int32)
    at, line = iota((8, HELD), 1), iota((8, HELD), 0)
    names = jnp.where(line == 0, (at >> 3) + 1, jnp.where(line == 1, at & 7, 0))
    names = names.astype(jnp.bfloat16)
    named = []
    for t in range(BLOCK // 128):
        here = pl.ds(128 * t, 128)
        pick = (iota((128, HELD), 0) + 128 * t == position).astype(jnp.bfloat16)
        packed[here, :FEAT] = matmul(pick, arrived[:, :FEAT], NN).astype(jnp.bfloat16)
        packed[here, FEAT:] = matmul(pick, marks, NN).astype(jnp.bfloat16)
        named.append(matmul(names, pick, NT))
    named = jnp.concatenate(named + [jnp.zeros((8, WIDE - BLOCK), jnp.float32)], axis=1)
    named = jnp.concatenate([named, jnp.zeros_like(named)], axis=0)
    packed[BLOCK:, :] = named.astype(jnp.bfloat16)


def column_fold(x, op):
    while x.shape[0] > 8:
        half = x.shape[0] // 2
        x = op(x[:half], x[half:])
    return x


def row_fold(x, op):
    total = x[:, :128]
    for t in range(1, x.shape[1] // 128):
        total = op(total, x[:, 128 * t : 128 * (t + 1)])
    return total


def clear(*refs):
    for ref in refs:
        ref[...] = jnp.zeros_like(ref)


def tile(x, y, cols, rows, state, diagonal=False):
    col_best, col_mass, row_best, row_mass = state
    product = matmul(x, y, NT)
    if diagonal:
        shape = product.shape
        product = jnp.where(iota(shape, 0) == iota(shape, 1), 0.0, product)
    soft = jnp.exp2((product - (OFFSET + 1.0)) * (sharpness * LOG2E))
    for first, size, c, start in cols:
        part = slice(first, first + size)
        here = slice(start, start + size)
        col_best[c, :, here] = jnp.maximum(
            col_best[c, :, here], column_fold(product[:, part], jnp.maximum)
        )
        col_mass[c, :, here] = col_mass[c, :, here] + column_fold(soft[:, part], jnp.add)
    for first, size, r, start in rows:
        part = slice(first, first + size)
        here = slice(start, start + size)
        row_best[r, here, :] = jnp.maximum(
            row_best[r, here, :], row_fold(product[part], jnp.maximum)
        )
        row_mass[r, here, :] = row_mass[r, here, :] + row_fold(soft[part], jnp.add)


PARTS = ((0, 256), (256, 256), (512, 128))


def square(rows, cols, c, r, state, own=False):
    for i, tall in PARTS:
        for j, wide in PARTS:
            tile(
                rows[i : i + tall, :],
                cols[j : j + wide, :],
                [(0, wide, c, j)],
                [] if r is None else [(0, tall, r, i)],
                state,
                own and i == j,
            )


def settle(e, state):
    col_best, col_mass, row_best, row_mass = state
    best = jnp.max(col_best[e], axis=0, keepdims=True)
    mass = jnp.sum(col_mass[e], axis=0, keepdims=True)
    if e in ROW_BLOCKS:
        r = ROW_BLOCKS.index(e)
        tops, sums = [], []
        for t in range(0, BLOCK, 128):
            tops.append(jnp.max(row_best[r, t : t + 128, :].T, axis=0, keepdims=True))
            sums.append(jnp.sum(row_mass[r, t : t + 128, :].T, axis=0, keepdims=True))
        best = jnp.maximum(best, jnp.concatenate(tops, axis=1))
        mass = mass + jnp.concatenate(sums, axis=1)
    return best, mass


def similarity(best):
    return jnp.where(best > 0.5 * OFFSET, jnp.maximum(best - OFFSET, -1.0), -1.0)


def early_kernel(b0, b1, b2, b3, best_out, mass_out, *state):
    clear(best_out, mass_out, *state)
    square(b0, b0, 0, None, state, True)
    square(b1, b0, 0, 0, state)
    square(b2, b0, 0, 1, state)
    square(b1, b3, 3, 0, state)
    square(b1, b2, 2, 0, state)
    square(b3, b2, 2, None, state)
    for e in range(4):
        best_out[e : e + 1, :], mass_out[e : e + 1, :] = settle(e, state)


def late_kernel(b0, b1, b2, b3, b4, b5, best_in, mass_in, out, *state):
    clear(*state)
    square(b4, b0, 0, None, state)
    square(b4, b5, 5, None, state)
    square(b1, b5, 5, 0, state)
    square(b2, b4, 4, 1, state)
    source_at = iota((DEVICES, BLOCK), 0) + 1
    column = iota((128, BLOCK), 0)
    back = jnp.zeros((DEVICES, 128), jnp.float32)
    for e, block in enumerate((b0, b1, b2, b3, b4, b5)):
        best, mass = settle(e, state)
        best = similarity(jnp.maximum(best, best_in[e : e + 1, :]))
        mass = mass + mass_in[e : e + 1, :]
        names = block[BLOCK:, :BLOCK].astype(jnp.int32)
        source, turn = names[0:1], names[1:2]
        spot = column - 16 * e
        values = jnp.where(
            (spot >= 0) & (spot < 16) & ((spot >> 1) == turn),
            jnp.where((spot & 1) == 0, best, mass),
            0.0,
        )
        back = back + matmul((source_at == source).astype(jnp.float32), values, NT, exact=True)
    out[...] = back


def finish_kernel(arrived, places, result):
    shape = (DEVICES, DEVICES)
    at, col = iota(shape, 0), iota(shape, 1)
    base, ay, az = at >> 4, (at >> 2) & 3, at & 3
    turned = (base & 1) == 1
    best = mass = None
    for e, (dy, dz) in enumerate(SPOTS):
        by = (ay + jnp.where(turned, dy, (-dy) & 3)) & 3
        bz = (az + jnp.where(turned, dz, (-dz) & 3)) & 3
        move = (col == base * MEMBERS + by * 4 + bz).astype(jnp.float32)
        moved = matmul(move, arrived[...], NN, exact=True)
        if e:
            moved = pltpu.roll(moved, 128 - 16 * e, 1)
        best = moved if best is None else jnp.maximum(best, moved)
        mass = moved if mass is None else mass + moved
    merged = jnp.where((col & 1) == 0, best, mass)
    sub = iota((128, ROWS), 0)
    holder = (sub == places[0:1, :]).astype(jnp.float32)
    picked = matmul(merged.T, holder, NN, exact=True)
    turn = places[1:2, :]
    best = jnp.sum(jnp.where(sub == 2 * turn, picked, 0.0), axis=0, keepdims=True)
    mass = jnp.sum(jnp.where(sub == 2 * turn + 1, picked, 0.0), axis=0, keepdims=True)
    result[0:1, :] = best
    result[1:2, :] = jnp.log1p(mass)


def call(kernel, out_shape, scratch=(), flops=0, name=None):
    return pl.pallas_call(
        kernel,
        out_shape=out_shape,
        scratch_shapes=scratch,
        compiler_params=pltpu.CompilerParams(vmem_limit_bytes=VMEM_LIMIT),
        cost_estimate=pl.CostEstimate(flops=flops, bytes_accessed=8_000_000, transcendentals=0),
        name=name,
    )


def hop(dy, dz):
    pairs = []
    for g in range(GROUPS):
        turn = -1 if g & 1 else 1
        for y in range(4):
            for z in range(4):
                source = ((y + turn * dy) % 4) * 4 + (z + turn * dz) % 4
                pairs.append((g * MEMBERS + source, g * MEMBERS + y * 4 + z))
    return pairs


def from_spot(x, dy, dz):
    return lax.ppermute(x, AXES, hop(dy, dz))


def fast(embeddings, labels, cluster_slot):
    f32, bf16, i32 = jnp.float32, jnp.bfloat16, jnp.int32
    shape = jax.ShapeDtypeStruct
    spread, places = call(
        prelude_kernel,
        (shape((HELD, WIDE), bf16), shape((8, ROWS), i32)),
        flops=3_000_000_000,
        name="prelude",
    )(labels.reshape(1, ROWS), cluster_slot.reshape(1, ROWS), embeddings)
    arrived = lax.all_to_all(spread, AXES, split_axis=0, concat_axis=0, tiled=True)
    b0, over = call(
        pack_kernel,
        (shape((SENT, WIDE), bf16), shape((8, 128), i32)),
        flops=3_000_000_000,
        name="pack",
    )(arrived)
    b2 = from_spot(b0, 0, 1)
    b3 = from_spot(b0, 0, 3)
    b1 = from_spot(b0, 1, 0)
    b4 = from_spot(b1, 1, 0)
    b5 = from_spot(b2, 0, 1)
    state = (
        pltpu.VMEM((6, 8, BLOCK), f32),
        pltpu.VMEM((6, 8, BLOCK), f32),
        pltpu.VMEM((2, BLOCK, 128), f32),
        pltpu.VMEM((2, BLOCK, 128), f32),
    )
    best, mass = call(
        early_kernel,
        (shape((8, BLOCK), f32), shape((8, BLOCK), f32)),
        scratch=state,
        flops=6_000_000_000,
        name="early",
    )(b0, b1, b2, b3)
    message = call(
        late_kernel,
        shape((DEVICES, 128), f32),
        scratch=state,
        flops=4_000_000_000,
        name="late",
    )(b0, b1, b2, b3, b4, b5, best, mass)
    answer = lax.all_to_all(message, AXES, split_axis=0, concat_axis=0, tiled=True)
    result = call(
        finish_kernel, shape((2, ROWS), f32), flops=ROWS * ROWS * 128, name="finish"
    )(answer, places)
    return (result[0], result[1]), jnp.max(over)


def general(embeddings, labels, cluster_slot):
    groups = lax.axis_size("grp")
    members = lax.axis_size("blk")
    row_count, feature_count = embeddings.shape
    capacity = row_count // 4
    held = groups * capacity
    widened = embeddings.astype(jnp.float32)
    units = (
        widened * lax.rsqrt(jnp.sum(widened * widened, axis=1, keepdims=True) + epsilon)
    ).astype(jnp.bfloat16)
    slot_ids = cluster_slot[labels]
    owner_group = slot_ids // (cluster_slot.shape[0] // groups)
    owner_onehot = (owner_group[:, None] == jnp.arange(groups, dtype=jnp.int32)[None, :]).astype(
        jnp.int32
    )
    earlier = jnp.cumsum(owner_onehot, axis=0) - owner_onehot
    send_place = owner_group * capacity + jnp.sum(earlier * owner_onehot, axis=1)
    outgoing = jnp.zeros((held, feature_count), jnp.bfloat16).at[send_place].set(units)
    outgoing_slots = jnp.full((held,), -1, jnp.int32).at[send_place].set(slot_ids)
    rows = lax.all_to_all(outgoing, "grp", split_axis=0, concat_axis=0, tiled=True)
    slots = lax.all_to_all(outgoing_slots, "grp", split_axis=0, concat_axis=0, tiled=True)
    ring = [(i, (i + 1) % members) for i in range(members)]
    local = jnp.arange(held, dtype=jnp.int32)
    place = lax.axis_index("blk")
    own_ids = place * held + local

    def step(turn, carry):
        key_rows, key_slots, best, mass = carry
        scores = jnp.einsum("qd,kd->qk", rows, key_rows, preferred_element_type=jnp.float32)
        matched = (slots[:, None] == key_slots[None, :]) & (key_slots[None, :] >= 0)
        owner = (place - turn) & (members - 1)
        matched = matched & (own_ids[:, None] != (owner * held + local)[None, :])
        best = jnp.maximum(best, jnp.max(jnp.where(matched, scores, -1.0), axis=1))
        mass = mass + jnp.sum(
            jnp.where(matched, jnp.exp(sharpness * (scores - 1.0)), 0.0), axis=1
        )
        key_rows = lax.ppermute(key_rows, "blk", ring)
        key_slots = lax.ppermute(key_slots, "blk", ring)
        return key_rows, key_slots, best, mass

    start = (
        rows,
        slots,
        jnp.full((held,), -1.0, jnp.float32),
        jnp.zeros((held,), jnp.float32),
    )
    _, _, best, mass = lax.fori_loop(0, members, step, start)
    best = lax.all_to_all(best, "grp", split_axis=0, concat_axis=0, tiled=True)
    mass = lax.all_to_all(mass, "grp", split_axis=0, concat_axis=0, tiled=True)
    return (best[send_place], jnp.log1p(mass[send_place]))


def body(embeddings, labels, cluster_slot):
    result, over = fast(embeddings, labels, cluster_slot)
    return lax.cond(
        over > 0, lambda: general(embeddings, labels, cluster_slot), lambda: result
    )


def solution(mesh):
    placed = (P(AXES, None), P(AXES), P())
    return jax.shard_map(
        body,
        mesh=mesh,
        in_specs=placed,
        out_specs=(P(AXES), P(AXES)),
        check_vma=False,
    )
```

```python
import jax
import jax.numpy as jnp
from jax import lax
from jax.experimental import pallas as pl
from jax.experimental.pallas import tpu as pltpu
from jax.sharding import PartitionSpec as P

epsilon = 1e-06
sharpness = 8.0

ROWS = 512
FEAT = 768
WIDE = 896
GROUPS = 8
MEMBERS = 16
DEVICES = GROUPS * MEMBERS
SHARE = 8
HELD = DEVICES * SHARE
BLOCK = 640
ROOM = BLOCK - 16
APART = -64.0
LOG2E = 1.4426950408889634
AXES = ("grp", "blk")
VMEM_LIMIT = 56 * 1024 * 1024

SPOTS = ((0, 0), (1, 0), (0, 1), (0, 3), (2, 0), (0, 2))
ROW_BLOCKS = (1, 2)


def iota(shape, axis):
    return lax.broadcasted_iota(jnp.int32, shape, axis)


def matmul(a, b, dims, exact=False):
    return lax.dot_general(
        a,
        b,
        (dims, ((), ())),
        precision=lax.Precision.HIGHEST if exact else None,
        preferred_element_type=jnp.float32,
    )


NN = ((1,), (0,))
NT = ((1,), (1,))


def split(x):
    high = x.astype(jnp.bfloat16)
    rest = x - high.astype(jnp.float32)
    middle = rest.astype(jnp.bfloat16)
    low = (rest - middle.astype(jnp.float32)).astype(jnp.bfloat16)
    return jnp.concatenate([high, middle, low], axis=0)


def joined(x):
    size = x.shape[0] // 3
    return x[:size] + x[size : 2 * size] + x[2 * size :]


def prelude_kernel(labels, slots, rows, spread, places):
    lab = labels[...]
    table = slots[...]
    by_cluster = (iota((ROWS, ROWS), 0) == lab).astype(jnp.bfloat16)
    sub = iota((8, ROWS), 0)
    parts = jnp.where(sub == 0, table >> 6, jnp.where(sub == 1, table & 63, 0)).astype(jnp.bfloat16)
    found = matmul(parts, by_cluster, NN)
    group = found[0:1].astype(jnp.int32)
    in_group = sub == group
    before = (iota((ROWS, ROWS), 0) < iota((ROWS, ROWS), 1)).astype(jnp.bfloat16)
    counts = matmul(in_group.astype(jnp.bfloat16), before, NN)
    rank = jnp.sum(jnp.where(in_group, counts, 0.0), axis=0, keepdims=True).astype(jnp.int32)
    holder = group * MEMBERS + ((rank + lax.axis_index("blk")) & (MEMBERS - 1))
    turn = rank >> 4
    places[...] = jnp.where(sub == 0, holder, turn)

    wide = rows[...].astype(jnp.float32)
    norm = lax.rsqrt(jnp.sum(wide * wide, axis=1, keepdims=True) + epsilon)
    units = (wide * norm).astype(jnp.bfloat16)
    lanes = iota((128, ROWS), 0)
    marks = jnp.where(lanes == 0, found[1:2] + 1.0, 0.0).astype(jnp.bfloat16)
    goal = holder * SHARE + turn
    totals = matmul(
        jnp.ones((128, ROWS), jnp.bfloat16), (lanes - 64 == group).astype(jnp.bfloat16), NT
    )
    totals = jnp.where((iota((ROWS, 128), 0) & (SHARE - 1)) == 0, totals[0:1], 0.0)
    for t in range(0, HELD, ROWS):
        here = pl.ds(t, ROWS)
        pick = (iota((ROWS, ROWS), 0) + t == goal).astype(jnp.bfloat16)
        spread[here, :FEAT] = matmul(pick, units, NN).astype(jnp.bfloat16)
        spread[here, FEAT:] = (matmul(pick, marks, NT) + totals).astype(jnp.bfloat16)


def pack_kernel(arrived, packed, over):
    tails = arrived[:, FEAT:]
    one = ((iota((128, HELD), 0) * SHARE) == iota((128, HELD), 1)).astype(jnp.bfloat16)
    counts = matmul(one, tails, NN).astype(jnp.int32)
    counts = jnp.where(iota((128, 128), 1) >= 64, counts, 0)
    turned = iota((128, 128), 0) & (MEMBERS - 1)
    most = jnp.zeros((1, 128), jnp.int32)
    for k in range(MEMBERS):
        gets = (counts + (MEMBERS - 1) - ((k - turned) & (MEMBERS - 1))) >> 4
        most = jnp.maximum(most, jnp.sum(gets, axis=0, keepdims=True))
    over[...] = jnp.broadcast_to((most > ROOM).astype(jnp.int32), (8, 128))

    at, line = iota((8, HELD), 1), iota((8, HELD), 0)
    clusters = matmul((iota((8, 128), 1) == 0).astype(jnp.bfloat16), tails, NT)
    held = clusters > 0.0
    before = (iota((HELD, HELD), 0) < iota((HELD, HELD), 1)).astype(jnp.bfloat16)
    position = matmul(held.astype(jnp.bfloat16), before, NN)
    position = jnp.where(held, position, -1.0)[0:1].astype(jnp.int32)
    names = jnp.where(line == 1, (at >> 3) + 1, jnp.where(line == 2, at & 7, 0))
    names = jnp.where(line == 0, clusters, names.astype(jnp.float32)).astype(jnp.bfloat16)
    pick = (iota((BLOCK, HELD), 0) == position).astype(jnp.bfloat16)
    packed[:ROOM, :] = matmul(pick[:ROOM], arrived[:, :FEAT], NN).astype(jnp.bfloat16)
    named = matmul(names, pick, NT)
    named = jnp.concatenate([named, jnp.zeros((8, FEAT - BLOCK), jnp.float32)], axis=1)
    packed[ROOM:, :] = jnp.concatenate([named, jnp.zeros_like(named)], axis=0).astype(jnp.bfloat16)


def column_fold(x, op):
    while x.shape[0] > 8:
        half = x.shape[0] // 2
        x = op(x[:half], x[half:])
    return x


def row_fold(x, op):
    total = x[:, :128]
    for t in range(1, x.shape[1] // 128):
        total = op(total, x[:, 128 * t : 128 * (t + 1)])
    return total


PARTS = ((0, 256), (256, 256), (512, 128))


def clear(state):
    col_best, col_mass, row_best, row_mass = state[:4]
    for ref in (col_best, row_best):
        ref[...] = jnp.full_like(ref, APART)
    for ref in (col_mass, row_mass):
        ref[...] = jnp.zeros_like(ref)


def names_of(block):
    return block[ROOM:, :BLOCK].astype(jnp.float32)


def spell(block, place, state):
    clusters = names_of(block)[0:1]
    clusters = jnp.where(clusters > 0.0, clusters, -1.0)
    for t in range(0, BLOCK, 128):
        here = slice(t, t + 128)
        state[4][place, here, :] = jnp.broadcast_to(clusters[:, here], (128, 128)).T


def square(rows, cols, place, c, r, state, own=False):
    col_best, col_mass, row_best, row_mass, spelt = state
    clusters = names_of(cols)[0:1]
    for i, tall in PARTS:
        for j, wide in PARTS:
            product = matmul(rows[i : i + tall, :], cols[j : j + wide, :], NT)
            down = slice(i, i + tall)
            mine = spelt[place, down, :]
            tops = sums = None
            for t in range(0, wide, 128):
                across = slice(j + t, j + t + 128)
                match = mine == clusters[:, across]
                if own and i == j:
                    match = match & (iota((tall, 128), 0) != iota((tall, 128), 1) + t)
                score = jnp.where(match, product[:, t : t + 128], APART)
                soft = jnp.exp2((score - 1.0) * (sharpness * LOG2E))
                col_best[c, :, across] = jnp.maximum(
                    col_best[c, :, across], column_fold(score, jnp.maximum)
                )
                col_mass[c, :, across] = col_mass[c, :, across] + column_fold(soft, jnp.add)
                tops = score if tops is None else jnp.maximum(tops, score)
                sums = soft if sums is None else sums + soft
            if r is not None:
                row_best[r, down, :] = jnp.maximum(row_best[r, down, :], tops)
                row_mass[r, down, :] = row_mass[r, down, :] + sums


def settle(e, state):
    col_best, col_mass, row_best, row_mass = state[:4]
    best = jnp.max(col_best[e], axis=0, keepdims=True)
    mass = jnp.sum(col_mass[e], axis=0, keepdims=True)
    if e in ROW_BLOCKS:
        r = ROW_BLOCKS.index(e)
        tops, sums = [], []
        for t in range(0, BLOCK, 128):
            tops.append(jnp.max(row_best[r, t : t + 128, :].T, axis=0, keepdims=True))
            sums.append(jnp.sum(row_mass[r, t : t + 128, :].T, axis=0, keepdims=True))
        best = jnp.maximum(best, jnp.concatenate(tops, axis=1))
        mass = mass + jnp.concatenate(sums, axis=1)
    return best, mass


def early_kernel(b0, b1, b2, b3, best_out, mass_out, *state):
    clear(state)
    for place, block in enumerate((b0, b1, b2, b3)):
        spell(block, place, state)
    square(b0, b0, 0, 0, None, state, True)
    square(b1, b0, 1, 0, 0, state)
    square(b2, b0, 2, 0, 1, state)
    square(b1, b3, 1, 3, 0, state)
    square(b1, b2, 1, 2, 0, state)
    square(b3, b2, 3, 2, None, state)
    best_out[...] = jnp.full_like(best_out, APART)
    mass_out[...] = jnp.zeros_like(mass_out)
    for e in range(4):
        best_out[e : e + 1, :], mass_out[e : e + 1, :] = settle(e, state)


def late_kernel(b0, b1, b2, b3, b4, b5, best_in, mass_in, out, *state):
    clear(state)
    for place, block in enumerate((b4, b1, b2)):
        spell(block, place, state)
    square(b4, b0, 0, 0, None, state)
    square(b4, b5, 0, 5, None, state)
    square(b1, b5, 1, 5, 0, state)
    square(b2, b4, 2, 4, 1, state)
    source_at = (iota((DEVICES, BLOCK), 0) + 1).astype(jnp.float32)
    line = iota((16, BLOCK), 0)
    back = []
    for e, block in enumerate((b0, b1, b2, b3, b4, b5)):
        best, mass = settle(e, state)
        best = jnp.maximum(jnp.maximum(best, best_in[e : e + 1, :]), -1.0)
        mass = mass + mass_in[e : e + 1, :]
        names = names_of(block)
        values = jnp.where((line & 1) == 0, best, mass)
        values = jnp.where((line >> 1).astype(jnp.float32) == names[2:3], values, 0.0)
        to = (source_at == names[1:2]).astype(jnp.bfloat16)
        back.append(joined(matmul(split(values), to, NT)))
    back.append(jnp.zeros((128 - 16 * len(back), DEVICES), jnp.float32))
    out[...] = jnp.concatenate(back, axis=0).T


def finish_kernel(arrived, places, best_out, mass_out):
    shape = (DEVICES, DEVICES)
    at, col = iota(shape, 0), iota(shape, 1)
    base, ay, az = at >> 4, (at >> 2) & 3, at & 3
    turned = (base & 1) == 1
    best = mass = None
    pieces = split(arrived[...].T)
    for e, (dy, dz) in enumerate(SPOTS):
        by = (ay + jnp.where(turned, dy, (-dy) & 3)) & 3
        bz = (az + jnp.where(turned, dz, (-dz) & 3)) & 3
        move = (col == base * MEMBERS + by * 4 + bz).astype(jnp.bfloat16)
        part = jnp.concatenate(
            [pieces[128 * p + 16 * e : 128 * p + 16 * e + 16] for p in range(3)], axis=0
        )
        moved = joined(matmul(part, move, NT))
        best = moved if best is None else jnp.maximum(best, moved)
        mass = moved if mass is None else mass + moved
    merged = jnp.where((iota((16, DEVICES), 0) & 1) == 0, best, mass)
    holder = (iota((DEVICES, ROWS), 0) == places[0:1, :]).astype(jnp.bfloat16)
    picked = joined(matmul(split(merged), holder, NN))
    line = iota((16, ROWS), 0)
    turn = places[1:2, :]
    best_out[...] = jnp.sum(jnp.where(line == 2 * turn, picked, 0.0), axis=0, keepdims=True)
    mass = jnp.sum(jnp.where(line == 2 * turn + 1, picked, 0.0), axis=0, keepdims=True)
    mass_out[...] = jnp.log1p(mass)


def call(kernel, out_shape, scratch=(), flops=0, name=None):
    return pl.pallas_call(
        kernel,
        out_shape=out_shape,
        scratch_shapes=scratch,
        compiler_params=pltpu.CompilerParams(vmem_limit_bytes=VMEM_LIMIT),
        cost_estimate=pl.CostEstimate(flops=flops, bytes_accessed=8_000_000, transcendentals=0),
        name=name,
    )


def hop(dy, dz):
    pairs = []
    for g in range(GROUPS):
        turn = -1 if g & 1 else 1
        for y in range(4):
            for z in range(4):
                source = ((y + turn * dy) % 4) * 4 + (z + turn * dz) % 4
                pairs.append((g * MEMBERS + source, g * MEMBERS + y * 4 + z))
    return pairs


def from_spot(x, dy, dz):
    return lax.ppermute(x, AXES, hop(dy, dz))


def fast(embeddings, labels, cluster_slot):
    f32, bf16, i32 = jnp.float32, jnp.bfloat16, jnp.int32
    shape = jax.ShapeDtypeStruct
    spread, places = call(
        prelude_kernel,
        (shape((HELD, WIDE), bf16), shape((8, ROWS), i32)),
        flops=3_000_000_000,
        name="prelude",
    )(labels.reshape(1, ROWS), cluster_slot.reshape(1, ROWS), embeddings)
    arrived = lax.all_to_all(spread, AXES, split_axis=0, concat_axis=0, tiled=True)
    b0, over = call(
        pack_kernel,
        (shape((BLOCK, FEAT), bf16), shape((8, 128), i32)),
        flops=3_000_000_000,
        name="pack",
    )(arrived)
    b2 = from_spot(b0, 0, 1)
    b3 = from_spot(b0, 0, 3)
    b1 = from_spot(b0, 1, 0)
    b4 = from_spot(b1, 1, 0)
    b5 = from_spot(b2, 0, 1)

    def state(places):
        return (
            pltpu.VMEM((6, 8, BLOCK), f32),
            pltpu.VMEM((6, 8, BLOCK), f32),
            pltpu.VMEM((2, BLOCK, 128), f32),
            pltpu.VMEM((2, BLOCK, 128), f32),
            pltpu.VMEM((places, BLOCK, 128), f32),
        )

    best, mass = call(
        early_kernel,
        (shape((8, BLOCK), f32), shape((8, BLOCK), f32)),
        scratch=state(4),
        flops=6_000_000_000,
        name="early",
    )(b0, b1, b2, b3)
    message = call(
        late_kernel,
        shape((DEVICES, 128), f32),
        scratch=state(3),
        flops=4_000_000_000,
        name="late",
    )(b0, b1, b2, b3, b4, b5, best, mass)
    answer = lax.all_to_all(message, AXES, split_axis=0, concat_axis=0, tiled=True)
    best, mass = call(
        finish_kernel,
        (shape((1, ROWS), f32), shape((1, ROWS), f32)),
        flops=ROWS * ROWS * 128,
        name="finish",
    )(answer, places)
    return (best.reshape(ROWS), mass.reshape(ROWS)), jnp.max(over)


def general(embeddings, labels, cluster_slot):
    groups = lax.axis_size("grp")
    members = lax.axis_size("blk")
    row_count, feature_count = embeddings.shape
    capacity = row_count // 4
    held = groups * capacity
    widened = embeddings.astype(jnp.float32)
    units = (
        widened * lax.rsqrt(jnp.sum(widened * widened, axis=1, keepdims=True) + epsilon)
    ).astype(jnp.bfloat16)
    slot_ids = cluster_slot[labels]
    owner_group = slot_ids // (cluster_slot.shape[0] // groups)
    owner_onehot = (owner_group[:, None] == jnp.arange(groups, dtype=jnp.int32)[None, :]).astype(
        jnp.int32
    )
    earlier = jnp.cumsum(owner_onehot, axis=0) - owner_onehot
    send_place = owner_group * capacity + jnp.sum(earlier * owner_onehot, axis=1)
    outgoing = jnp.zeros((held, feature_count), jnp.bfloat16).at[send_place].set(units)
    outgoing_slots = jnp.full((held,), -1, jnp.int32).at[send_place].set(slot_ids)
    rows = lax.all_to_all(outgoing, "grp", split_axis=0, concat_axis=0, tiled=True)
    slots = lax.all_to_all(outgoing_slots, "grp", split_axis=0, concat_axis=0, tiled=True)
    ring = [(i, (i + 1) % members) for i in range(members)]
    local = jnp.arange(held, dtype=jnp.int32)
    place = lax.axis_index("blk")
    own_ids = place * held + local

    def step(turn, carry):
        key_rows, key_slots, best, mass = carry
        scores = jnp.einsum("qd,kd->qk", rows, key_rows, preferred_element_type=jnp.float32)
        matched = (slots[:, None] == key_slots[None, :]) & (key_slots[None, :] >= 0)
        owner = (place - turn) & (members - 1)
        matched = matched & (own_ids[:, None] != (owner * held + local)[None, :])
        best = jnp.maximum(best, jnp.max(jnp.where(matched, scores, -1.0), axis=1))
        mass = mass + jnp.sum(
            jnp.where(matched, jnp.exp(sharpness * (scores - 1.0)), 0.0), axis=1
        )
        key_rows = lax.ppermute(key_rows, "blk", ring)
        key_slots = lax.ppermute(key_slots, "blk", ring)
        return key_rows, key_slots, best, mass

    start = (
        rows,
        slots,
        jnp.full((held,), -1.0, jnp.float32),
        jnp.zeros((held,), jnp.float32),
    )
    _, _, best, mass = lax.fori_loop(0, members, step, start)
    best = lax.all_to_all(best, "grp", split_axis=0, concat_axis=0, tiled=True)
    mass = lax.all_to_all(mass, "grp", split_axis=0, concat_axis=0, tiled=True)
    return (best[send_place], jnp.log1p(mass[send_place]))


def body(embeddings, labels, cluster_slot):
    result, over = fast(embeddings, labels, cluster_slot)
    return lax.cond(
        over > 0, lambda: general(embeddings, labels, cluster_slot), lambda: result
    )


def solution(mesh):
    placed = (P(AXES, None), P(AXES), P())
    return jax.shard_map(
        body,
        mesh=mesh,
        in_specs=placed,
        out_specs=(P(AXES), P(AXES)),
        check_vma=False,
    )
```

```python
import jax
import jax.numpy as jnp
from jax import lax
from jax.experimental import pallas as pl
from jax.experimental.pallas import tpu as pltpu
from jax.sharding import PartitionSpec as P

epsilon = 1e-06
sharpness = 8.0

ROWS = 512
FEAT = 768
WIDE = 896
GROUPS = 8
MEMBERS = 16
DEVICES = GROUPS * MEMBERS
SHARE = 8
HELD = DEVICES * SHARE
BLOCK = 640
ROOM = BLOCK - 16
APART = -64.0
LOG2E = 1.4426950408889634
AXES = ("grp", "blk")
VMEM_LIMIT = 24 * 1024 * 1024

SPOTS = ((0, 0), (1, 0), (0, 1), (0, 3), (2, 0), (0, 2))
ROW_BLOCKS = (1, 2)


def iota(shape, axis):
    return lax.broadcasted_iota(jnp.int32, shape, axis)


def matmul(a, b, dims, exact=False):
    return lax.dot_general(
        a,
        b,
        (dims, ((), ())),
        precision=lax.Precision.HIGHEST if exact else None,
        preferred_element_type=jnp.float32,
    )


NN = ((1,), (0,))
NT = ((1,), (1,))


def split(x):
    high = x.astype(jnp.bfloat16)
    rest = x - high.astype(jnp.float32)
    middle = rest.astype(jnp.bfloat16)
    low = (rest - middle.astype(jnp.float32)).astype(jnp.bfloat16)
    return jnp.concatenate([high, middle, low], axis=0)


def joined(x):
    size = x.shape[0] // 3
    return x[:size] + x[size : 2 * size] + x[2 * size :]


def prelude_kernel(labels, slots, rows, spread, places):
    lab = labels[...]
    table = slots[...]
    by_cluster = (iota((ROWS, ROWS), 0) == lab).astype(jnp.bfloat16)
    sub = iota((8, ROWS), 0)
    parts = jnp.where(sub == 0, table >> 6, jnp.where(sub == 1, table & 63, 0)).astype(jnp.bfloat16)
    found = matmul(parts, by_cluster, NN)
    group = found[0:1].astype(jnp.int32)
    in_group = sub == group
    before = (iota((ROWS, ROWS), 0) < iota((ROWS, ROWS), 1)).astype(jnp.bfloat16)
    counts = matmul(in_group.astype(jnp.bfloat16), before, NN)
    rank = jnp.sum(jnp.where(in_group, counts, 0.0), axis=0, keepdims=True).astype(jnp.int32)
    holder = group * MEMBERS + ((rank + lax.axis_index("blk")) & (MEMBERS - 1))
    turn = rank >> 4
    places[...] = jnp.where(sub == 0, holder, turn)

    wide = rows[...].astype(jnp.float32)
    norm = lax.rsqrt(jnp.sum(wide * wide, axis=1, keepdims=True) + epsilon)
    units = (wide * norm).astype(jnp.bfloat16)
    lanes = iota((128, ROWS), 0)
    marks = jnp.where(lanes == 0, found[1:2] + 1.0, 0.0).astype(jnp.bfloat16)
    goal = holder * SHARE + turn
    totals = matmul(
        jnp.ones((128, ROWS), jnp.bfloat16), (lanes - 64 == group).astype(jnp.bfloat16), NT
    )
    totals = jnp.where((iota((ROWS, 128), 0) & (SHARE - 1)) == 0, totals[0:1], 0.0)
    for t in range(0, HELD, ROWS):
        here = pl.ds(t, ROWS)
        pick = (iota((ROWS, ROWS), 0) + t == goal).astype(jnp.bfloat16)
        spread[here, :FEAT] = matmul(pick, units, NN).astype(jnp.bfloat16)
        spread[here, FEAT:] = (matmul(pick, marks, NT) + totals).astype(jnp.bfloat16)


def pack_kernel(arrived, packed, over):
    tails = arrived[:, FEAT:]
    one = ((iota((128, HELD), 0) * SHARE) == iota((128, HELD), 1)).astype(jnp.bfloat16)
    counts = matmul(one, tails, NN).astype(jnp.int32)
    counts = jnp.where(iota((128, 128), 1) >= 64, counts, 0)
    turned = iota((128, 128), 0) & (MEMBERS - 1)
    most = jnp.zeros((1, 128), jnp.int32)
    for k in range(MEMBERS):
        gets = (counts + (MEMBERS - 1) - ((k - turned) & (MEMBERS - 1))) >> 4
        most = jnp.maximum(most, jnp.sum(gets, axis=0, keepdims=True))
    over[...] = jnp.broadcast_to((most > ROOM).astype(jnp.int32), (8, 128))

    at, line = iota((8, HELD), 1), iota((8, HELD), 0)
    clusters = matmul((iota((8, 128), 1) == 0).astype(jnp.bfloat16), tails, NT)
    held = clusters > 0.0
    before = (iota((HELD, HELD), 0) < iota((HELD, HELD), 1)).astype(jnp.bfloat16)
    position = matmul(held.astype(jnp.bfloat16), before, NN)
    position = jnp.where(held, position, -1.0)[0:1].astype(jnp.int32)
    names = jnp.where(line == 1, (at >> 3) + 1, jnp.where(line == 2, at & 7, 0))
    names = jnp.where(line == 0, clusters, names.astype(jnp.float32)).astype(jnp.bfloat16)
    pick = (iota((BLOCK, HELD), 0) == position).astype(jnp.bfloat16)
    packed[:ROOM, :] = matmul(pick[:ROOM], arrived[:, :FEAT], NN).astype(jnp.bfloat16)
    named = matmul(names, pick, NT)
    named = jnp.concatenate([named, jnp.zeros((8, FEAT - BLOCK), jnp.float32)], axis=1)
    packed[ROOM:, :] = jnp.concatenate([named, jnp.zeros_like(named)], axis=0).astype(jnp.bfloat16)


def column_fold(x, op):
    while x.shape[0] > 8:
        half = x.shape[0] // 2
        x = op(x[:half], x[half:])
    return x


def row_fold(x, op):
    total = x[:, :128]
    for t in range(1, x.shape[1] // 128):
        total = op(total, x[:, 128 * t : 128 * (t + 1)])
    return total


PARTS = ((0, 256), (256, 256), (512, 128))


def clear(state):
    col_best, col_mass, row_best, row_mass = state[:4]
    for ref in (col_best, row_best):
        ref[...] = jnp.full_like(ref, APART)
    for ref in (col_mass, row_mass):
        ref[...] = jnp.zeros_like(ref)


def names_of(block):
    return block[ROOM:, :BLOCK].astype(jnp.float32)


def spell(block, place, state):
    clusters = names_of(block)[0:1]
    clusters = jnp.where(clusters > 0.0, clusters, -1.0)
    for t in range(0, BLOCK, 128):
        here = slice(t, t + 128)
        state[4][place, here, :] = jnp.broadcast_to(clusters[:, here], (128, 128)).T


def square(rows, cols, place, c, r, state, own=False):
    col_best, col_mass, row_best, row_mass, spelt = state
    clusters = names_of(cols)[0:1]
    for i, tall in PARTS:
        for j, wide in PARTS:
            product = matmul(rows[i : i + tall, :], cols[j : j + wide, :], NT)
            down = slice(i, i + tall)
            mine = spelt[place, down, :]
            tops = sums = None
            for t in range(0, wide, 128):
                across = slice(j + t, j + t + 128)
                match = mine == clusters[:, across]
                if own and i == j:
                    match = match & (iota((tall, 128), 0) != iota((tall, 128), 1) + t)
                score = jnp.where(match, product[:, t : t + 128], APART)
                soft = jnp.exp2((score - 1.0) * (sharpness * LOG2E))
                col_best[c, :, across] = jnp.maximum(
                    col_best[c, :, across], column_fold(score, jnp.maximum)
                )
                col_mass[c, :, across] = col_mass[c, :, across] + column_fold(soft, jnp.add)
                tops = score if tops is None else jnp.maximum(tops, score)
                sums = soft if sums is None else sums + soft
            if r is not None:
                row_best[r, down, :] = jnp.maximum(row_best[r, down, :], tops)
                row_mass[r, down, :] = row_mass[r, down, :] + sums


def settle(e, state):
    col_best, col_mass, row_best, row_mass = state[:4]
    best = jnp.max(col_best[e], axis=0, keepdims=True)
    mass = jnp.sum(col_mass[e], axis=0, keepdims=True)
    if e in ROW_BLOCKS:
        r = ROW_BLOCKS.index(e)
        tops, sums = [], []
        for t in range(0, BLOCK, 128):
            tops.append(jnp.max(row_best[r, t : t + 128, :].T, axis=0, keepdims=True))
            sums.append(jnp.sum(row_mass[r, t : t + 128, :].T, axis=0, keepdims=True))
        best = jnp.maximum(best, jnp.concatenate(tops, axis=1))
        mass = mass + jnp.concatenate(sums, axis=1)
    return best, mass


def store(blocks, best_out, mass_out, state):
    best_out[...] = jnp.full_like(best_out, APART)
    mass_out[...] = jnp.zeros_like(mass_out)
    for e in blocks:
        best_out[e : e + 1, :], mass_out[e : e + 1, :] = settle(e, state)


def early_kernel(b0, b1, b2, b3, best_out, mass_out, *state):
    clear(state)
    for place, block in enumerate((b0, b1, b2, b3)):
        spell(block, place, state)
    square(b0, b0, 0, 0, None, state, True)
    square(b2, b0, 2, 0, 1, state)
    square(b1, b0, 1, 0, 0, state)
    square(b1, b2, 1, 2, 0, state)
    square(b1, b3, 1, 3, 0, state)
    square(b3, b2, 3, 2, None, state)
    store((0, 1, 2, 3), best_out, mass_out, state)


def late_kernel(b0, b1, b2, b3, b4, b5, best_in, mass_in, out, *state):
    clear(state)
    for place, block in enumerate((b4, b1, b2)):
        spell(block, place, state)
    square(b1, b5, 1, 5, 0, state)
    square(b4, b0, 0, 0, None, state)
    square(b4, b5, 0, 5, None, state)
    square(b2, b4, 2, 4, 1, state)
    source_at = (iota((DEVICES, BLOCK), 0) + 1).astype(jnp.float32)
    line = iota((16, BLOCK), 0)
    back = []
    for e, block in enumerate((b0, b1, b2, b3, b4, b5)):
        here = slice(e, e + 1)
        best, mass = jnp.maximum(best_in[here, :], -1.0), mass_in[here, :]
        if e != 3:
            more, extra = settle(e, state)
            best = jnp.maximum(best, more)
            mass = mass + extra
        names = names_of(block)
        values = jnp.where((line & 1) == 0, best, mass)
        values = jnp.where((line >> 1).astype(jnp.float32) == names[2:3], values, 0.0)
        to = (source_at == names[1:2]).astype(jnp.bfloat16)
        back.append(joined(matmul(split(values), to, NT)))
    back.append(jnp.zeros((128 - 16 * len(back), DEVICES), jnp.float32))
    out[...] = jnp.concatenate(back, axis=0).T


def finish_kernel(arrived, places, best_out, mass_out):
    shape = (DEVICES, DEVICES)
    at, col = iota(shape, 0), iota(shape, 1)
    base, ay, az = at >> 4, (at >> 2) & 3, at & 3
    turned = (base & 1) == 1
    best = mass = None
    pieces = split(arrived[...].T)
    for e, (dy, dz) in enumerate(SPOTS):
        by = (ay + jnp.where(turned, dz, (-dy) & 3)) & 3
        bz = (az + jnp.where(turned, dy, (-dz) & 3)) & 3
        move = (col == base * MEMBERS + by * 4 + bz).astype(jnp.bfloat16)
        part = jnp.concatenate(
            [pieces[128 * p + 16 * e : 128 * p + 16 * e + 16] for p in range(3)], axis=0
        )
        moved = joined(matmul(part, move, NT))
        best = moved if best is None else jnp.maximum(best, moved)
        mass = moved if mass is None else mass + moved
    merged = jnp.where((iota((16, DEVICES), 0) & 1) == 0, best, mass)
    holder = (iota((DEVICES, ROWS), 0) == places[0:1, :]).astype(jnp.bfloat16)
    picked = joined(matmul(split(merged), holder, NN))
    line = iota((16, ROWS), 0)
    turn = places[1:2, :]
    best_out[...] = jnp.sum(jnp.where(line == 2 * turn, picked, 0.0), axis=0, keepdims=True)
    mass = jnp.sum(jnp.where(line == 2 * turn + 1, picked, 0.0), axis=0, keepdims=True)
    mass_out[...] = jnp.log1p(mass)


def call(kernel, out_shape, scratch=(), flops=0, name=None):
    return pl.pallas_call(
        kernel,
        out_shape=out_shape,
        scratch_shapes=scratch,
        compiler_params=pltpu.CompilerParams(vmem_limit_bytes=VMEM_LIMIT),
        cost_estimate=pl.CostEstimate(flops=flops, bytes_accessed=8_000_000, transcendentals=0),
        name=name,
    )


def hop(dy, dz):
    pairs = []
    for g in range(GROUPS):
        up, along = (-dz, -dy) if g & 1 else (dy, dz)
        for y in range(4):
            for z in range(4):
                source = ((y + up) % 4) * 4 + (z + along) % 4
                pairs.append((g * MEMBERS + source, g * MEMBERS + y * 4 + z))
    return pairs


def from_spot(x, dy, dz):
    return lax.ppermute(x, AXES, hop(dy, dz))


def fast(embeddings, labels, cluster_slot):
    f32, bf16, i32 = jnp.float32, jnp.bfloat16, jnp.int32
    shape = jax.ShapeDtypeStruct
    spread, places = call(
        prelude_kernel,
        (shape((HELD, WIDE), bf16), shape((8, ROWS), i32)),
        flops=3_000_000_000,
        name="prelude",
    )(labels.reshape(1, ROWS), cluster_slot.reshape(1, ROWS), embeddings)
    arrived = lax.all_to_all(spread, AXES, split_axis=0, concat_axis=0, tiled=True)
    b0, over = call(
        pack_kernel,
        (shape((BLOCK, FEAT), bf16), shape((8, 128), i32)),
        flops=3_000_000_000,
        name="pack",
    )(arrived)
    b2 = from_spot(b0, 0, 1)
    b3 = from_spot(b0, 0, 3)
    b1 = from_spot(b0, 1, 0)
    b4 = from_spot(b1, 1, 0)
    b5 = from_spot(b2, 0, 1)

    def state(places):
        return (
            pltpu.VMEM((6, 8, BLOCK), f32),
            pltpu.VMEM((6, 8, BLOCK), f32),
            pltpu.VMEM((2, BLOCK, 128), f32),
            pltpu.VMEM((2, BLOCK, 128), f32),
            pltpu.VMEM((places, BLOCK, 128), f32),
        )

    best, mass = call(
        early_kernel,
        (shape((8, BLOCK), f32), shape((8, BLOCK), f32)),
        scratch=state(4),
        flops=6_000_000_000,
        name="early",
    )(b0, b1, b2, b3)
    message = call(
        late_kernel,
        shape((DEVICES, 128), f32),
        scratch=state(3),
        flops=4_000_000_000,
        name="late",
    )(b0, b1, b2, b3, b4, b5, best, mass)
    answer = lax.all_to_all(message, AXES, split_axis=0, concat_axis=0, tiled=True)
    best, mass = call(
        finish_kernel,
        (shape((1, ROWS), f32), shape((1, ROWS), f32)),
        flops=ROWS * ROWS * 128,
        name="finish",
    )(answer, places)
    return (best.reshape(ROWS), mass.reshape(ROWS)), jnp.max(over)


def general(embeddings, labels, cluster_slot):
    groups = lax.axis_size("grp")
    members = lax.axis_size("blk")
    row_count, feature_count = embeddings.shape
    capacity = row_count // 4
    held = groups * capacity
    widened = embeddings.astype(jnp.float32)
    units = (
        widened * lax.rsqrt(jnp.sum(widened * widened, axis=1, keepdims=True) + epsilon)
    ).astype(jnp.bfloat16)
    slot_ids = cluster_slot[labels]
    owner_group = slot_ids // (cluster_slot.shape[0] // groups)
    owner_onehot = (owner_group[:, None] == jnp.arange(groups, dtype=jnp.int32)[None, :]).astype(
        jnp.int32
    )
    earlier = jnp.cumsum(owner_onehot, axis=0) - owner_onehot
    send_place = owner_group * capacity + jnp.sum(earlier * owner_onehot, axis=1)
    outgoing = jnp.zeros((held, feature_count), jnp.bfloat16).at[send_place].set(units)
    outgoing_slots = jnp.full((held,), -1, jnp.int32).at[send_place].set(slot_ids)
    rows = lax.all_to_all(outgoing, "grp", split_axis=0, concat_axis=0, tiled=True)
    slots = lax.all_to_all(outgoing_slots, "grp", split_axis=0, concat_axis=0, tiled=True)
    ring = [(i, (i + 1) % members) for i in range(members)]
    local = jnp.arange(held, dtype=jnp.int32)
    place = lax.axis_index("blk")
    own_ids = place * held + local

    def step(turn, carry):
        key_rows, key_slots, best, mass = carry
        scores = jnp.einsum("qd,kd->qk", rows, key_rows, preferred_element_type=jnp.float32)
        matched = (slots[:, None] == key_slots[None, :]) & (key_slots[None, :] >= 0)
        owner = (place - turn) & (members - 1)
        matched = matched & (own_ids[:, None] != (owner * held + local)[None, :])
        best = jnp.maximum(best, jnp.max(jnp.where(matched, scores, -1.0), axis=1))
        mass = mass + jnp.sum(
            jnp.where(matched, jnp.exp(sharpness * (scores - 1.0)), 0.0), axis=1
        )
        key_rows = lax.ppermute(key_rows, "blk", ring)
        key_slots = lax.ppermute(key_slots, "blk", ring)
        return key_rows, key_slots, best, mass

    start = (
        rows,
        slots,
        jnp.full((held,), -1.0, jnp.float32),
        jnp.zeros((held,), jnp.float32),
    )
    _, _, best, mass = lax.fori_loop(0, members, step, start)
    best = lax.all_to_all(best, "grp", split_axis=0, concat_axis=0, tiled=True)
    mass = lax.all_to_all(mass, "grp", split_axis=0, concat_axis=0, tiled=True)
    return (best[send_place], jnp.log1p(mass[send_place]))


def body(embeddings, labels, cluster_slot):
    result, over = fast(embeddings, labels, cluster_slot)
    return lax.cond(
        over > 0, lambda: general(embeddings, labels, cluster_slot), lambda: result
    )


def solution(mesh):
    placed = (P(AXES, None), P(AXES), P())
    return jax.shard_map(
        body,
        mesh=mesh,
        in_specs=placed,
        out_specs=(P(AXES), P(AXES)),
        check_vma=False,
    )
```

```python
import jax
import jax.numpy as jnp
from jax import lax
from jax.experimental import pallas as pl
from jax.experimental.pallas import tpu as pltpu
from jax.sharding import PartitionSpec as P

epsilon = 1e-06
sharpness = 8.0

ROWS = 512
FEAT = 768
WIDE = 896
GROUPS = 8
MEMBERS = 16
DEVICES = GROUPS * MEMBERS
SHARE = 8
HELD = DEVICES * SHARE
BLOCK = 640
ROOM = BLOCK - 16
APART = -64.0
LOG2E = 1.4426950408889634
AXES = ("grp", "blk")
VMEM_LIMIT = 24 * 1024 * 1024

SPOTS = ((0, 0), (1, 0), (0, 1), (2, 0), (0, 2), (0, 3), (3, 0))
LOW = 256
LOW_SENT = LOW + 16
HIGH_SENT = BLOCK - LOW
ROW_BLOCKS = (1, 2)
SHIFT = 2.0


def iota(shape, axis):
    return lax.broadcasted_iota(jnp.int32, shape, axis)


def matmul(a, b, dims, exact=False):
    return lax.dot_general(
        a,
        b,
        (dims, ((), ())),
        precision=lax.Precision.HIGHEST if exact else None,
        preferred_element_type=jnp.float32,
    )


NN = ((1,), (0,))
NT = ((1,), (1,))


def split(x):
    high = x.astype(jnp.bfloat16)
    rest = x - high.astype(jnp.float32)
    middle = rest.astype(jnp.bfloat16)
    low = (rest - middle.astype(jnp.float32)).astype(jnp.bfloat16)
    return jnp.concatenate([high, middle, low], axis=0)


def joined(x):
    size = x.shape[0] // 3
    return x[:size] + x[size : 2 * size] + x[2 * size :]


def prelude_kernel(labels, slots, rows, spread, places):
    lab = labels[...]
    table = slots[...]
    by_cluster = (iota((ROWS, ROWS), 0) == lab).astype(jnp.bfloat16)
    sub = iota((8, ROWS), 0)
    parts = jnp.where(sub == 0, table >> 6, jnp.where(sub == 1, table & 63, 0)).astype(jnp.bfloat16)
    found = matmul(parts, by_cluster, NN)
    group = found[0:1].astype(jnp.int32)
    in_group = sub == group
    before = (iota((ROWS, ROWS), 0) < iota((ROWS, ROWS), 1)).astype(jnp.bfloat16)
    counts = matmul(in_group.astype(jnp.bfloat16), before, NN)
    rank = jnp.sum(jnp.where(in_group, counts, 0.0), axis=0, keepdims=True).astype(jnp.int32)
    holder = group * MEMBERS + ((rank + lax.axis_index("blk")) & (MEMBERS - 1))
    turn = rank >> 4
    places[...] = jnp.where(sub == 0, holder, turn)

    wide = rows[...].astype(jnp.float32)
    norm = lax.rsqrt(jnp.sum(wide * wide, axis=1, keepdims=True) + epsilon)
    units = (wide * norm).astype(jnp.bfloat16)
    lanes = iota((128, ROWS), 0)
    marks = jnp.where(lanes == 0, found[1:2] + 1.0, 0.0).astype(jnp.bfloat16)
    goal = holder * SHARE + turn
    totals = matmul(
        jnp.ones((128, ROWS), jnp.bfloat16), (lanes - 64 == group).astype(jnp.bfloat16), NT
    )
    totals = jnp.where((iota((ROWS, 128), 0) & (SHARE - 1)) == 0, totals[0:1], 0.0)
    for t in range(0, HELD, ROWS):
        here = pl.ds(t, ROWS)
        pick = (iota((ROWS, ROWS), 0) + t == goal).astype(jnp.bfloat16)
        spread[here, :FEAT] = matmul(pick, units, NN).astype(jnp.bfloat16)
        spread[here, FEAT:] = (matmul(pick, marks, NT) + totals).astype(jnp.bfloat16)


def pack_kernel(arrived, packed, low, high, over):
    tails = arrived[:, FEAT:]
    one = ((iota((128, HELD), 0) * SHARE) == iota((128, HELD), 1)).astype(jnp.bfloat16)
    counts = matmul(one, tails, NN).astype(jnp.int32)
    counts = jnp.where(iota((128, 128), 1) >= 64, counts, 0)
    turned = iota((128, 128), 0) & (MEMBERS - 1)
    most = jnp.zeros((1, 128), jnp.int32)
    for k in range(MEMBERS):
        gets = (counts + (MEMBERS - 1) - ((k - turned) & (MEMBERS - 1))) >> 4
        most = jnp.maximum(most, jnp.sum(gets, axis=0, keepdims=True))
    over[...] = jnp.broadcast_to((most > ROOM).astype(jnp.int32), (8, 128))

    at, line = iota((8, HELD), 1), iota((8, HELD), 0)
    clusters = matmul((iota((8, 128), 1) == 0).astype(jnp.bfloat16), tails, NT)
    held = clusters > 0.0
    before = (iota((HELD, HELD), 0) < iota((HELD, HELD), 1)).astype(jnp.bfloat16)
    position = matmul(held.astype(jnp.bfloat16), before, NN)
    position = jnp.where(held, position, -1.0)[0:1].astype(jnp.int32)
    names = jnp.where(line == 1, (at >> 3) + 1, jnp.where(line == 2, at & 7, 0))
    names = jnp.where(line == 0, clusters, names.astype(jnp.float32)).astype(jnp.bfloat16)
    pick = (iota((BLOCK, HELD), 0) == position).astype(jnp.bfloat16)
    packed[:ROOM, :] = matmul(pick[:ROOM], arrived[:, :FEAT], NN).astype(jnp.bfloat16)
    named = matmul(names, pick, NT)
    named = jnp.concatenate([named, jnp.zeros((8, FEAT - BLOCK), jnp.float32)], axis=1)
    named = jnp.concatenate([named, jnp.zeros_like(named)], axis=0).astype(jnp.bfloat16)
    packed[ROOM:, :] = named
    low[:LOW, :] = packed[:LOW, :]
    low[LOW:, :] = named
    high[...] = packed[LOW:, :]


def column_fold(x, op):
    while x.shape[0] > 8:
        half = x.shape[0] // 2
        x = op(x[:half], x[half:])
    return x


def row_fold(x, op):
    total = x[:, :128]
    for t in range(1, x.shape[1] // 128):
        total = op(total, x[:, 128 * t : 128 * (t + 1)])
    return total


LOWS = ((0, 256),)
HIGHS = ((256, 256), (512, 128))
PARTS = LOWS + HIGHS


def clear(state):
    col_best, col_mass, row_best, row_mass = state[:4]
    for ref in (col_best, row_best):
        ref[...] = jnp.full_like(ref, APART)
    for ref in (col_mass, row_mass):
        ref[...] = jnp.zeros_like(ref)


def names_of(block):
    return block[block.shape[0] - 16 :, :BLOCK].astype(jnp.float32)


def spell(block, place, state):
    clusters = names_of(block)[0:1]
    clusters = jnp.where(clusters > 0.0, clusters, -1.0)
    for t in range(0, BLOCK, 128):
        here = slice(t, t + 128)
        state[4][place, here, :] = jnp.broadcast_to(clusters[:, here], (128, 128)).T


def square(rows, cols, place, c, r, state, own=False, downs=PARTS, parts=PARTS, first=0):
    col_best, col_mass, row_best, row_mass, spelt = state
    clusters = names_of(cols)[0:1]
    for i, tall in downs:
        for j, wide in parts:
            product = matmul(rows[i : i + tall, :], cols[j - first : j - first + wide, :], NT)
            down = slice(i, i + tall)
            mine = spelt[place, down, :]
            tops = sums = None
            for t in range(0, wide, 128):
                across = slice(j + t, j + t + 128)
                match = mine == clusters[:, across]
                if own and i == j:
                    match = match & (iota((tall, 128), 0) != iota((tall, 128), 1) + t)
                score = jnp.where(match, product[:, t : t + 128], APART)
                soft = jnp.exp2((score - 1.0) * (sharpness * LOG2E))
                col_best[c, :, across] = jnp.maximum(
                    col_best[c, :, across], column_fold(score, jnp.maximum)
                )
                col_mass[c, :, across] = col_mass[c, :, across] + column_fold(soft, jnp.add)
                tops = score if tops is None else jnp.maximum(tops, score)
                sums = soft if sums is None else sums + soft
            if r is not None:
                row_best[r, down, :] = jnp.maximum(row_best[r, down, :], tops)
                row_mass[r, down, :] = row_mass[r, down, :] + sums


def settle(e, state):
    col_best, col_mass, row_best, row_mass = state[:4]
    best = jnp.max(col_best[e], axis=0, keepdims=True)
    mass = jnp.sum(col_mass[e], axis=0, keepdims=True)
    if e in ROW_BLOCKS:
        r = ROW_BLOCKS.index(e)
        tops, sums = [], []
        for t in range(0, BLOCK, 128):
            tops.append(jnp.max(row_best[r, t : t + 128, :].T, axis=0, keepdims=True))
            sums.append(jnp.sum(row_mass[r, t : t + 128, :].T, axis=0, keepdims=True))
        best = jnp.maximum(best, jnp.concatenate(tops, axis=1))
        mass = mass + jnp.concatenate(sums, axis=1)
    return best, mass


def store(blocks, best_out, mass_out, state):
    best_out[...] = jnp.full_like(best_out, APART)
    mass_out[...] = jnp.zeros_like(mass_out)
    for e in blocks:
        best_out[e : e + 1, :], mass_out[e : e + 1, :] = settle(e, state)


def early_kernel(b0, b1, b2, low, high, best_out, mass_out, *state):
    clear(state)
    for place, block in enumerate((b0, b1, b2)):
        spell(block, place, state)
    square(b0, b0, 0, 0, None, state, True)
    square(b1, b0, 1, 0, 0, state)
    square(b1, b2, 1, 2, 0, state)
    square(b1, low, 1, 5, 0, state, parts=LOWS)
    square(b2, b0, 2, 0, 1, state)
    square(b2, high, 2, 6, 1, state, parts=HIGHS, first=LOW)
    square(b1, high, 1, 6, 0, state, downs=LOWS, parts=HIGHS, first=LOW)
    square(b1, high, 1, 6, None, state, downs=HIGHS, parts=HIGHS, first=LOW)
    square(b2, low, 2, 5, 1, state, downs=HIGHS, parts=LOWS)
    square(b2, low, 2, 5, None, state, downs=LOWS, parts=LOWS)
    store((0, 1, 2, 5, 6), best_out, mass_out, state)


def late_kernel(b0, b1, b2, b3, b4, low, high, best_in, mass_in, out, *state):
    clear(state)
    for place, block in enumerate((b0, b1, b2, b4)):
        spell(block, place, state)
    square(b0, b3, 0, 3, None, state, downs=LOWS, parts=LOWS)
    square(b0, b4, 0, 4, None, state, downs=HIGHS, parts=HIGHS)
    square(b1, b4, 1, 4, 0, state)
    square(b2, b3, 2, 3, 1, state)
    square(b4, b3, 3, 3, None, state)
    source_at = (iota((DEVICES, BLOCK), 0) + 1).astype(jnp.float32)
    line = iota((16, BLOCK), 0)
    back = []
    for e, block in enumerate((b0, b1, b2, b3, b4, low, high)):
        here = slice(e, e + 1)
        best, mass = jnp.maximum(best_in[here, :], -1.0), mass_in[here, :]
        if e in (1, 2, 3, 4):
            more, extra = settle(e, state)
            best = jnp.maximum(best, more)
            mass = mass + extra
        best = best + SHIFT
        names = names_of(block)
        if e == 5:
            names = jnp.where(iota(names.shape, 1) < LOW, names, 0.0)
        if e == 6:
            names = jnp.where(iota(names.shape, 1) >= LOW, names, 0.0)
        values = jnp.where((line & 1) == 0, best, mass)
        values = jnp.where((line >> 1).astype(jnp.float32) == names[2:3], values, 0.0)
        to = (source_at == names[1:2]).astype(jnp.bfloat16)
        back.append(joined(matmul(split(values), to, NT)))
    back.append(jnp.zeros((128 - 16 * len(back), DEVICES), jnp.float32))
    out[...] = jnp.concatenate(back, axis=0).T


def finish_kernel(arrived, places, best_out, mass_out):
    shape = (DEVICES, DEVICES)
    at, col = iota(shape, 0), iota(shape, 1)
    base, ay, az = at >> 4, (at >> 2) & 3, at & 3
    turned = (base & 1) == 1
    best = mass = None
    pieces = split(arrived[...].T)
    for e, (dy, dz) in enumerate(SPOTS):
        by = (ay + jnp.where(turned, dz, (-dy) & 3)) & 3
        bz = (az + jnp.where(turned, dy, (-dz) & 3)) & 3
        move = (col == base * MEMBERS + by * 4 + bz).astype(jnp.bfloat16)
        part = jnp.concatenate(
            [pieces[128 * p + 16 * e : 128 * p + 16 * e + 16] for p in range(3)], axis=0
        )
        moved = joined(matmul(part, move, NT))
        best = moved if best is None else jnp.maximum(best, moved)
        mass = moved if mass is None else mass + moved
    merged = jnp.where((iota((16, DEVICES), 0) & 1) == 0, best, mass)
    holder = (iota((DEVICES, ROWS), 0) == places[0:1, :]).astype(jnp.bfloat16)
    picked = joined(matmul(split(merged), holder, NN))
    line = iota((16, ROWS), 0)
    turn = places[1:2, :]
    best = jnp.sum(jnp.where(line == 2 * turn, picked, 0.0), axis=0, keepdims=True)
    best_out[...] = best - SHIFT
    mass = jnp.sum(jnp.where(line == 2 * turn + 1, picked, 0.0), axis=0, keepdims=True)
    mass_out[...] = jnp.log1p(mass)


def call(kernel, out_shape, scratch=(), flops=0, name=None):
    return pl.pallas_call(
        kernel,
        out_shape=out_shape,
        scratch_shapes=scratch,
        compiler_params=pltpu.CompilerParams(vmem_limit_bytes=VMEM_LIMIT),
        cost_estimate=pl.CostEstimate(flops=flops, bytes_accessed=8_000_000, transcendentals=0),
        name=name,
    )


def hop(dy, dz):
    pairs = []
    for g in range(GROUPS):
        up, along = (-dz, -dy) if g & 1 else (dy, dz)
        for y in range(4):
            for z in range(4):
                source = ((y + up) % 4) * 4 + (z + along) % 4
                pairs.append((g * MEMBERS + source, g * MEMBERS + y * 4 + z))
    return pairs


def from_spot(x, dy, dz):
    return lax.ppermute(x, AXES, hop(dy, dz))


def fast(embeddings, labels, cluster_slot):
    f32, bf16, i32 = jnp.float32, jnp.bfloat16, jnp.int32
    shape = jax.ShapeDtypeStruct
    spread, places = call(
        prelude_kernel,
        (shape((HELD, WIDE), bf16), shape((8, ROWS), i32)),
        flops=3_000_000_000,
        name="prelude",
    )(labels.reshape(1, ROWS), cluster_slot.reshape(1, ROWS), embeddings)
    arrived = lax.all_to_all(spread, AXES, split_axis=0, concat_axis=0, tiled=True)
    b0, low, high, over = call(
        pack_kernel,
        (
            shape((BLOCK, FEAT), bf16),
            shape((LOW_SENT, FEAT), bf16),
            shape((HIGH_SENT, FEAT), bf16),
            shape((8, 128), i32),
        ),
        flops=3_000_000_000,
        name="pack",
    )(arrived)
    b1 = from_spot(b0, 1, 0)
    b2 = from_spot(b0, 0, 1)
    low = from_spot(low, 0, 3)
    high = from_spot(high, 3, 0)
    b1, b2, low, high = lax.optimization_barrier((b1, b2, low, high))
    b3 = from_spot(b1, 1, 0)
    b4 = from_spot(b2, 0, 1)

    def state(places):
        return (
            pltpu.VMEM((7, 8, BLOCK), f32),
            pltpu.VMEM((7, 8, BLOCK), f32),
            pltpu.VMEM((2, BLOCK, 128), f32),
            pltpu.VMEM((2, BLOCK, 128), f32),
            pltpu.VMEM((places, BLOCK, 128), f32),
        )

    best, mass = call(
        early_kernel,
        (shape((8, BLOCK), f32), shape((8, BLOCK), f32)),
        scratch=state(3),
        flops=6_000_000_000,
        name="early",
    )(b0, b1, b2, low, high)
    message = call(
        late_kernel,
        shape((DEVICES, 128), f32),
        scratch=state(4),
        flops=4_000_000_000,
        name="late",
    )(b0, b1, b2, b3, b4, low, high, best, mass)
    answer = lax.all_to_all(message, AXES, split_axis=0, concat_axis=0, tiled=True)
    best, mass = call(
        finish_kernel,
        (shape((1, ROWS), f32), shape((1, ROWS), f32)),
        flops=ROWS * ROWS * 128,
        name="finish",
    )(answer, places)
    return (best.reshape(ROWS), mass.reshape(ROWS)), jnp.max(over)


def general(embeddings, labels, cluster_slot):
    groups = lax.axis_size("grp")
    members = lax.axis_size("blk")
    row_count, feature_count = embeddings.shape
    capacity = row_count // 4
    held = groups * capacity
    widened = embeddings.astype(jnp.float32)
    units = (
        widened * lax.rsqrt(jnp.sum(widened * widened, axis=1, keepdims=True) + epsilon)
    ).astype(jnp.bfloat16)
    slot_ids = cluster_slot[labels]
    owner_group = slot_ids // (cluster_slot.shape[0] // groups)
    owner_onehot = (owner_group[:, None] == jnp.arange(groups, dtype=jnp.int32)[None, :]).astype(
        jnp.int32
    )
    earlier = jnp.cumsum(owner_onehot, axis=0) - owner_onehot
    send_place = owner_group * capacity + jnp.sum(earlier * owner_onehot, axis=1)
    outgoing = jnp.zeros((held, feature_count), jnp.bfloat16).at[send_place].set(units)
    outgoing_slots = jnp.full((held,), -1, jnp.int32).at[send_place].set(slot_ids)
    rows = lax.all_to_all(outgoing, "grp", split_axis=0, concat_axis=0, tiled=True)
    slots = lax.all_to_all(outgoing_slots, "grp", split_axis=0, concat_axis=0, tiled=True)
    ring = [(i, (i + 1) % members) for i in range(members)]
    local = jnp.arange(held, dtype=jnp.int32)
    place = lax.axis_index("blk")
    own_ids = place * held + local

    def step(turn, carry):
        key_rows, key_slots, best, mass = carry
        scores = jnp.einsum("qd,kd->qk", rows, key_rows, preferred_element_type=jnp.float32)
        matched = (slots[:, None] == key_slots[None, :]) & (key_slots[None, :] >= 0)
        owner = (place - turn) & (members - 1)
        matched = matched & (own_ids[:, None] != (owner * held + local)[None, :])
        best = jnp.maximum(best, jnp.max(jnp.where(matched, scores, -1.0), axis=1))
        mass = mass + jnp.sum(
            jnp.where(matched, jnp.exp(sharpness * (scores - 1.0)), 0.0), axis=1
        )
        key_rows = lax.ppermute(key_rows, "blk", ring)
        key_slots = lax.ppermute(key_slots, "blk", ring)
        return key_rows, key_slots, best, mass

    start = (
        rows,
        slots,
        jnp.full((held,), -1.0, jnp.float32),
        jnp.zeros((held,), jnp.float32),
    )
    _, _, best, mass = lax.fori_loop(0, members, step, start)
    best = lax.all_to_all(best, "grp", split_axis=0, concat_axis=0, tiled=True)
    mass = lax.all_to_all(mass, "grp", split_axis=0, concat_axis=0, tiled=True)
    return (best[send_place], jnp.log1p(mass[send_place]))


def body(embeddings, labels, cluster_slot):
    result, over = fast(embeddings, labels, cluster_slot)
    return lax.cond(
        over > 0, lambda: general(embeddings, labels, cluster_slot), lambda: result
    )


def solution(mesh):
    placed = (P(AXES, None), P(AXES), P())
    return jax.shard_map(
        body,
        mesh=mesh,
        in_specs=placed,
        out_specs=(P(AXES), P(AXES)),
        check_vma=False,
    )
```

```python
import jax
import jax.numpy as jnp
from jax import lax
from jax.experimental import pallas as pl
from jax.experimental.pallas import tpu as pltpu
from jax.sharding import PartitionSpec as P

epsilon = 1e-06
sharpness = 8.0

ROWS = 512
FEAT = 768
WIDE = 896
GROUPS = 8
MEMBERS = 16
DEVICES = GROUPS * MEMBERS
SHARE = 8
HELD = DEVICES * SHARE
SENT = 608
ROOM = SENT - 16
BLOCK = 640
APART = -64.0
LOG2E = 1.4426950408889634
AXES = ("grp", "blk")
VMEM_LIMIT = 24 * 1024 * 1024

SPOTS = ((0, 0), (1, 0), (0, 1), (2, 0), (0, 2), (0, 3), (3, 0))
LOW = 256
LOW_SENT = LOW + 16
HIGH_SENT = SENT - LOW
ROW_BLOCKS = (1, 2)
SHIFT = 2.0


def iota(shape, axis):
    return lax.broadcasted_iota(jnp.int32, shape, axis)


def matmul(a, b, dims, exact=False):
    return lax.dot_general(
        a,
        b,
        (dims, ((), ())),
        precision=lax.Precision.HIGHEST if exact else None,
        preferred_element_type=jnp.float32,
    )


NN = ((1,), (0,))
NT = ((1,), (1,))


def split(x):
    high = x.astype(jnp.bfloat16)
    rest = x - high.astype(jnp.float32)
    middle = rest.astype(jnp.bfloat16)
    low = (rest - middle.astype(jnp.float32)).astype(jnp.bfloat16)
    return jnp.concatenate([high, middle, low], axis=0)


def joined(x):
    size = x.shape[0] // 3
    return x[:size] + x[size : 2 * size] + x[2 * size :]


def prelude_kernel(labels, slots, rows, spread, places):
    lab = labels[...]
    table = slots[...]
    by_cluster = (iota((ROWS, ROWS), 0) == lab).astype(jnp.bfloat16)
    sub = iota((8, ROWS), 0)
    parts = jnp.where(sub == 0, table >> 6, jnp.where(sub == 1, table & 63, 0)).astype(jnp.bfloat16)
    found = matmul(parts, by_cluster, NN)
    group = found[0:1].astype(jnp.int32)
    in_group = sub == group
    before = (iota((ROWS, ROWS), 0) < iota((ROWS, ROWS), 1)).astype(jnp.bfloat16)
    counts = matmul(in_group.astype(jnp.bfloat16), before, NN)
    rank = jnp.sum(jnp.where(in_group, counts, 0.0), axis=0, keepdims=True).astype(jnp.int32)
    holder = group * MEMBERS + ((rank + lax.axis_index("blk")) & (MEMBERS - 1))
    turn = rank >> 4
    places[...] = jnp.where(sub == 0, holder, turn)

    wide = rows[...].astype(jnp.float32)
    norm = lax.rsqrt(jnp.sum(wide * wide, axis=1, keepdims=True) + epsilon)
    units = (wide * norm).astype(jnp.bfloat16)
    lanes = iota((128, ROWS), 0)
    marks = jnp.where(lanes == 0, found[1:2] + 1.0, 0.0).astype(jnp.bfloat16)
    goal = holder * SHARE + turn
    totals = matmul(
        jnp.ones((128, ROWS), jnp.bfloat16), (lanes - 64 == group).astype(jnp.bfloat16), NT
    )
    totals = jnp.where((iota((ROWS, 128), 0) & (SHARE - 1)) == 0, totals[0:1], 0.0)
    for t in range(0, HELD, ROWS):
        here = pl.ds(t, ROWS)
        pick = (iota((ROWS, ROWS), 0) + t == goal).astype(jnp.bfloat16)
        spread[here, :FEAT] = matmul(pick, units, NN).astype(jnp.bfloat16)
        spread[here, FEAT:] = (matmul(pick, marks, NT) + totals).astype(jnp.bfloat16)


def pack_kernel(arrived, low, high, over):
    tails = arrived[:, FEAT:]
    one = ((iota((128, HELD), 0) * SHARE) == iota((128, HELD), 1)).astype(jnp.bfloat16)
    counts = matmul(one, tails, NN).astype(jnp.int32)
    counts = jnp.where(iota((128, 128), 1) >= 64, counts, 0)
    turned = iota((128, 128), 0) & (MEMBERS - 1)
    most = jnp.zeros((1, 128), jnp.int32)
    for k in range(MEMBERS):
        gets = (counts + (MEMBERS - 1) - ((k - turned) & (MEMBERS - 1))) >> 4
        most = jnp.maximum(most, jnp.sum(gets, axis=0, keepdims=True))
    over[...] = jnp.broadcast_to((most > ROOM).astype(jnp.int32), (8, 128))

    at, line = iota((8, HELD), 1), iota((8, HELD), 0)
    clusters = matmul((iota((8, 128), 1) == 0).astype(jnp.bfloat16), tails, NT)
    held = clusters > 0.0
    before = (iota((HELD, HELD), 0) < iota((HELD, HELD), 1)).astype(jnp.bfloat16)
    position = matmul(held.astype(jnp.bfloat16), before, NN)
    position = jnp.where(held, position, -1.0)[0:1].astype(jnp.int32)
    names = jnp.where(line == 1, (at >> 3) + 1, jnp.where(line == 2, at & 7, 0))
    names = jnp.where(line == 0, clusters, names.astype(jnp.float32)).astype(jnp.bfloat16)
    pick = (iota((BLOCK, HELD), 0) == position).astype(jnp.bfloat16)
    rows = matmul(pick[:ROOM], arrived[:, :FEAT], NN).astype(jnp.bfloat16)
    named = matmul(names, pick, NT)
    named = jnp.concatenate([named, jnp.zeros((8, FEAT - BLOCK), jnp.float32)], axis=1)
    named = jnp.concatenate([named, jnp.zeros_like(named)], axis=0).astype(jnp.bfloat16)
    low[:LOW, :] = rows[:LOW]
    low[LOW:, :] = named
    high[: ROOM - LOW, :] = rows[LOW:]
    high[ROOM - LOW :, :] = named


def column_fold(x, op):
    while x.shape[0] > 8:
        half = x.shape[0] // 16 * 8
        rest = x[2 * half :]
        x = op(x[:half], x[half : 2 * half])
        if rest.shape[0]:
            x = jnp.concatenate([op(x[:8], rest), x[8:]], axis=0) if half > 8 else op(x, rest)
    return x


LOWS = ((0, 256),)
HIGHS = ((256, 256), (512, SENT - 512))
PARTS = LOWS + HIGHS


def clear(state):
    col_best, col_mass, row_best, row_mass = state[:4]
    for ref in (col_best, row_best):
        ref[...] = jnp.full_like(ref, APART)
    for ref in (col_mass, row_mass):
        ref[...] = jnp.zeros_like(ref)


def names_of(block):
    part = block[0] if block[1] is None else block[1]
    return part[part.shape[0] - 16 :, :BLOCK].astype(jnp.float32)


def spell(block, place, state):
    clusters = names_of(block)[0:1]
    clusters = jnp.where(clusters > 0.0, clusters, -1.0)
    for t in range(0, BLOCK, 128):
        here = slice(t, t + 128)
        state[4][place, here, :] = jnp.broadcast_to(clusters[:, here], (128, 128)).T


def part_of(block, first, size):
    if first < LOW:
        return block[0][first : first + size, :]
    return block[1][first - LOW : first - LOW + size, :]


def square(rows, cols, place, c, r, state, own=False, downs=PARTS, parts=PARTS):
    col_best, col_mass, row_best, row_mass, spelt = state
    clusters = names_of(cols)[0:1]
    for i, tall in downs:
        for j, wide in parts:
            product = matmul(part_of(rows, i, tall), part_of(cols, j, wide), NT)
            down = slice(i, i + tall)
            tops = sums = None
            for t in range(0, wide, 128):
                size = min(128, wide - t)
                across = slice(j + t, j + t + size)
                match = spelt[place, down, :size] == clusters[:, across]
                if own and i == j:
                    match = match & (iota((tall, size), 0) != iota((tall, size), 1) + t)
                score = jnp.where(match, product[:, t : t + size], APART)
                soft = jnp.exp2((score - 1.0) * (sharpness * LOG2E))
                col_best[c, :, across] = jnp.maximum(
                    col_best[c, :, across], column_fold(score, jnp.maximum)
                )
                col_mass[c, :, across] = col_mass[c, :, across] + column_fold(soft, jnp.add)
                tops = score if tops is None else jnp.maximum(tops, score)
                sums = soft if sums is None else sums + soft
            if r is not None:
                size = tops.shape[1]
                row_best[r, down, :size] = jnp.maximum(row_best[r, down, :size], tops)
                row_mass[r, down, :size] = row_mass[r, down, :size] + sums


def settle(e, state):
    col_best, col_mass, row_best, row_mass = state[:4]
    best = jnp.max(col_best[e], axis=0, keepdims=True)
    mass = jnp.sum(col_mass[e], axis=0, keepdims=True)
    if e in ROW_BLOCKS:
        r = ROW_BLOCKS.index(e)
        tops, sums = [], []
        for t in range(0, BLOCK, 128):
            tops.append(jnp.max(row_best[r, t : t + 128, :].T, axis=0, keepdims=True))
            sums.append(jnp.sum(row_mass[r, t : t + 128, :].T, axis=0, keepdims=True))
        best = jnp.maximum(best, jnp.concatenate(tops, axis=1))
        mass = mass + jnp.concatenate(sums, axis=1)
    return best, mass


def store(blocks, best_in, mass_in, best_out, mass_out, state):
    if best_in is None:
        best_out[...] = jnp.full_like(best_out, APART)
        mass_out[...] = jnp.zeros_like(mass_out)
    else:
        best_out[...] = best_in[...]
        mass_out[...] = mass_in[...]
    for e in blocks:
        here = slice(e, e + 1)
        best, mass = settle(e, state)
        best_out[here, :] = jnp.maximum(best_out[here, :], best)
        mass_out[here, :] = mass_out[here, :] + mass


def early_kernel(b0l, b0h, b1l, b1h, b2l, b2h, best_out, mass_out, *state):
    b0, b1, b2 = (b0l, b0h), (b1l, b1h), (b2l, b2h)
    clear(state)
    for place, block in enumerate((b0, b1, b2)):
        spell(block, place, state)
    square(b0, b0, 0, 0, None, state, True)
    square(b1, b0, 1, 0, 0, state)
    square(b1, b2, 1, 2, 0, state)
    square(b2, b0, 2, 0, 1, state)
    store((0, 1, 2), None, None, best_out, mass_out, state)


def middle_kernel(
    b0l, b1l, b1h, b2l, b2h, b3l, b4l, low, high, best_in, mass_in, best_out, mass_out, *state
):
    b0, b1, b2, b3, b4 = (b0l, None), (b1l, b1h), (b2l, b2h), (b3l, None), (b4l, None)
    low, high = (low, None), (None, high)
    clear(state)
    for place, block in enumerate((b0, b1, b2, b4)):
        spell(block, place, state)
    square(b1, low, 1, 5, 0, state, parts=LOWS)
    square(b2, high, 2, 6, 1, state, parts=HIGHS)
    square(b1, high, 1, 6, 0, state, downs=LOWS, parts=HIGHS)
    square(b1, high, 1, 6, None, state, downs=HIGHS, parts=HIGHS)
    square(b2, low, 2, 5, 1, state, downs=HIGHS, parts=LOWS)
    square(b2, low, 2, 5, None, state, downs=LOWS, parts=LOWS)
    square(b0, b3, 0, 3, None, state, downs=LOWS, parts=LOWS)
    square(b1, b4, 1, 4, 0, state, parts=LOWS)
    square(b2, b3, 2, 3, 1, state, parts=LOWS)
    square(b4, b3, 3, 3, None, state, downs=LOWS, parts=LOWS)
    store((1, 2, 3, 4, 5, 6), best_in, mass_in, best_out, mass_out, state)


def late_kernel(
    b0h, b1l, b1h, b2l, b2h, b3l, b3h, b4l, b4h, low, high, best_in, mass_in, out, *state
):
    b0, b1, b2, b3, b4 = (None, b0h), (b1l, b1h), (b2l, b2h), (b3l, b3h), (b4l, b4h)
    low, high = (low, None), (None, high)
    clear(state)
    for place, block in enumerate((b0, b1, b2, b4)):
        spell(block, place, state)
    square(b0, b4, 0, 4, None, state, downs=HIGHS, parts=HIGHS)
    square(b1, b4, 1, 4, 0, state, parts=HIGHS)
    square(b2, b3, 2, 3, 1, state, parts=HIGHS)
    square(b4, b3, 3, 3, None, state, parts=HIGHS)
    square(b4, b3, 3, 3, None, state, downs=HIGHS, parts=LOWS)
    source_at = (iota((DEVICES, BLOCK), 0) + 1).astype(jnp.float32)
    line = iota((16, BLOCK), 0)
    back = []
    for e, block in enumerate((b0, b1, b2, b3, b4, low, high)):
        here = slice(e, e + 1)
        best, mass = jnp.maximum(best_in[here, :], -1.0), mass_in[here, :]
        if e in (1, 2, 3, 4):
            more, extra = settle(e, state)
            best = jnp.maximum(best, more)
            mass = mass + extra
        best = best + SHIFT
        names = names_of(block)
        if e == 5:
            names = jnp.where(iota(names.shape, 1) < LOW, names, 0.0)
        if e == 6:
            names = jnp.where(iota(names.shape, 1) >= LOW, names, 0.0)
        values = jnp.where((line & 1) == 0, best, mass)
        values = jnp.where((line >> 1).astype(jnp.float32) == names[2:3], values, 0.0)
        to = (source_at == names[1:2]).astype(jnp.bfloat16)
        back.append(joined(matmul(split(values), to, NT)))
    back.append(jnp.zeros((128 - 16 * len(back), DEVICES), jnp.float32))
    out[...] = jnp.concatenate(back, axis=0).T


def finish_kernel(arrived, places, best_out, mass_out):
    shape = (DEVICES, DEVICES)
    at, col = iota(shape, 0), iota(shape, 1)
    base, ay, az = at >> 4, (at >> 2) & 3, at & 3
    turned = (base & 1) == 1
    best = mass = None
    pieces = split(arrived[...].T)
    for e, (dy, dz) in enumerate(SPOTS):
        by = (ay + jnp.where(turned, dz, (-dy) & 3)) & 3
        bz = (az + jnp.where(turned, dy, (-dz) & 3)) & 3
        move = (col == base * MEMBERS + by * 4 + bz).astype(jnp.bfloat16)
        part = jnp.concatenate(
            [pieces[128 * p + 16 * e : 128 * p + 16 * e + 16] for p in range(3)], axis=0
        )
        moved = joined(matmul(part, move, NT))
        best = moved if best is None else jnp.maximum(best, moved)
        mass = moved if mass is None else mass + moved
    merged = jnp.where((iota((16, DEVICES), 0) & 1) == 0, best, mass)
    holder = (iota((DEVICES, ROWS), 0) == places[0:1, :]).astype(jnp.bfloat16)
    picked = joined(matmul(split(merged), holder, NN))
    line = iota((16, ROWS), 0)
    turn = places[1:2, :]
    best = jnp.sum(jnp.where(line == 2 * turn, picked, 0.0), axis=0, keepdims=True)
    best_out[...] = best - SHIFT
    mass = jnp.sum(jnp.where(line == 2 * turn + 1, picked, 0.0), axis=0, keepdims=True)
    mass_out[...] = jnp.log1p(mass)


def call(kernel, out_shape, scratch=(), flops=0, name=None):
    return pl.pallas_call(
        kernel,
        out_shape=out_shape,
        scratch_shapes=scratch,
        compiler_params=pltpu.CompilerParams(vmem_limit_bytes=VMEM_LIMIT),
        cost_estimate=pl.CostEstimate(flops=flops, bytes_accessed=8_000_000, transcendentals=0),
        name=name,
    )


def hop(dy, dz):
    pairs = []
    for g in range(GROUPS):
        up, along = (-dz, -dy) if g & 1 else (dy, dz)
        for y in range(4):
            for z in range(4):
                source = ((y + up) % 4) * 4 + (z + along) % 4
                pairs.append((g * MEMBERS + source, g * MEMBERS + y * 4 + z))
    return pairs


def from_spot(x, dy, dz):
    return lax.ppermute(x, AXES, hop(dy, dz))


def fast(embeddings, labels, cluster_slot):
    f32, bf16, i32 = jnp.float32, jnp.bfloat16, jnp.int32
    shape = jax.ShapeDtypeStruct
    spread, places = call(
        prelude_kernel,
        (shape((HELD, WIDE), bf16), shape((8, ROWS), i32)),
        flops=3_000_000_000,
        name="prelude",
    )(labels.reshape(1, ROWS), cluster_slot.reshape(1, ROWS), embeddings)
    arrived = lax.all_to_all(spread, AXES, split_axis=0, concat_axis=0, tiled=True)
    b0l, b0h, over = call(
        pack_kernel,
        (
            shape((LOW_SENT, FEAT), bf16),
            shape((HIGH_SENT, FEAT), bf16),
            shape((8, 128), i32),
        ),
        flops=3_000_000_000,
        name="pack",
    )(arrived)
    b1l = from_spot(b0l, 1, 0)
    b2l = from_spot(b0l, 0, 1)
    b1h = from_spot(b0h, 1, 0)
    b2h = from_spot(b0h, 0, 1)
    high, b1l, b2l = lax.optimization_barrier((b0h, b1l, b2l))
    high = from_spot(high, 3, 0)
    b3l = from_spot(b1l, 1, 0)
    b4l = from_spot(b2l, 0, 1)
    low, b2h = lax.optimization_barrier((b0l, b2h))
    b3h = from_spot(b1h, 1, 0)
    b4h = from_spot(b2h, 0, 1)
    low = from_spot(low, 0, 3)

    def state(places):
        return (
            pltpu.VMEM((7, 8, BLOCK), f32),
            pltpu.VMEM((7, 8, BLOCK), f32),
            pltpu.VMEM((2, BLOCK, 128), f32),
            pltpu.VMEM((2, BLOCK, 128), f32),
            pltpu.VMEM((places, BLOCK, 128), f32),
        )

    stats = (shape((8, BLOCK), f32), shape((8, BLOCK), f32))
    best, mass = call(
        early_kernel, stats, scratch=state(3), flops=6_000_000_000, name="early"
    )(b0l, b0h, b1l, b1h, b2l, b2h)
    best, mass = call(
        middle_kernel, stats, scratch=state(4), flops=1_500_000_000, name="middle"
    )(b0l, b1l, b1h, b2l, b2h, b3l, b4l, low, high, best, mass)
    message = call(
        late_kernel,
        shape((DEVICES, 128), f32),
        scratch=state(4),
        flops=3_000_000_000,
        name="late",
    )(b0h, b1l, b1h, b2l, b2h, b3l, b3h, b4l, b4h, low, high, best, mass)
    answer = lax.all_to_all(message, AXES, split_axis=0, concat_axis=0, tiled=True)
    best, mass = call(
        finish_kernel,
        (shape((1, ROWS), f32), shape((1, ROWS), f32)),
        flops=ROWS * ROWS * 128,
        name="finish",
    )(answer, places)
    return (best.reshape(ROWS), mass.reshape(ROWS)), jnp.max(over)


def general(embeddings, labels, cluster_slot):
    groups = lax.axis_size("grp")
    members = lax.axis_size("blk")
    row_count, feature_count = embeddings.shape
    capacity = row_count // 4
    held = groups * capacity
    widened = embeddings.astype(jnp.float32)
    units = (
        widened * lax.rsqrt(jnp.sum(widened * widened, axis=1, keepdims=True) + epsilon)
    ).astype(jnp.bfloat16)
    slot_ids = cluster_slot[labels]
    owner_group = slot_ids // (cluster_slot.shape[0] // groups)
    owner_onehot = (owner_group[:, None] == jnp.arange(groups, dtype=jnp.int32)[None, :]).astype(
        jnp.int32
    )
    earlier = jnp.cumsum(owner_onehot, axis=0) - owner_onehot
    send_place = owner_group * capacity + jnp.sum(earlier * owner_onehot, axis=1)
    outgoing = jnp.zeros((held, feature_count), jnp.bfloat16).at[send_place].set(units)
    outgoing_slots = jnp.full((held,), -1, jnp.int32).at[send_place].set(slot_ids)
    rows = lax.all_to_all(outgoing, "grp", split_axis=0, concat_axis=0, tiled=True)
    slots = lax.all_to_all(outgoing_slots, "grp", split_axis=0, concat_axis=0, tiled=True)
    ring = [(i, (i + 1) % members) for i in range(members)]
    local = jnp.arange(held, dtype=jnp.int32)
    place = lax.axis_index("blk")
    own_ids = place * held + local

    def step(turn, carry):
        key_rows, key_slots, best, mass = carry
        scores = jnp.einsum("qd,kd->qk", rows, key_rows, preferred_element_type=jnp.float32)
        matched = (slots[:, None] == key_slots[None, :]) & (key_slots[None, :] >= 0)
        owner = (place - turn) & (members - 1)
        matched = matched & (own_ids[:, None] != (owner * held + local)[None, :])
        best = jnp.maximum(best, jnp.max(jnp.where(matched, scores, -1.0), axis=1))
        mass = mass + jnp.sum(
            jnp.where(matched, jnp.exp(sharpness * (scores - 1.0)), 0.0), axis=1
        )
        key_rows = lax.ppermute(key_rows, "blk", ring)
        key_slots = lax.ppermute(key_slots, "blk", ring)
        return key_rows, key_slots, best, mass

    start = (
        rows,
        slots,
        jnp.full((held,), -1.0, jnp.float32),
        jnp.zeros((held,), jnp.float32),
    )
    _, _, best, mass = lax.fori_loop(0, members, step, start)
    best = lax.all_to_all(best, "grp", split_axis=0, concat_axis=0, tiled=True)
    mass = lax.all_to_all(mass, "grp", split_axis=0, concat_axis=0, tiled=True)
    return (best[send_place], jnp.log1p(mass[send_place]))


def body(embeddings, labels, cluster_slot):
    result, over = fast(embeddings, labels, cluster_slot)
    return lax.cond(
        over > 0, lambda: general(embeddings, labels, cluster_slot), lambda: result
    )


def solution(mesh):
    placed = (P(AXES, None), P(AXES), P())
    return jax.shard_map(
        body,
        mesh=mesh,
        in_specs=placed,
        out_specs=(P(AXES), P(AXES)),
        check_vma=False,
    )
```

```python
import jax
import jax.numpy as jnp
from jax import lax
from jax.experimental import pallas as pl
from jax.experimental.pallas import tpu as pltpu
from jax.sharding import PartitionSpec as P

epsilon = 1e-06
sharpness = 8.0

ROWS = 512
FEAT = 768
WIDE = 896
GROUPS = 8
MEMBERS = 16
DEVICES = GROUPS * MEMBERS
SHARE = 8
HELD = DEVICES * SHARE
SENT = 608
ROOM = SENT - 16
BLOCK = 640
APART = -64.0
LOG2E = 1.4426950408889634
AXES = ("grp", "blk")
VMEM_LIMIT = 24 * 1024 * 1024

SPOTS = ((0, 0), (1, 0), (0, 1), (2, 0), (0, 2), (0, 3), (3, 0))
LOW = 256
LOW_SENT = LOW + 16
HIGH_SENT = SENT - LOW
ROW_BLOCKS = (1, 2)
SHIFT = 2.0


def iota(shape, axis):
    return lax.broadcasted_iota(jnp.int32, shape, axis)


def matmul(a, b, dims, exact=False):
    return lax.dot_general(
        a,
        b,
        (dims, ((), ())),
        precision=lax.Precision.HIGHEST if exact else None,
        preferred_element_type=jnp.float32,
    )


NN = ((1,), (0,))
NT = ((1,), (1,))


def split(x):
    high = x.astype(jnp.bfloat16)
    rest = x - high.astype(jnp.float32)
    middle = rest.astype(jnp.bfloat16)
    low = (rest - middle.astype(jnp.float32)).astype(jnp.bfloat16)
    return jnp.concatenate([high, middle, low], axis=0)


def joined(x):
    size = x.shape[0] // 3
    return x[:size] + x[size : 2 * size] + x[2 * size :]


def prelude_kernel(labels, slots, rows, spread, places):
    lab = labels[...]
    table = slots[...]
    by_cluster = (iota((ROWS, ROWS), 0) == lab).astype(jnp.bfloat16)
    sub = iota((8, ROWS), 0)
    parts = jnp.where(sub == 0, table >> 6, jnp.where(sub == 1, table & 63, 0)).astype(jnp.bfloat16)
    found = matmul(parts, by_cluster, NN)
    group = found[0:1].astype(jnp.int32)
    in_group = sub == group
    before = (iota((ROWS, ROWS), 0) < iota((ROWS, ROWS), 1)).astype(jnp.bfloat16)
    counts = matmul(in_group.astype(jnp.bfloat16), before, NN)
    rank = jnp.sum(jnp.where(in_group, counts, 0.0), axis=0, keepdims=True).astype(jnp.int32)
    holder = group * MEMBERS + ((rank + lax.axis_index("blk")) & (MEMBERS - 1))
    turn = rank >> 4
    places[...] = jnp.where(sub == 0, holder, turn)

    wide = rows[...].astype(jnp.float32)
    norm = lax.rsqrt(jnp.sum(wide * wide, axis=1, keepdims=True) + epsilon)
    units = (wide * norm).astype(jnp.bfloat16)
    lanes = iota((128, ROWS), 0)
    marks = jnp.where(lanes == 0, found[1:2] + 1.0, 0.0).astype(jnp.bfloat16)
    goal = holder * SHARE + turn
    totals = matmul(
        jnp.ones((128, ROWS), jnp.bfloat16), (lanes - 64 == group).astype(jnp.bfloat16), NT
    )
    totals = jnp.where((iota((ROWS, 128), 0) & (SHARE - 1)) == 0, totals[0:1], 0.0)
    for t in range(0, HELD, ROWS):
        here = pl.ds(t, ROWS)
        pick = (iota((ROWS, ROWS), 0) + t == goal).astype(jnp.bfloat16)
        spread[here, :FEAT] = matmul(pick, units, NN).astype(jnp.bfloat16)
        spread[here, FEAT:] = (matmul(pick, marks, NT) + totals).astype(jnp.bfloat16)


def pack_low_kernel(arrived, low, position_out):
    tails = arrived[:, FEAT:]
    at, line = iota((8, HELD), 1), iota((8, HELD), 0)
    clusters = matmul((iota((8, 128), 1) == 0).astype(jnp.bfloat16), tails, NT)
    held = clusters > 0.0
    before = (iota((HELD, HELD), 0) < iota((HELD, HELD), 1)).astype(jnp.bfloat16)
    position = matmul(held.astype(jnp.bfloat16), before, NN)
    position = jnp.where(held, position, -1.0).astype(jnp.int32)
    position_out[...] = position
    names = jnp.where(line == 1, (at >> 3) + 1, jnp.where(line == 2, at & 7, 0))
    names = jnp.where(line == 0, clusters, names.astype(jnp.float32)).astype(jnp.bfloat16)
    pick = (iota((BLOCK, HELD), 0) == position[0:1]).astype(jnp.bfloat16)
    low[:LOW, :] = matmul(pick[:LOW], arrived[:, :FEAT], NN).astype(jnp.bfloat16)
    named = matmul(names, pick, NT)
    named = jnp.concatenate([named, jnp.zeros((8, FEAT - BLOCK), jnp.float32)], axis=1)
    low[LOW:, :] = jnp.concatenate([named, jnp.zeros_like(named)], axis=0).astype(jnp.bfloat16)


def pack_high_kernel(arrived, low, position, high):
    pick = (iota((ROOM - LOW, HELD), 0) + LOW == position[0:1, :]).astype(jnp.bfloat16)
    high[: ROOM - LOW, :] = matmul(pick, arrived[:, :FEAT], NN).astype(jnp.bfloat16)
    high[ROOM - LOW :, :] = low[LOW:, :]


def over_kernel(arrived, over):
    one = ((iota((128, HELD), 0) * SHARE) == iota((128, HELD), 1)).astype(jnp.bfloat16)
    counts = matmul(one, arrived[:, FEAT:], NN).astype(jnp.int32)
    counts = jnp.where(iota((128, 128), 1) >= 64, counts, 0)
    turned = iota((128, 128), 0) & (MEMBERS - 1)
    most = jnp.zeros((1, 128), jnp.int32)
    for k in range(MEMBERS):
        gets = (counts + (MEMBERS - 1) - ((k - turned) & (MEMBERS - 1))) >> 4
        most = jnp.maximum(most, jnp.sum(gets, axis=0, keepdims=True))
    over[...] = jnp.broadcast_to((most > ROOM).astype(jnp.int32), (8, 128))


def column_fold(x, op):
    while x.shape[0] > 8:
        half = x.shape[0] // 16 * 8
        rest = x[2 * half :]
        x = op(x[:half], x[half : 2 * half])
        if rest.shape[0]:
            x = jnp.concatenate([op(x[:8], rest), x[8:]], axis=0) if half > 8 else op(x, rest)
    return x


LOWS = ((0, 256),)
HIGHS = ((256, 256), (512, SENT - 512))
PARTS = LOWS + HIGHS


def clear(state):
    col_best, col_mass, row_best, row_mass = state[:4]
    for ref in (col_best, row_best):
        ref[...] = jnp.full_like(ref, APART)
    for ref in (col_mass, row_mass):
        ref[...] = jnp.zeros_like(ref)


def names_of(block):
    part = block[0] if block[1] is None else block[1]
    return part[part.shape[0] - 16 :, :BLOCK].astype(jnp.float32)


def spell(block, place, state):
    clusters = names_of(block)[0:1]
    clusters = jnp.where(clusters > 0.0, clusters, -1.0)
    for t in range(0, BLOCK, 128):
        here = slice(t, t + 128)
        state[4][place, here, :] = jnp.broadcast_to(clusters[:, here], (128, 128)).T


def part_of(block, first, size):
    if first < LOW:
        return block[0][first : first + size, :]
    return block[1][first - LOW : first - LOW + size, :]


def square(rows, cols, place, c, r, state, own=False, downs=PARTS, parts=PARTS):
    col_best, col_mass, row_best, row_mass, spelt = state
    clusters = names_of(cols)[0:1]
    for i, tall in downs:
        for j, wide in parts:
            product = matmul(part_of(rows, i, tall), part_of(cols, j, wide), NT)
            down = slice(i, i + tall)
            tops = sums = None
            for t in range(0, wide, 128):
                size = min(128, wide - t)
                across = slice(j + t, j + t + size)
                match = spelt[place, down, :size] == clusters[:, across]
                if own and i == j:
                    match = match & (iota((tall, size), 0) != iota((tall, size), 1) + t)
                score = jnp.where(match, product[:, t : t + size], APART)
                soft = jnp.exp2((score - 1.0) * (sharpness * LOG2E))
                col_best[c, :, across] = jnp.maximum(
                    col_best[c, :, across], column_fold(score, jnp.maximum)
                )
                col_mass[c, :, across] = col_mass[c, :, across] + column_fold(soft, jnp.add)
                tops = score if tops is None else jnp.maximum(tops, score)
                sums = soft if sums is None else sums + soft
            if r is not None:
                size = tops.shape[1]
                row_best[r, down, :size] = jnp.maximum(row_best[r, down, :size], tops)
                row_mass[r, down, :size] = row_mass[r, down, :size] + sums


def settle(e, state):
    col_best, col_mass, row_best, row_mass = state[:4]
    best = jnp.max(col_best[e], axis=0, keepdims=True)
    mass = jnp.sum(col_mass[e], axis=0, keepdims=True)
    if e in ROW_BLOCKS:
        r = ROW_BLOCKS.index(e)
        tops, sums = [], []
        for t in range(0, BLOCK, 128):
            tops.append(jnp.max(row_best[r, t : t + 128, :].T, axis=0, keepdims=True))
            sums.append(jnp.sum(row_mass[r, t : t + 128, :].T, axis=0, keepdims=True))
        best = jnp.maximum(best, jnp.concatenate(tops, axis=1))
        mass = mass + jnp.concatenate(sums, axis=1)
    return best, mass


def store(blocks, best_in, mass_in, best_out, mass_out, state):
    if best_in is None:
        best_out[...] = jnp.full_like(best_out, APART)
        mass_out[...] = jnp.zeros_like(mass_out)
    else:
        best_out[...] = best_in[...]
        mass_out[...] = mass_in[...]
    for e in blocks:
        here = slice(e, e + 1)
        best, mass = settle(e, state)
        best_out[here, :] = jnp.maximum(best_out[here, :], best)
        mass_out[here, :] = mass_out[here, :] + mass


def early_kernel(b0l, b0h, b1l, b1h, b2l, b2h, best_out, mass_out, *state):
    b0, b1, b2 = (b0l, b0h), (b1l, b1h), (b2l, b2h)
    clear(state)
    for place, block in enumerate((b0, b1, b2)):
        spell(block, place, state)
    square(b0, b0, 0, 0, None, state, True)
    square(b1, b0, 1, 0, 0, state)
    square(b1, b2, 1, 2, 0, state)
    square(b2, b0, 2, 0, 1, state)
    store((0, 1, 2), None, None, best_out, mass_out, state)


def middle_kernel(
    b0l, b1l, b1h, b2l, b2h, b3l, b4l, low, high, best_in, mass_in, best_out, mass_out, *state
):
    b0, b1, b2, b3, b4 = (b0l, None), (b1l, b1h), (b2l, b2h), (b3l, None), (b4l, None)
    low, high = (low, None), (None, high)
    clear(state)
    for place, block in enumerate((b0, b1, b2, b4)):
        spell(block, place, state)
    square(b1, low, 1, 5, 0, state, parts=LOWS)
    square(b2, high, 2, 6, 1, state, parts=HIGHS)
    square(b1, high, 1, 6, 0, state, downs=LOWS, parts=HIGHS)
    square(b1, high, 1, 6, None, state, downs=HIGHS, parts=HIGHS)
    square(b2, low, 2, 5, 1, state, downs=HIGHS, parts=LOWS)
    square(b2, low, 2, 5, None, state, downs=LOWS, parts=LOWS)
    square(b0, b3, 0, 3, None, state, downs=LOWS, parts=LOWS)
    square(b1, b4, 1, 4, 0, state, parts=LOWS)
    square(b2, b3, 2, 3, 1, state, parts=LOWS)
    square(b4, b3, 3, 3, None, state, downs=LOWS, parts=LOWS)
    store((1, 2, 3, 4, 5, 6), best_in, mass_in, best_out, mass_out, state)


def late_kernel(
    b0h, b1l, b1h, b2l, b2h, b3l, b3h, b4l, b4h, low, high, best_in, mass_in, out, *state
):
    b0, b1, b2, b3, b4 = (None, b0h), (b1l, b1h), (b2l, b2h), (b3l, b3h), (b4l, b4h)
    low, high = (low, None), (None, high)
    clear(state)
    for place, block in enumerate((b0, b1, b2, b4)):
        spell(block, place, state)
    square(b0, b4, 0, 4, None, state, downs=HIGHS, parts=HIGHS)
    square(b1, b4, 1, 4, 0, state, parts=HIGHS)
    square(b2, b3, 2, 3, 1, state, parts=HIGHS)
    square(b4, b3, 3, 3, None, state, parts=HIGHS)
    square(b4, b3, 3, 3, None, state, downs=HIGHS, parts=LOWS)
    source_at = (iota((DEVICES, BLOCK), 0) + 1).astype(jnp.float32)
    line = iota((16, BLOCK), 0)
    back = []
    for e, block in enumerate((b0, b1, b2, b3, b4, low, high)):
        here = slice(e, e + 1)
        best, mass = jnp.maximum(best_in[here, :], -1.0), mass_in[here, :]
        if e in (1, 2, 3, 4):
            more, extra = settle(e, state)
            best = jnp.maximum(best, more)
            mass = mass + extra
        best = best + SHIFT
        names = names_of(block)
        if e == 5:
            names = jnp.where(iota(names.shape, 1) < LOW, names, 0.0)
        if e == 6:
            names = jnp.where(iota(names.shape, 1) >= LOW, names, 0.0)
        values = jnp.where((line & 1) == 0, best, mass)
        values = jnp.where((line >> 1).astype(jnp.float32) == names[2:3], values, 0.0)
        to = (source_at == names[1:2]).astype(jnp.bfloat16)
        back.append(joined(matmul(split(values), to, NT)))
    back.append(jnp.zeros((128 - 16 * len(back), DEVICES), jnp.float32))
    out[...] = jnp.concatenate(back, axis=0).T


def finish_kernel(arrived, places, best_out, mass_out):
    shape = (DEVICES, DEVICES)
    at, col = iota(shape, 0), iota(shape, 1)
    base, ay, az = at >> 4, (at >> 2) & 3, at & 3
    turned = (base & 1) == 1
    best = mass = None
    pieces = split(arrived[...].T)
    for e, (dy, dz) in enumerate(SPOTS):
        by = (ay + jnp.where(turned, dz, (-dy) & 3)) & 3
        bz = (az + jnp.where(turned, dy, (-dz) & 3)) & 3
        move = (col == base * MEMBERS + by * 4 + bz).astype(jnp.bfloat16)
        part = jnp.concatenate(
            [pieces[128 * p + 16 * e : 128 * p + 16 * e + 16] for p in range(3)], axis=0
        )
        moved = joined(matmul(part, move, NT))
        best = moved if best is None else jnp.maximum(best, moved)
        mass = moved if mass is None else mass + moved
    merged = jnp.where((iota((16, DEVICES), 0) & 1) == 0, best, mass)
    holder = (iota((DEVICES, ROWS), 0) == places[0:1, :]).astype(jnp.bfloat16)
    picked = joined(matmul(split(merged), holder, NN))
    line = iota((16, ROWS), 0)
    turn = places[1:2, :]
    best = jnp.sum(jnp.where(line == 2 * turn, picked, 0.0), axis=0, keepdims=True)
    best_out[...] = best - SHIFT
    mass = jnp.sum(jnp.where(line == 2 * turn + 1, picked, 0.0), axis=0, keepdims=True)
    mass_out[...] = jnp.log1p(mass)


def call(kernel, out_shape, scratch=(), flops=0, name=None):
    return pl.pallas_call(
        kernel,
        out_shape=out_shape,
        scratch_shapes=scratch,
        compiler_params=pltpu.CompilerParams(vmem_limit_bytes=VMEM_LIMIT),
        cost_estimate=pl.CostEstimate(flops=flops, bytes_accessed=8_000_000, transcendentals=0),
        name=name,
    )


def hop(dy, dz):
    pairs = []
    for g in range(GROUPS):
        up, along = (-dz, -dy) if g & 1 else (dy, dz)
        for y in range(4):
            for z in range(4):
                source = ((y + up) % 4) * 4 + (z + along) % 4
                pairs.append((g * MEMBERS + source, g * MEMBERS + y * 4 + z))
    return pairs


def from_spot(x, dy, dz):
    return lax.ppermute(x, AXES, hop(dy, dz))


def fast(embeddings, labels, cluster_slot):
    f32, bf16, i32 = jnp.float32, jnp.bfloat16, jnp.int32
    shape = jax.ShapeDtypeStruct
    spread, places = call(
        prelude_kernel,
        (shape((HELD, WIDE), bf16), shape((8, ROWS), i32)),
        flops=3_000_000_000,
        name="prelude",
    )(labels.reshape(1, ROWS), cluster_slot.reshape(1, ROWS), embeddings)
    arrived = lax.all_to_all(spread, AXES, split_axis=0, concat_axis=0, tiled=True)
    b0l, position = call(
        pack_low_kernel,
        (shape((LOW_SENT, FEAT), bf16), shape((8, HELD), i32)),
        flops=2_000_000_000,
        name="pack_low",
    )(arrived)
    b0h = call(
        pack_high_kernel, shape((HIGH_SENT, FEAT), bf16), flops=1_000_000_000, name="pack_high"
    )(arrived, b0l, position)
    b1l = from_spot(b0l, 1, 0)
    b2l = from_spot(b0l, 0, 1)
    b1h = from_spot(b0h, 1, 0)
    b2h = from_spot(b0h, 0, 1)
    high, b1l, b2l = lax.optimization_barrier((b0h, b1l, b2l))
    high = from_spot(high, 3, 0)
    b3l = from_spot(b1l, 1, 0)
    b4l = from_spot(b2l, 0, 1)
    low, b1h, b2h = lax.optimization_barrier((b0l, b1h, b2h))
    over = call(over_kernel, shape((8, 128), i32), flops=10_000_000, name="over")(arrived)
    b3h = from_spot(b1h, 1, 0)
    b4h = from_spot(b2h, 0, 1)
    low = from_spot(low, 0, 3)

    def state(places):
        return (
            pltpu.VMEM((7, 8, BLOCK), f32),
            pltpu.VMEM((7, 8, BLOCK), f32),
            pltpu.VMEM((2, BLOCK, 128), f32),
            pltpu.VMEM((2, BLOCK, 128), f32),
            pltpu.VMEM((places, BLOCK, 128), f32),
        )

    stats = (shape((8, BLOCK), f32), shape((8, BLOCK), f32))
    best, mass = call(
        early_kernel, stats, scratch=state(3), flops=6_000_000_000, name="early"
    )(b0l, b0h, b1l, b1h, b2l, b2h)
    best, mass = call(
        middle_kernel, stats, scratch=state(4), flops=1_500_000_000, name="middle"
    )(b0l, b1l, b1h, b2l, b2h, b3l, b4l, low, high, best, mass)
    message = call(
        late_kernel,
        shape((DEVICES, 128), f32),
        scratch=state(4),
        flops=3_000_000_000,
        name="late",
    )(b0h, b1l, b1h, b2l, b2h, b3l, b3h, b4l, b4h, low, high, best, mass)
    answer = lax.all_to_all(message, AXES, split_axis=0, concat_axis=0, tiled=True)
    best, mass = call(
        finish_kernel,
        (shape((1, ROWS), f32), shape((1, ROWS), f32)),
        flops=ROWS * ROWS * 128,
        name="finish",
    )(answer, places)
    return (best.reshape(ROWS), mass.reshape(ROWS)), jnp.max(over)


def general(embeddings, labels, cluster_slot):
    groups = lax.axis_size("grp")
    members = lax.axis_size("blk")
    row_count, feature_count = embeddings.shape
    capacity = row_count // 4
    held = groups * capacity
    widened = embeddings.astype(jnp.float32)
    units = (
        widened * lax.rsqrt(jnp.sum(widened * widened, axis=1, keepdims=True) + epsilon)
    ).astype(jnp.bfloat16)
    slot_ids = cluster_slot[labels]
    owner_group = slot_ids // (cluster_slot.shape[0] // groups)
    owner_onehot = (owner_group[:, None] == jnp.arange(groups, dtype=jnp.int32)[None, :]).astype(
        jnp.int32
    )
    earlier = jnp.cumsum(owner_onehot, axis=0) - owner_onehot
    send_place = owner_group * capacity + jnp.sum(earlier * owner_onehot, axis=1)
    outgoing = jnp.zeros((held, feature_count), jnp.bfloat16).at[send_place].set(units)
    outgoing_slots = jnp.full((held,), -1, jnp.int32).at[send_place].set(slot_ids)
    rows = lax.all_to_all(outgoing, "grp", split_axis=0, concat_axis=0, tiled=True)
    slots = lax.all_to_all(outgoing_slots, "grp", split_axis=0, concat_axis=0, tiled=True)
    ring = [(i, (i + 1) % members) for i in range(members)]
    local = jnp.arange(held, dtype=jnp.int32)
    place = lax.axis_index("blk")
    own_ids = place * held + local

    def step(turn, carry):
        key_rows, key_slots, best, mass = carry
        scores = jnp.einsum("qd,kd->qk", rows, key_rows, preferred_element_type=jnp.float32)
        matched = (slots[:, None] == key_slots[None, :]) & (key_slots[None, :] >= 0)
        owner = (place - turn) & (members - 1)
        matched = matched & (own_ids[:, None] != (owner * held + local)[None, :])
        best = jnp.maximum(best, jnp.max(jnp.where(matched, scores, -1.0), axis=1))
        mass = mass + jnp.sum(
            jnp.where(matched, jnp.exp(sharpness * (scores - 1.0)), 0.0), axis=1
        )
        key_rows = lax.ppermute(key_rows, "blk", ring)
        key_slots = lax.ppermute(key_slots, "blk", ring)
        return key_rows, key_slots, best, mass

    start = (
        rows,
        slots,
        jnp.full((held,), -1.0, jnp.float32),
        jnp.zeros((held,), jnp.float32),
    )
    _, _, best, mass = lax.fori_loop(0, members, step, start)
    best = lax.all_to_all(best, "grp", split_axis=0, concat_axis=0, tiled=True)
    mass = lax.all_to_all(mass, "grp", split_axis=0, concat_axis=0, tiled=True)
    return (best[send_place], jnp.log1p(mass[send_place]))


def body(embeddings, labels, cluster_slot):
    result, over = fast(embeddings, labels, cluster_slot)
    return lax.cond(
        over > 0, lambda: general(embeddings, labels, cluster_slot), lambda: result
    )


def solution(mesh):
    placed = (P(AXES, None), P(AXES), P())
    return jax.shard_map(
        body,
        mesh=mesh,
        in_specs=placed,
        out_specs=(P(AXES), P(AXES)),
        check_vma=False,
    )
```

```python
import jax
import jax.numpy as jnp
from jax import lax
from jax.experimental import pallas as pl
from jax.experimental.pallas import tpu as pltpu
from jax.sharding import PartitionSpec as P

epsilon = 1e-06
sharpness = 8.0

ROWS = 512
FEAT = 768
WIDE = 896
GROUPS = 8
MEMBERS = 16
DEVICES = GROUPS * MEMBERS
SHARE = 8
HELD = DEVICES * SHARE
SENT = 608
ROOM = SENT - 16
BLOCK = 640
APART = -64.0
LOG2E = 1.4426950408889634
AXES = ("grp", "blk")
VMEM_LIMIT = 24 * 1024 * 1024

SPOTS = ((0, 0), (1, 0), (0, 1), (2, 0), (0, 2), (0, 3), (3, 0))
LOW = 256
LOW_SENT = LOW + 16
HIGH_SENT = SENT - LOW
ROW_BLOCKS = (1, 2)
SHIFT = 2.0


def iota(shape, axis):
    return lax.broadcasted_iota(jnp.int32, shape, axis)


def matmul(a, b, dims, exact=False):
    return lax.dot_general(
        a,
        b,
        (dims, ((), ())),
        precision=lax.Precision.HIGHEST if exact else None,
        preferred_element_type=jnp.float32,
    )


NN = ((1,), (0,))
NT = ((1,), (1,))


def split(x):
    high = x.astype(jnp.bfloat16)
    rest = x - high.astype(jnp.float32)
    middle = rest.astype(jnp.bfloat16)
    low = (rest - middle.astype(jnp.float32)).astype(jnp.bfloat16)
    return jnp.concatenate([high, middle, low], axis=0)


def joined(x):
    size = x.shape[0] // 3
    return x[:size] + x[size : 2 * size] + x[2 * size :]


def prelude_kernel(labels, slots, rows, spread, places):
    lab = labels[...]
    table = slots[...]
    by_cluster = (iota((ROWS, ROWS), 0) == lab).astype(jnp.bfloat16)
    sub = iota((8, ROWS), 0)
    parts = jnp.where(sub == 0, table >> 6, jnp.where(sub == 1, table & 63, 0)).astype(jnp.bfloat16)
    found = matmul(parts, by_cluster, NN)
    group = found[0:1].astype(jnp.int32)
    in_group = sub == group
    before = (iota((ROWS, ROWS), 0) < iota((ROWS, ROWS), 1)).astype(jnp.bfloat16)
    counts = matmul(in_group.astype(jnp.bfloat16), before, NN)
    rank = jnp.sum(jnp.where(in_group, counts, 0.0), axis=0, keepdims=True).astype(jnp.int32)
    holder = group * MEMBERS + ((rank + lax.axis_index("blk")) & (MEMBERS - 1))
    turn = rank >> 4
    places[...] = jnp.where(sub == 0, holder, turn)

    wide = rows[...].astype(jnp.float32)
    norm = lax.rsqrt(jnp.sum(wide * wide, axis=1, keepdims=True) + epsilon)
    units = (wide * norm).astype(jnp.bfloat16)
    lanes = iota((128, ROWS), 0)
    marks = jnp.where(lanes == 0, found[1:2] + 1.0, 0.0).astype(jnp.bfloat16)
    goal = holder * SHARE + turn
    totals = matmul(
        jnp.ones((128, ROWS), jnp.bfloat16), (lanes - 64 == group).astype(jnp.bfloat16), NT
    )
    totals = jnp.where((iota((ROWS, 128), 0) & (SHARE - 1)) == 0, totals[0:1], 0.0)
    for t in range(0, HELD, ROWS):
        here = pl.ds(t, ROWS)
        pick = (iota((ROWS, ROWS), 0) + t == goal).astype(jnp.bfloat16)
        spread[here, :FEAT] = matmul(pick, units, NN).astype(jnp.bfloat16)
        spread[here, FEAT:] = (matmul(pick, marks, NT) + totals).astype(jnp.bfloat16)


def pack_low_kernel(arrived, low, position_out, names_out):
    tails = arrived[:, FEAT:]
    at, line = iota((8, HELD), 1), iota((8, HELD), 0)
    clusters = matmul((iota((8, 128), 1) == 0).astype(jnp.bfloat16), tails, NT)
    held = clusters > 0.0
    before = (iota((HELD, HELD), 0) < iota((HELD, HELD), 1)).astype(jnp.bfloat16)
    position = matmul(held.astype(jnp.bfloat16), before, NN)
    position = jnp.where(held, position, -1.0).astype(jnp.int32)
    position_out[...] = position
    names = jnp.where(line == 1, (at >> 3) + 1, jnp.where(line == 2, at & 7, 0))
    names = jnp.where(line == 0, clusters, names.astype(jnp.float32))
    names_out[...] = names
    pick = (iota((LOW, HELD), 0) == position[0:1]).astype(jnp.bfloat16)
    low[:LOW, :] = matmul(pick, arrived[:, :FEAT], NN).astype(jnp.bfloat16)
    named = matmul(names.astype(jnp.bfloat16), pick, NT)
    named = jnp.concatenate([named, jnp.zeros((8, FEAT - LOW), jnp.float32)], axis=1)
    low[LOW:, :] = jnp.concatenate([named, jnp.zeros_like(named)], axis=0).astype(jnp.bfloat16)


def pack_high_kernel(arrived, low, position, names, high):
    pick = (iota((BLOCK - LOW, HELD), 0) + LOW == position[0:1, :]).astype(jnp.bfloat16)
    high[: ROOM - LOW, :] = matmul(pick[: ROOM - LOW], arrived[:, :FEAT], NN).astype(jnp.bfloat16)
    named = matmul(names[...].astype(jnp.bfloat16), pick, NT)
    named = jnp.concatenate([named, jnp.zeros_like(named)], axis=0).astype(jnp.bfloat16)
    high[ROOM - LOW :, :LOW] = low[LOW:, :LOW]
    high[ROOM - LOW :, LOW:BLOCK] = named
    high[ROOM - LOW :, BLOCK:] = jnp.zeros((16, FEAT - BLOCK), jnp.bfloat16)


def over_kernel(arrived, over):
    one = ((iota((128, HELD), 0) * SHARE) == iota((128, HELD), 1)).astype(jnp.bfloat16)
    counts = matmul(one, arrived[:, FEAT:], NN).astype(jnp.int32)
    counts = jnp.where(iota((128, 128), 1) >= 64, counts, 0)
    turned = iota((128, 128), 0) & (MEMBERS - 1)
    most = jnp.zeros((1, 128), jnp.int32)
    for k in range(MEMBERS):
        gets = (counts + (MEMBERS - 1) - ((k - turned) & (MEMBERS - 1))) >> 4
        most = jnp.maximum(most, jnp.sum(gets, axis=0, keepdims=True))
    over[...] = jnp.broadcast_to((most > ROOM).astype(jnp.int32), (8, 128))


def column_fold(x, op):
    while x.shape[0] > 8:
        half = x.shape[0] // 16 * 8
        rest = x[2 * half :]
        x = op(x[:half], x[half : 2 * half])
        if rest.shape[0]:
            x = jnp.concatenate([op(x[:8], rest), x[8:]], axis=0) if half > 8 else op(x, rest)
    return x


LOWS = ((0, 256),)
HIGHS = ((256, 256), (512, SENT - 512))
PARTS = LOWS + HIGHS


def clear(state):
    col_best, col_mass, row_best, row_mass = state[:4]
    for ref in (col_best, row_best):
        ref[...] = jnp.full_like(ref, APART)
    for ref in (col_mass, row_mass):
        ref[...] = jnp.zeros_like(ref)


def names_of(block):
    part = block[0] if block[1] is None else block[1]
    return part[part.shape[0] - 16 :, :BLOCK].astype(jnp.float32)


def spell(block, place, state):
    clusters = names_of(block)[0:1]
    clusters = jnp.where(clusters > 0.0, clusters, -1.0)
    for t in range(0, BLOCK, 128):
        here = slice(t, t + 128)
        state[4][place, here, :] = jnp.broadcast_to(clusters[:, here], (128, 128)).T


def part_of(block, first, size):
    if first < LOW:
        return block[0][first : first + size, :]
    return block[1][first - LOW : first - LOW + size, :]


def square(rows, cols, place, c, r, state, own=False, downs=PARTS, parts=PARTS):
    col_best, col_mass, row_best, row_mass, spelt = state
    clusters = names_of(cols)[0:1]
    for i, tall in downs:
        for j, wide in parts:
            product = matmul(part_of(rows, i, tall), part_of(cols, j, wide), NT)
            down = slice(i, i + tall)
            tops = sums = None
            for t in range(0, wide, 128):
                size = min(128, wide - t)
                across = slice(j + t, j + t + size)
                match = spelt[place, down, :size] == clusters[:, across]
                if own and i == j:
                    match = match & (iota((tall, size), 0) != iota((tall, size), 1) + t)
                score = jnp.where(match, product[:, t : t + size], APART)
                soft = jnp.exp2((score - 1.0) * (sharpness * LOG2E))
                col_best[c, :, across] = jnp.maximum(
                    col_best[c, :, across], column_fold(score, jnp.maximum)
                )
                col_mass[c, :, across] = col_mass[c, :, across] + column_fold(soft, jnp.add)
                tops = score if tops is None else jnp.maximum(tops, score)
                sums = soft if sums is None else sums + soft
            if r is not None:
                size = tops.shape[1]
                row_best[r, down, :size] = jnp.maximum(row_best[r, down, :size], tops)
                row_mass[r, down, :size] = row_mass[r, down, :size] + sums


def settle(e, state):
    col_best, col_mass, row_best, row_mass = state[:4]
    best = jnp.max(col_best[e], axis=0, keepdims=True)
    mass = jnp.sum(col_mass[e], axis=0, keepdims=True)
    if e in ROW_BLOCKS:
        r = ROW_BLOCKS.index(e)
        tops, sums = [], []
        for t in range(0, BLOCK, 128):
            tops.append(jnp.max(row_best[r, t : t + 128, :].T, axis=0, keepdims=True))
            sums.append(jnp.sum(row_mass[r, t : t + 128, :].T, axis=0, keepdims=True))
        best = jnp.maximum(best, jnp.concatenate(tops, axis=1))
        mass = mass + jnp.concatenate(sums, axis=1)
    return best, mass


def store(blocks, best_in, mass_in, best_out, mass_out, state):
    if best_in is None:
        best_out[...] = jnp.full_like(best_out, APART)
        mass_out[...] = jnp.zeros_like(mass_out)
    else:
        best_out[...] = best_in[...]
        mass_out[...] = mass_in[...]
    for e in blocks:
        here = slice(e, e + 1)
        best, mass = settle(e, state)
        best_out[here, :] = jnp.maximum(best_out[here, :], best)
        mass_out[here, :] = mass_out[here, :] + mass


def early_kernel(b0l, b0h, b1l, b1h, b2l, b2h, best_out, mass_out, *state):
    b0, b1, b2 = (b0l, b0h), (b1l, b1h), (b2l, b2h)
    clear(state)
    for place, block in enumerate((b0, b1, b2)):
        spell(block, place, state)
    square(b0, b0, 0, 0, None, state, True)
    square(b1, b0, 1, 0, 0, state)
    square(b1, b2, 1, 2, 0, state)
    square(b2, b0, 2, 0, 1, state)
    store((0, 1, 2), None, None, best_out, mass_out, state)


def middle_kernel(
    b0l, b1l, b1h, b2l, b2h, b3l, b4l, low, high, best_in, mass_in, best_out, mass_out, *state
):
    b0, b1, b2, b3, b4 = (b0l, None), (b1l, b1h), (b2l, b2h), (b3l, None), (b4l, None)
    low, high = (low, None), (None, high)
    clear(state)
    for place, block in enumerate((b0, b1, b2, b4)):
        spell(block, place, state)
    square(b1, low, 1, 5, 0, state, parts=LOWS)
    square(b2, high, 2, 6, 1, state, parts=HIGHS)
    square(b1, high, 1, 6, 0, state, downs=LOWS, parts=HIGHS)
    square(b1, high, 1, 6, None, state, downs=HIGHS, parts=HIGHS)
    square(b2, low, 2, 5, 1, state, downs=HIGHS, parts=LOWS)
    square(b2, low, 2, 5, None, state, downs=LOWS, parts=LOWS)
    square(b0, b3, 0, 3, None, state, downs=LOWS, parts=LOWS)
    square(b1, b4, 1, 4, 0, state, parts=LOWS)
    square(b2, b3, 2, 3, 1, state, parts=LOWS)
    square(b4, b3, 3, 3, None, state, downs=LOWS, parts=LOWS)
    store((1, 2, 3, 4, 5, 6), best_in, mass_in, best_out, mass_out, state)


def late_kernel(
    b0h, b1l, b1h, b2l, b2h, b3l, b3h, b4l, b4h, low, high, best_in, mass_in, out, *state
):
    b0, b1, b2, b3, b4 = (None, b0h), (b1l, b1h), (b2l, b2h), (b3l, b3h), (b4l, b4h)
    low, high = (low, None), (None, high)
    clear(state)
    for place, block in enumerate((b0, b1, b2, b4)):
        spell(block, place, state)
    square(b0, b4, 0, 4, None, state, downs=HIGHS, parts=HIGHS)
    square(b1, b4, 1, 4, 0, state, parts=HIGHS)
    square(b2, b3, 2, 3, 1, state, parts=HIGHS)
    square(b4, b3, 3, 3, None, state, parts=HIGHS)
    square(b4, b3, 3, 3, None, state, downs=HIGHS, parts=LOWS)
    source_at = (iota((DEVICES, BLOCK), 0) + 1).astype(jnp.float32)
    line = iota((16, BLOCK), 0)
    back = []
    for e, block in enumerate((b0, b1, b2, b3, b4, low, high)):
        here = slice(e, e + 1)
        best, mass = jnp.maximum(best_in[here, :], -1.0), mass_in[here, :]
        if e in (1, 2, 3, 4):
            more, extra = settle(e, state)
            best = jnp.maximum(best, more)
            mass = mass + extra
        best = best + SHIFT
        names = names_of(block)
        if e == 5:
            names = jnp.where(iota(names.shape, 1) < LOW, names, 0.0)
        if e == 6:
            names = jnp.where(iota(names.shape, 1) >= LOW, names, 0.0)
        values = jnp.where((line & 1) == 0, best, mass)
        values = jnp.where((line >> 1).astype(jnp.float32) == names[2:3], values, 0.0)
        to = (source_at == names[1:2]).astype(jnp.bfloat16)
        back.append(joined(matmul(split(values), to, NT)))
    back.append(jnp.zeros((128 - 16 * len(back), DEVICES), jnp.float32))
    out[...] = jnp.concatenate(back, axis=0).T


def finish_kernel(arrived, places, best_out, mass_out):
    shape = (DEVICES, DEVICES)
    at, col = iota(shape, 0), iota(shape, 1)
    base, ay, az = at >> 4, (at >> 2) & 3, at & 3
    turned = (base & 1) == 1
    best = mass = None
    pieces = split(arrived[...].T)
    for e, (dy, dz) in enumerate(SPOTS):
        by = (ay + jnp.where(turned, dz, (-dy) & 3)) & 3
        bz = (az + jnp.where(turned, dy, (-dz) & 3)) & 3
        move = (col == base * MEMBERS + by * 4 + bz).astype(jnp.bfloat16)
        part = jnp.concatenate(
            [pieces[128 * p + 16 * e : 128 * p + 16 * e + 16] for p in range(3)], axis=0
        )
        moved = joined(matmul(part, move, NT))
        best = moved if best is None else jnp.maximum(best, moved)
        mass = moved if mass is None else mass + moved
    merged = jnp.where((iota((16, DEVICES), 0) & 1) == 0, best, mass)
    holder = (iota((DEVICES, ROWS), 0) == places[0:1, :]).astype(jnp.bfloat16)
    picked = joined(matmul(split(merged), holder, NN))
    line = iota((16, ROWS), 0)
    turn = places[1:2, :]
    best = jnp.sum(jnp.where(line == 2 * turn, picked, 0.0), axis=0, keepdims=True)
    best_out[...] = best - SHIFT
    mass = jnp.sum(jnp.where(line == 2 * turn + 1, picked, 0.0), axis=0, keepdims=True)
    mass_out[...] = jnp.log1p(mass)


def call(kernel, out_shape, scratch=(), flops=0, name=None):
    return pl.pallas_call(
        kernel,
        out_shape=out_shape,
        scratch_shapes=scratch,
        compiler_params=pltpu.CompilerParams(vmem_limit_bytes=VMEM_LIMIT),
        cost_estimate=pl.CostEstimate(flops=flops, bytes_accessed=8_000_000, transcendentals=0),
        name=name,
    )


def hop(dy, dz):
    pairs = []
    for g in range(GROUPS):
        up, along = (-dz, -dy) if g & 1 else (dy, dz)
        for y in range(4):
            for z in range(4):
                source = ((y + up) % 4) * 4 + (z + along) % 4
                pairs.append((g * MEMBERS + source, g * MEMBERS + y * 4 + z))
    return pairs


def from_spot(x, dy, dz):
    return lax.ppermute(x, AXES, hop(dy, dz))


def fast(embeddings, labels, cluster_slot):
    f32, bf16, i32 = jnp.float32, jnp.bfloat16, jnp.int32
    shape = jax.ShapeDtypeStruct
    spread, places = call(
        prelude_kernel,
        (shape((HELD, WIDE), bf16), shape((8, ROWS), i32)),
        flops=3_000_000_000,
        name="prelude",
    )(labels.reshape(1, ROWS), cluster_slot.reshape(1, ROWS), embeddings)
    arrived = lax.all_to_all(spread, AXES, split_axis=0, concat_axis=0, tiled=True)
    b0l, position, names = call(
        pack_low_kernel,
        (shape((LOW_SENT, FEAT), bf16), shape((8, HELD), i32), shape((8, HELD), f32)),
        flops=2_000_000_000,
        name="pack_low",
    )(arrived)
    b0h = call(
        pack_high_kernel, shape((HIGH_SENT, FEAT), bf16), flops=1_000_000_000, name="pack_high"
    )(arrived, b0l, position, names)
    b1l = from_spot(b0l, 1, 0)
    b2l = from_spot(b0l, 0, 1)
    b1h = from_spot(b0h, 1, 0)
    b2h = from_spot(b0h, 0, 1)
    high, b1l, b2l = lax.optimization_barrier((b0h, b1l, b2l))
    high = from_spot(high, 3, 0)
    b3l = from_spot(b1l, 1, 0)
    b4l = from_spot(b2l, 0, 1)
    low, b1h, b2h = lax.optimization_barrier((b0l, b1h, b2h))
    over = call(over_kernel, shape((8, 128), i32), flops=10_000_000, name="over")(arrived)
    b3h = from_spot(b1h, 1, 0)
    b4h = from_spot(b2h, 0, 1)
    low = from_spot(low, 0, 3)

    def state(places):
        return (
            pltpu.VMEM((7, 8, BLOCK), f32),
            pltpu.VMEM((7, 8, BLOCK), f32),
            pltpu.VMEM((2, BLOCK, 128), f32),
            pltpu.VMEM((2, BLOCK, 128), f32),
            pltpu.VMEM((places, BLOCK, 128), f32),
        )

    stats = (shape((8, BLOCK), f32), shape((8, BLOCK), f32))
    best, mass = call(
        early_kernel, stats, scratch=state(3), flops=6_000_000_000, name="early"
    )(b0l, b0h, b1l, b1h, b2l, b2h)
    best, mass = call(
        middle_kernel, stats, scratch=state(4), flops=1_500_000_000, name="middle"
    )(b0l, b1l, b1h, b2l, b2h, b3l, b4l, low, high, best, mass)
    message = call(
        late_kernel,
        shape((DEVICES, 128), f32),
        scratch=state(4),
        flops=3_000_000_000,
        name="late",
    )(b0h, b1l, b1h, b2l, b2h, b3l, b3h, b4l, b4h, low, high, best, mass)
    answer = lax.all_to_all(message, AXES, split_axis=0, concat_axis=0, tiled=True)
    best, mass = call(
        finish_kernel,
        (shape((1, ROWS), f32), shape((1, ROWS), f32)),
        flops=ROWS * ROWS * 128,
        name="finish",
    )(answer, places)
    return (best.reshape(ROWS), mass.reshape(ROWS)), jnp.max(over)


def general(embeddings, labels, cluster_slot):
    groups = lax.axis_size("grp")
    members = lax.axis_size("blk")
    row_count, feature_count = embeddings.shape
    capacity = row_count // 4
    held = groups * capacity
    widened = embeddings.astype(jnp.float32)
    units = (
        widened * lax.rsqrt(jnp.sum(widened * widened, axis=1, keepdims=True) + epsilon)
    ).astype(jnp.bfloat16)
    slot_ids = cluster_slot[labels]
    owner_group = slot_ids // (cluster_slot.shape[0] // groups)
    owner_onehot = (owner_group[:, None] == jnp.arange(groups, dtype=jnp.int32)[None, :]).astype(
        jnp.int32
    )
    earlier = jnp.cumsum(owner_onehot, axis=0) - owner_onehot
    send_place = owner_group * capacity + jnp.sum(earlier * owner_onehot, axis=1)
    outgoing = jnp.zeros((held, feature_count), jnp.bfloat16).at[send_place].set(units)
    outgoing_slots = jnp.full((held,), -1, jnp.int32).at[send_place].set(slot_ids)
    rows = lax.all_to_all(outgoing, "grp", split_axis=0, concat_axis=0, tiled=True)
    slots = lax.all_to_all(outgoing_slots, "grp", split_axis=0, concat_axis=0, tiled=True)
    ring = [(i, (i + 1) % members) for i in range(members)]
    local = jnp.arange(held, dtype=jnp.int32)
    place = lax.axis_index("blk")
    own_ids = place * held + local

    def step(turn, carry):
        key_rows, key_slots, best, mass = carry
        scores = jnp.einsum("qd,kd->qk", rows, key_rows, preferred_element_type=jnp.float32)
        matched = (slots[:, None] == key_slots[None, :]) & (key_slots[None, :] >= 0)
        owner = (place - turn) & (members - 1)
        matched = matched & (own_ids[:, None] != (owner * held + local)[None, :])
        best = jnp.maximum(best, jnp.max(jnp.where(matched, scores, -1.0), axis=1))
        mass = mass + jnp.sum(
            jnp.where(matched, jnp.exp(sharpness * (scores - 1.0)), 0.0), axis=1
        )
        key_rows = lax.ppermute(key_rows, "blk", ring)
        key_slots = lax.ppermute(key_slots, "blk", ring)
        return key_rows, key_slots, best, mass

    start = (
        rows,
        slots,
        jnp.full((held,), -1.0, jnp.float32),
        jnp.zeros((held,), jnp.float32),
    )
    _, _, best, mass = lax.fori_loop(0, members, step, start)
    best = lax.all_to_all(best, "grp", split_axis=0, concat_axis=0, tiled=True)
    mass = lax.all_to_all(mass, "grp", split_axis=0, concat_axis=0, tiled=True)
    return (best[send_place], jnp.log1p(mass[send_place]))


def body(embeddings, labels, cluster_slot):
    result, over = fast(embeddings, labels, cluster_slot)
    return lax.cond(
        over > 0, lambda: general(embeddings, labels, cluster_slot), lambda: result
    )


def solution(mesh):
    placed = (P(AXES, None), P(AXES), P())
    return jax.shard_map(
        body,
        mesh=mesh,
        in_specs=placed,
        out_specs=(P(AXES), P(AXES)),
        check_vma=False,
    )
```

```python
import jax
import jax.numpy as jnp
from jax import lax
from jax.experimental import pallas as pl
from jax.experimental.pallas import tpu as pltpu
from jax.sharding import PartitionSpec as P

epsilon = 1e-06
sharpness = 8.0

ROWS = 512
FEAT = 768
WIDE = 896
GROUPS = 8
MEMBERS = 16
DEVICES = GROUPS * MEMBERS
SHARE = 8
HELD = DEVICES * SHARE
SENT = 608
ROOM = SENT - 16
BLOCK = 640
APART = -64.0
LOG2E = 1.4426950408889634
AXES = ("grp", "blk")
VMEM_LIMIT = 24 * 1024 * 1024

SPOTS = ((0, 0), (1, 0), (0, 1), (2, 0), (0, 2), (0, 3), (3, 0))
LOW = 256
LOW_SENT = LOW + 16
HIGH_SENT = SENT - LOW
ROW_BLOCKS = (1, 2)
SHIFT = 2.0


def iota(shape, axis):
    return lax.broadcasted_iota(jnp.int32, shape, axis)


def matmul(a, b, dims, exact=False):
    return lax.dot_general(
        a,
        b,
        (dims, ((), ())),
        precision=lax.Precision.HIGHEST if exact else None,
        preferred_element_type=jnp.float32,
    )


NN = ((1,), (0,))
NT = ((1,), (1,))


def split(x):
    high = x.astype(jnp.bfloat16)
    rest = x - high.astype(jnp.float32)
    middle = rest.astype(jnp.bfloat16)
    low = (rest - middle.astype(jnp.float32)).astype(jnp.bfloat16)
    return jnp.concatenate([high, middle, low], axis=0)


def joined(x):
    size = x.shape[0] // 3
    return x[:size] + x[size : 2 * size] + x[2 * size :]


def prelude_kernel(labels, slots, rows, spread, places):
    lab = labels[...]
    table = slots[...]
    by_cluster = (iota((ROWS, ROWS), 0) == lab).astype(jnp.bfloat16)
    sub = iota((8, ROWS), 0)
    parts = jnp.where(sub == 0, table >> 6, jnp.where(sub == 1, table & 63, 0)).astype(jnp.bfloat16)
    found = matmul(parts, by_cluster, NN)
    group = found[0:1].astype(jnp.int32)
    in_group = sub == group
    before = (iota((ROWS, ROWS), 0) < iota((ROWS, ROWS), 1)).astype(jnp.bfloat16)
    counts = matmul(in_group.astype(jnp.bfloat16), before, NN)
    rank = jnp.sum(jnp.where(in_group, counts, 0.0), axis=0, keepdims=True).astype(jnp.int32)
    holder = group * MEMBERS + ((rank + lax.axis_index("blk")) & (MEMBERS - 1))
    turn = rank >> 4
    places[...] = jnp.where(sub == 0, holder, turn)

    wide = rows[...].astype(jnp.float32)
    norm = lax.rsqrt(jnp.sum(wide * wide, axis=1, keepdims=True) + epsilon)
    units = (wide * norm).astype(jnp.bfloat16)
    lanes = iota((128, ROWS), 0)
    marks = jnp.where(lanes == 0, found[1:2] + 1.0, 0.0).astype(jnp.bfloat16)
    goal = holder * SHARE + turn
    totals = matmul(
        jnp.ones((8, ROWS), jnp.bfloat16), (lanes - 64 == group).astype(jnp.bfloat16), NT
    )
    totals = jnp.where((iota((ROWS, 128), 0) & (SHARE - 1)) == 0, totals[0:1], 0.0)
    for t in range(0, HELD, ROWS):
        here = pl.ds(t, ROWS)
        pick = (iota((ROWS, ROWS), 0) + t == goal).astype(jnp.bfloat16)
        spread[here, :FEAT] = matmul(pick, units, NN).astype(jnp.bfloat16)
        spread[here, FEAT:] = (matmul(pick, marks, NT) + totals).astype(jnp.bfloat16)


def pack_low_kernel(arrived, low, position_out, names_out):
    tails = arrived[:, FEAT:]
    at, line = iota((8, HELD), 1), iota((8, HELD), 0)
    clusters = matmul((iota((8, 128), 1) == 0).astype(jnp.bfloat16), tails, NT)
    held = clusters > 0.0
    before = (iota((HELD, HELD), 0) < iota((HELD, HELD), 1)).astype(jnp.bfloat16)
    position = matmul(held.astype(jnp.bfloat16), before, NN)
    position = jnp.where(held, position, -1.0).astype(jnp.int32)
    position_out[...] = position
    names = jnp.where(line == 1, (at >> 3) + 1, jnp.where(line == 2, at & 7, 0))
    names = jnp.where(line == 0, clusters, names.astype(jnp.float32))
    names_out[...] = names
    pick = (iota((LOW, HELD), 0) == position[0:1]).astype(jnp.bfloat16)
    low[:LOW, :] = matmul(pick, arrived[:, :FEAT], NN).astype(jnp.bfloat16)
    named = matmul(names.astype(jnp.bfloat16), pick, NT)
    named = jnp.concatenate([named, jnp.zeros((8, FEAT - LOW), jnp.float32)], axis=1)
    low[LOW:, :] = jnp.concatenate([named, jnp.zeros_like(named)], axis=0).astype(jnp.bfloat16)


def pack_high_kernel(arrived, low, position, names, high):
    pick = (iota((BLOCK - LOW, HELD), 0) + LOW == position[0:1, :]).astype(jnp.bfloat16)
    high[: ROOM - LOW, :] = matmul(pick[: ROOM - LOW], arrived[:, :FEAT], NN).astype(jnp.bfloat16)
    named = matmul(names[...].astype(jnp.bfloat16), pick, NT)
    named = jnp.concatenate([named, jnp.zeros_like(named)], axis=0).astype(jnp.bfloat16)
    high[ROOM - LOW :, :LOW] = low[LOW:, :LOW]
    high[ROOM - LOW :, LOW:BLOCK] = named
    high[ROOM - LOW :, BLOCK:] = jnp.zeros((16, FEAT - BLOCK), jnp.bfloat16)


def over_kernel(arrived, over):
    one = ((iota((128, HELD), 0) * SHARE) == iota((128, HELD), 1)).astype(jnp.bfloat16)
    counts = matmul(one, arrived[:, FEAT:], NN).astype(jnp.int32)
    counts = jnp.where(iota((128, 128), 1) >= 64, counts, 0)
    turned = iota((128, 128), 0) & (MEMBERS - 1)
    most = jnp.zeros((1, 128), jnp.int32)
    for k in range(MEMBERS):
        gets = (counts + (MEMBERS - 1) - ((k - turned) & (MEMBERS - 1))) >> 4
        most = jnp.maximum(most, jnp.sum(gets, axis=0, keepdims=True))
    over[...] = jnp.broadcast_to((most > ROOM).astype(jnp.int32), (8, 128))


def column_fold(x, op):
    while x.shape[0] > 8:
        half = x.shape[0] // 16 * 8
        rest = x[2 * half :]
        x = op(x[:half], x[half : 2 * half])
        if rest.shape[0]:
            x = jnp.concatenate([op(x[:8], rest), x[8:]], axis=0) if half > 8 else op(x, rest)
    return x


LOWS = ((0, 256),)
HIGHS = ((256, 256), (512, SENT - 512))
PARTS = LOWS + HIGHS


def clear(state):
    col_best, col_mass, row_best, row_mass = state[:4]
    for ref in (col_best, row_best):
        ref[...] = jnp.full_like(ref, APART)
    for ref in (col_mass, row_mass):
        ref[...] = jnp.zeros_like(ref)


def names_of(block):
    part = block[0] if block[1] is None else block[1]
    return part[part.shape[0] - 16 :, :BLOCK].astype(jnp.float32)


def spell(block, place, state):
    clusters = names_of(block)[0:1]
    clusters = jnp.where(clusters > 0.0, clusters, -1.0)
    for t in range(0, BLOCK, 128):
        here = slice(t, t + 128)
        state[4][place, here, :] = jnp.broadcast_to(clusters[:, here], (128, 128)).T


def part_of(block, first, size):
    if first < LOW:
        return block[0][first : first + size, :]
    return block[1][first - LOW : first - LOW + size, :]


def square(rows, cols, place, c, r, state, own=False, downs=PARTS, parts=PARTS):
    col_best, col_mass, row_best, row_mass, spelt = state
    clusters = names_of(cols)[0:1]
    for i, tall in downs:
        for j, wide in parts:
            product = matmul(part_of(rows, i, tall), part_of(cols, j, wide), NT)
            down = slice(i, i + tall)
            tops = sums = None
            for t in range(0, wide, 128):
                size = min(128, wide - t)
                across = slice(j + t, j + t + size)
                match = spelt[place, down, :size] == clusters[:, across]
                if own and i == j:
                    match = match & (iota((tall, size), 0) != iota((tall, size), 1) + t)
                score = jnp.where(match, product[:, t : t + size], APART)
                soft = jnp.exp2((score - 1.0) * (sharpness * LOG2E))
                col_best[c, :, across] = jnp.maximum(
                    col_best[c, :, across], column_fold(score, jnp.maximum)
                )
                col_mass[c, :, across] = col_mass[c, :, across] + column_fold(soft, jnp.add)
                tops = score if tops is None else jnp.maximum(tops, score)
                sums = soft if sums is None else sums + soft
            if r is not None:
                size = tops.shape[1]
                row_best[r, down, :size] = jnp.maximum(row_best[r, down, :size], tops)
                row_mass[r, down, :size] = row_mass[r, down, :size] + sums


def settle(e, state):
    col_best, col_mass, row_best, row_mass = state[:4]
    best = jnp.max(col_best[e], axis=0, keepdims=True)
    mass = jnp.sum(col_mass[e], axis=0, keepdims=True)
    if e in ROW_BLOCKS:
        r = ROW_BLOCKS.index(e)
        tops, sums = [], []
        for t in range(0, BLOCK, 128):
            tops.append(jnp.max(row_best[r, t : t + 128, :].T, axis=0, keepdims=True))
            sums.append(jnp.sum(row_mass[r, t : t + 128, :].T, axis=0, keepdims=True))
        best = jnp.maximum(best, jnp.concatenate(tops, axis=1))
        mass = mass + jnp.concatenate(sums, axis=1)
    return best, mass


def store(blocks, best_in, mass_in, best_out, mass_out, state):
    if best_in is None:
        best_out[...] = jnp.full_like(best_out, APART)
        mass_out[...] = jnp.zeros_like(mass_out)
    else:
        best_out[...] = best_in[...]
        mass_out[...] = mass_in[...]
    for e in blocks:
        here = slice(e, e + 1)
        best, mass = settle(e, state)
        best_out[here, :] = jnp.maximum(best_out[here, :], best)
        mass_out[here, :] = mass_out[here, :] + mass


def early_kernel(b0l, b0h, b1l, b1h, b2l, b2h, best_out, mass_out, *state):
    b0, b1, b2 = (b0l, b0h), (b1l, b1h), (b2l, b2h)
    clear(state)
    for place, block in enumerate((b0, b1, b2)):
        spell(block, place, state)
    square(b0, b0, 0, 0, None, state, True)
    square(b1, b0, 1, 0, 0, state)
    square(b1, b2, 1, 2, 0, state)
    square(b2, b0, 2, 0, 1, state)
    store((0, 1, 2), None, None, best_out, mass_out, state)


def middle_kernel(
    b0l, b1l, b1h, b2l, b2h, b3l, b4l, low, high, best_in, mass_in, best_out, mass_out, *state
):
    b0, b1, b2, b3, b4 = (b0l, None), (b1l, b1h), (b2l, b2h), (b3l, None), (b4l, None)
    low, high = (low, None), (None, high)
    clear(state)
    for place, block in enumerate((b0, b1, b2, b4)):
        spell(block, place, state)
    square(b1, low, 1, 5, 0, state, parts=LOWS)
    square(b2, high, 2, 6, 1, state, parts=HIGHS)
    square(b1, high, 1, 6, 0, state, downs=LOWS, parts=HIGHS)
    square(b1, high, 1, 6, None, state, downs=HIGHS, parts=HIGHS)
    square(b2, low, 2, 5, 1, state, downs=HIGHS, parts=LOWS)
    square(b2, low, 2, 5, None, state, downs=LOWS, parts=LOWS)
    square(b0, b3, 0, 3, None, state, downs=LOWS, parts=LOWS)
    square(b1, b4, 1, 4, 0, state, parts=LOWS)
    square(b2, b3, 2, 3, 1, state, parts=LOWS)
    square(b4, b3, 3, 3, None, state, downs=LOWS, parts=LOWS)
    store((1, 2, 3, 4, 5, 6), best_in, mass_in, best_out, mass_out, state)


def late_kernel(
    b0h, b1l, b1h, b2l, b2h, b3l, b3h, b4l, b4h, low, high, best_in, mass_in, out, *state
):
    b0, b1, b2, b3, b4 = (None, b0h), (b1l, b1h), (b2l, b2h), (b3l, b3h), (b4l, b4h)
    low, high = (low, None), (None, high)
    clear(state)
    for place, block in enumerate((b0, b1, b2, b4)):
        spell(block, place, state)
    square(b0, b4, 0, 4, None, state, downs=HIGHS, parts=HIGHS)
    square(b1, b4, 1, 4, 0, state, parts=HIGHS)
    square(b2, b3, 2, 3, 1, state, parts=HIGHS)
    square(b4, b3, 3, 3, None, state, parts=HIGHS)
    square(b4, b3, 3, 3, None, state, downs=HIGHS, parts=LOWS)
    source_at = (iota((DEVICES, BLOCK), 0) + 1).astype(jnp.float32)
    line = iota((16, BLOCK), 0)
    back = []
    for e, block in enumerate((b0, b1, b2, b3, b4, low, high)):
        here = slice(e, e + 1)
        best, mass = jnp.maximum(best_in[here, :], -1.0), mass_in[here, :]
        if e in (1, 2, 3, 4):
            more, extra = settle(e, state)
            best = jnp.maximum(best, more)
            mass = mass + extra
        best = best + SHIFT
        names = names_of(block)
        if e == 5:
            names = jnp.where(iota(names.shape, 1) < LOW, names, 0.0)
        if e == 6:
            names = jnp.where(iota(names.shape, 1) >= LOW, names, 0.0)
        values = jnp.where((line & 1) == 0, best, mass)
        values = jnp.where((line >> 1).astype(jnp.float32) == names[2:3], values, 0.0)
        to = (source_at == names[1:2]).astype(jnp.bfloat16)
        back.append(joined(matmul(split(values), to, NT)))
    back.append(jnp.zeros((128 - 16 * len(back), DEVICES), jnp.float32))
    out[...] = jnp.concatenate(back, axis=0).T


def finish_kernel(arrived, places, best_out, mass_out):
    shape = (DEVICES, DEVICES)
    at, col = iota(shape, 0), iota(shape, 1)
    base, ay, az = at >> 4, (at >> 2) & 3, at & 3
    turned = (base & 1) == 1
    best = mass = None
    pieces = split(arrived[...].T)
    for e, (dy, dz) in enumerate(SPOTS):
        by = (ay + jnp.where(turned, dz, (-dy) & 3)) & 3
        bz = (az + jnp.where(turned, dy, (-dz) & 3)) & 3
        move = (col == base * MEMBERS + by * 4 + bz).astype(jnp.bfloat16)
        part = jnp.concatenate(
            [pieces[128 * p + 16 * e : 128 * p + 16 * e + 16] for p in range(3)], axis=0
        )
        moved = joined(matmul(part, move, NT))
        best = moved if best is None else jnp.maximum(best, moved)
        mass = moved if mass is None else mass + moved
    merged = jnp.where((iota((16, DEVICES), 0) & 1) == 0, best, mass)
    holder = (iota((DEVICES, ROWS), 0) == places[0:1, :]).astype(jnp.bfloat16)
    picked = joined(matmul(split(merged), holder, NN))
    line = iota((16, ROWS), 0)
    turn = places[1:2, :]
    best = jnp.sum(jnp.where(line == 2 * turn, picked, 0.0), axis=0, keepdims=True)
    best_out[...] = best - SHIFT
    mass = jnp.sum(jnp.where(line == 2 * turn + 1, picked, 0.0), axis=0, keepdims=True)
    mass_out[...] = jnp.log1p(mass)


def call(kernel, out_shape, scratch=(), flops=0, name=None):
    return pl.pallas_call(
        kernel,
        out_shape=out_shape,
        scratch_shapes=scratch,
        compiler_params=pltpu.CompilerParams(vmem_limit_bytes=VMEM_LIMIT),
        cost_estimate=pl.CostEstimate(flops=flops, bytes_accessed=8_000_000, transcendentals=0),
        name=name,
    )


def hop(dy, dz):
    pairs = []
    for g in range(GROUPS):
        up, along = (-dz, -dy) if g & 1 else (dy, dz)
        for y in range(4):
            for z in range(4):
                source = ((y + up) % 4) * 4 + (z + along) % 4
                pairs.append((g * MEMBERS + source, g * MEMBERS + y * 4 + z))
    return pairs


def from_spot(x, dy, dz):
    return lax.ppermute(x, AXES, hop(dy, dz))


def fast(embeddings, labels, cluster_slot):
    f32, bf16, i32 = jnp.float32, jnp.bfloat16, jnp.int32
    shape = jax.ShapeDtypeStruct
    spread, places = call(
        prelude_kernel,
        (shape((HELD, WIDE), bf16), shape((8, ROWS), i32)),
        flops=3_000_000_000,
        name="prelude",
    )(labels.reshape(1, ROWS), cluster_slot.reshape(1, ROWS), embeddings)
    arrived = lax.all_to_all(spread, AXES, split_axis=0, concat_axis=0, tiled=True)
    b0l, position, names = call(
        pack_low_kernel,
        (shape((LOW_SENT, FEAT), bf16), shape((8, HELD), i32), shape((8, HELD), f32)),
        flops=2_000_000_000,
        name="pack_low",
    )(arrived)
    b0h = call(
        pack_high_kernel, shape((HIGH_SENT, FEAT), bf16), flops=1_000_000_000, name="pack_high"
    )(arrived, b0l, position, names)
    b1l = from_spot(b0l, 1, 0)
    b2l = from_spot(b0l, 0, 1)
    b1h = from_spot(b0h, 1, 0)
    b2h = from_spot(b0h, 0, 1)
    high, b1l, b2l = lax.optimization_barrier((b0h, b1l, b2l))
    high = from_spot(high, 3, 0)
    b3l = from_spot(b1l, 1, 0)
    b4l = from_spot(b2l, 0, 1)
    low, b1h, b2h = lax.optimization_barrier((b0l, b1h, b2h))
    over = call(over_kernel, shape((8, 128), i32), flops=10_000_000, name="over")(arrived)
    b4h = from_spot(b2h, 0, 1)
    b3h = from_spot(b1h, 1, 0)
    low = from_spot(low, 0, 3)

    def state(places):
        return (
            pltpu.VMEM((7, 8, BLOCK), f32),
            pltpu.VMEM((7, 8, BLOCK), f32),
            pltpu.VMEM((2, BLOCK, 128), f32),
            pltpu.VMEM((2, BLOCK, 128), f32),
            pltpu.VMEM((places, BLOCK, 128), f32),
        )

    stats = (shape((8, BLOCK), f32), shape((8, BLOCK), f32))
    best, mass = call(
        early_kernel, stats, scratch=state(3), flops=6_000_000_000, name="early"
    )(b0l, b0h, b1l, b1h, b2l, b2h)
    best, mass = call(
        middle_kernel, stats, scratch=state(4), flops=1_500_000_000, name="middle"
    )(b0l, b1l, b1h, b2l, b2h, b3l, b4l, low, high, best, mass)
    message = call(
        late_kernel,
        shape((DEVICES, 128), f32),
        scratch=state(4),
        flops=3_000_000_000,
        name="late",
    )(b0h, b1l, b1h, b2l, b2h, b3l, b3h, b4l, b4h, low, high, best, mass)
    answer = lax.all_to_all(message, AXES, split_axis=0, concat_axis=0, tiled=True)
    best, mass = call(
        finish_kernel,
        (shape((1, ROWS), f32), shape((1, ROWS), f32)),
        flops=ROWS * ROWS * 128,
        name="finish",
    )(answer, places)
    return (best.reshape(ROWS), mass.reshape(ROWS)), jnp.max(over)


def general(embeddings, labels, cluster_slot):
    groups = lax.axis_size("grp")
    members = lax.axis_size("blk")
    row_count, feature_count = embeddings.shape
    capacity = row_count // 4
    held = groups * capacity
    widened = embeddings.astype(jnp.float32)
    units = (
        widened * lax.rsqrt(jnp.sum(widened * widened, axis=1, keepdims=True) + epsilon)
    ).astype(jnp.bfloat16)
    slot_ids = cluster_slot[labels]
    owner_group = slot_ids // (cluster_slot.shape[0] // groups)
    owner_onehot = (owner_group[:, None] == jnp.arange(groups, dtype=jnp.int32)[None, :]).astype(
        jnp.int32
    )
    earlier = jnp.cumsum(owner_onehot, axis=0) - owner_onehot
    send_place = owner_group * capacity + jnp.sum(earlier * owner_onehot, axis=1)
    outgoing = jnp.zeros((held, feature_count), jnp.bfloat16).at[send_place].set(units)
    outgoing_slots = jnp.full((held,), -1, jnp.int32).at[send_place].set(slot_ids)
    rows = lax.all_to_all(outgoing, "grp", split_axis=0, concat_axis=0, tiled=True)
    slots = lax.all_to_all(outgoing_slots, "grp", split_axis=0, concat_axis=0, tiled=True)
    ring = [(i, (i + 1) % members) for i in range(members)]
    local = jnp.arange(held, dtype=jnp.int32)
    place = lax.axis_index("blk")
    own_ids = place * held + local

    def step(turn, carry):
        key_rows, key_slots, best, mass = carry
        scores = jnp.einsum("qd,kd->qk", rows, key_rows, preferred_element_type=jnp.float32)
        matched = (slots[:, None] == key_slots[None, :]) & (key_slots[None, :] >= 0)
        owner = (place - turn) & (members - 1)
        matched = matched & (own_ids[:, None] != (owner * held + local)[None, :])
        best = jnp.maximum(best, jnp.max(jnp.where(matched, scores, -1.0), axis=1))
        mass = mass + jnp.sum(
            jnp.where(matched, jnp.exp(sharpness * (scores - 1.0)), 0.0), axis=1
        )
        key_rows = lax.ppermute(key_rows, "blk", ring)
        key_slots = lax.ppermute(key_slots, "blk", ring)
        return key_rows, key_slots, best, mass

    start = (
        rows,
        slots,
        jnp.full((held,), -1.0, jnp.float32),
        jnp.zeros((held,), jnp.float32),
    )
    _, _, best, mass = lax.fori_loop(0, members, step, start)
    best = lax.all_to_all(best, "grp", split_axis=0, concat_axis=0, tiled=True)
    mass = lax.all_to_all(mass, "grp", split_axis=0, concat_axis=0, tiled=True)
    return (best[send_place], jnp.log1p(mass[send_place]))


def body(embeddings, labels, cluster_slot):
    result, over = fast(embeddings, labels, cluster_slot)
    return lax.cond(
        over > 0, lambda: general(embeddings, labels, cluster_slot), lambda: result
    )


def solution(mesh):
    placed = (P(AXES, None), P(AXES), P())
    return jax.shard_map(
        body,
        mesh=mesh,
        in_specs=placed,
        out_specs=(P(AXES), P(AXES)),
        check_vma=False,
    )
```

```python
import jax
import jax.numpy as jnp
from jax import lax
from jax.experimental import pallas as pl
from jax.experimental.pallas import tpu as pltpu
from jax.sharding import PartitionSpec as P

epsilon = 1e-06
sharpness = 8.0

ROWS = 512
FEAT = 768
WIDE = 896
GROUPS = 8
MEMBERS = 16
DEVICES = GROUPS * MEMBERS
SHARE = 8
HELD = DEVICES * SHARE
SENT = 608
ROOM = SENT - 16
BLOCK = 640
APART = -64.0
LOG2E = 1.4426950408889634
AXES = ("grp", "blk")
VMEM_LIMIT = 24 * 1024 * 1024

SPOTS = ((0, 0), (1, 0), (0, 1), (2, 0), (0, 2), (0, 3), (3, 0))
LOW = 256
LOW_SENT = LOW + 16
HIGH_SENT = SENT - LOW
ROW_BLOCKS = (1, 2)
SHIFT = 2.0


def iota(shape, axis):
    return lax.broadcasted_iota(jnp.int32, shape, axis)


def matmul(a, b, dims, exact=False):
    return lax.dot_general(
        a,
        b,
        (dims, ((), ())),
        precision=lax.Precision.HIGHEST if exact else None,
        preferred_element_type=jnp.float32,
    )


NN = ((1,), (0,))
NT = ((1,), (1,))


def split(x):
    high = x.astype(jnp.bfloat16)
    rest = x - high.astype(jnp.float32)
    middle = rest.astype(jnp.bfloat16)
    low = (rest - middle.astype(jnp.float32)).astype(jnp.bfloat16)
    return jnp.concatenate([high, middle, low], axis=0)


def joined(x):
    size = x.shape[0] // 3
    return x[:size] + x[size : 2 * size] + x[2 * size :]


def prelude_kernel(labels, slots, rows, spread, places):
    lab = labels[...]
    table = slots[...]
    by_cluster = (iota((ROWS, ROWS), 0) == lab).astype(jnp.bfloat16)
    sub = iota((8, ROWS), 0)
    parts = jnp.where(sub == 0, table >> 6, jnp.where(sub == 1, table & 63, 0)).astype(jnp.bfloat16)
    found = matmul(parts, by_cluster, NN)
    group = found[0:1].astype(jnp.int32)
    in_group = sub == group
    before = (iota((ROWS, ROWS), 0) < iota((ROWS, ROWS), 1)).astype(jnp.bfloat16)
    counts = matmul(in_group.astype(jnp.bfloat16), before, NN)
    rank = jnp.sum(jnp.where(in_group, counts, 0.0), axis=0, keepdims=True).astype(jnp.int32)
    holder = group * MEMBERS + ((rank + lax.axis_index("blk")) & (MEMBERS - 1))
    turn = rank >> 4
    places[...] = jnp.where(sub == 0, holder, turn)

    wide = rows[...].astype(jnp.float32)
    norm = lax.rsqrt(jnp.sum(wide * wide, axis=1, keepdims=True) + epsilon)
    units = (wide * norm).astype(jnp.bfloat16)
    lanes = iota((128, ROWS), 0)
    marks = jnp.where(lanes == 0, found[1:2] + 1.0, 0.0).astype(jnp.bfloat16)
    goal = holder * SHARE + turn
    totals = matmul(
        jnp.ones((8, ROWS), jnp.bfloat16), (lanes - 64 == group).astype(jnp.bfloat16), NT
    )
    totals = jnp.where((iota((ROWS, 128), 0) & (SHARE - 1)) == 0, totals[0:1], 0.0)
    for t in range(0, HELD, ROWS):
        here = pl.ds(t, ROWS)
        pick = (iota((ROWS, ROWS), 0) + t == goal).astype(jnp.bfloat16)
        spread[here, :FEAT] = matmul(pick, units, NN).astype(jnp.bfloat16)
        spread[here, FEAT:] = (matmul(pick, marks, NT) + totals).astype(jnp.bfloat16)


def pack_low_kernel(arrived, low, position_out, names_out):
    tails = arrived[:, FEAT:]
    at, line = iota((8, HELD), 1), iota((8, HELD), 0)
    clusters = matmul((iota((8, 128), 1) == 0).astype(jnp.bfloat16), tails, NT)
    held = clusters > 0.0
    before = (iota((HELD, HELD), 0) < iota((HELD, HELD), 1)).astype(jnp.bfloat16)
    position = matmul(held.astype(jnp.bfloat16), before, NN)
    position = jnp.where(held, position, -1.0).astype(jnp.int32)
    position_out[...] = position
    names = jnp.where(line == 1, (at >> 3) + 1, jnp.where(line == 2, at & 7, 0))
    names = jnp.where(line == 0, clusters, names.astype(jnp.float32))
    names_out[...] = names
    pick = (iota((LOW, HELD), 0) == position[0:1]).astype(jnp.bfloat16)
    low[:LOW, :] = matmul(pick, arrived[:, :FEAT], NN).astype(jnp.bfloat16)
    named = matmul(names.astype(jnp.bfloat16), pick, NT)
    named = jnp.concatenate([named, jnp.zeros((8, FEAT - LOW), jnp.float32)], axis=1)
    low[LOW:, :] = jnp.concatenate([named, jnp.zeros_like(named)], axis=0).astype(jnp.bfloat16)


def pack_high_kernel(arrived, low, position, names, high):
    pick = (iota((BLOCK - LOW, HELD), 0) + LOW == position[0:1, :]).astype(jnp.bfloat16)
    high[: ROOM - LOW, :] = matmul(pick[: ROOM - LOW], arrived[:, :FEAT], NN).astype(jnp.bfloat16)
    named = matmul(names[...].astype(jnp.bfloat16), pick, NT)
    named = jnp.concatenate([named, jnp.zeros_like(named)], axis=0).astype(jnp.bfloat16)
    high[ROOM - LOW :, :LOW] = low[LOW:, :LOW]
    high[ROOM - LOW :, LOW:BLOCK] = named
    high[ROOM - LOW :, BLOCK:] = jnp.zeros((16, FEAT - BLOCK), jnp.bfloat16)


def over_kernel(arrived, over):
    one = ((iota((128, HELD), 0) * SHARE) == iota((128, HELD), 1)).astype(jnp.bfloat16)
    counts = matmul(one, arrived[:, FEAT:], NN).astype(jnp.int32)
    counts = jnp.where(iota((128, 128), 1) >= 64, counts, 0)
    turned = iota((128, 128), 0) & (MEMBERS - 1)
    most = jnp.zeros((1, 128), jnp.int32)
    for k in range(MEMBERS):
        gets = (counts + (MEMBERS - 1) - ((k - turned) & (MEMBERS - 1))) >> 4
        most = jnp.maximum(most, jnp.sum(gets, axis=0, keepdims=True))
    over[...] = jnp.broadcast_to((most > ROOM).astype(jnp.int32), (8, 128))


def column_fold(x, op):
    while x.shape[0] > 8:
        half = x.shape[0] // 16 * 8
        rest = x[2 * half :]
        x = op(x[:half], x[half : 2 * half])
        if rest.shape[0]:
            x = jnp.concatenate([op(x[:8], rest), x[8:]], axis=0) if half > 8 else op(x, rest)
    return x


LOWS = ((0, 256),)
HIGHS = ((256, 256), (512, SENT - 512))
PARTS = LOWS + HIGHS
TALL = ((0, 256), (256, SENT - 256))


def clear(state):
    col_best, col_mass, row_best, row_mass = state[:4]
    for ref in (col_best, row_best):
        ref[...] = jnp.full_like(ref, APART)
    for ref in (col_mass, row_mass):
        ref[...] = jnp.zeros_like(ref)


def names_of(block):
    part = block[0] if block[1] is None else block[1]
    return part[part.shape[0] - 16 :, :BLOCK].astype(jnp.float32)


def spell(block, place, state):
    clusters = names_of(block)[0:1]
    clusters = jnp.where(clusters > 0.0, clusters, -1.0)
    for t in range(0, BLOCK, 128):
        here = slice(t, t + 128)
        state[4][place, here, :] = jnp.broadcast_to(clusters[:, here], (128, 128)).T


def part_of(block, first, size):
    if first < LOW:
        return block[0][first : first + size, :]
    return block[1][first - LOW : first - LOW + size, :]


def square(rows, cols, place, c, r, state, own=False, downs=PARTS, parts=PARTS):
    col_best, col_mass, row_best, row_mass, spelt = state
    clusters = names_of(cols)[0:1]
    if downs is PARTS and not own:
        downs = TALL
    for i, tall in downs:
        for j, wide in parts:
            product = matmul(part_of(rows, i, tall), part_of(cols, j, wide), NT)
            down = slice(i, i + tall)
            tops = sums = None
            for t in range(0, wide, 128):
                size = min(128, wide - t)
                across = slice(j + t, j + t + size)
                match = spelt[place, down, :size] == clusters[:, across]
                if own and i == j:
                    match = match & (iota((tall, size), 0) != iota((tall, size), 1) + t)
                score = jnp.where(match, product[:, t : t + size], APART)
                soft = jnp.exp2((score - 1.0) * (sharpness * LOG2E))
                col_best[c, :, across] = jnp.maximum(
                    col_best[c, :, across], column_fold(score, jnp.maximum)
                )
                col_mass[c, :, across] = col_mass[c, :, across] + column_fold(soft, jnp.add)
                tops = score if tops is None else jnp.maximum(tops, score)
                sums = soft if sums is None else sums + soft
            if r is not None:
                size = tops.shape[1]
                row_best[r, down, :size] = jnp.maximum(row_best[r, down, :size], tops)
                row_mass[r, down, :size] = row_mass[r, down, :size] + sums


def settle(e, state):
    col_best, col_mass, row_best, row_mass = state[:4]
    best = jnp.max(col_best[e], axis=0, keepdims=True)
    mass = jnp.sum(col_mass[e], axis=0, keepdims=True)
    if e in ROW_BLOCKS:
        r = ROW_BLOCKS.index(e)
        tops, sums = [], []
        for t in range(0, BLOCK, 128):
            tops.append(jnp.max(row_best[r, t : t + 128, :].T, axis=0, keepdims=True))
            sums.append(jnp.sum(row_mass[r, t : t + 128, :].T, axis=0, keepdims=True))
        best = jnp.maximum(best, jnp.concatenate(tops, axis=1))
        mass = mass + jnp.concatenate(sums, axis=1)
    return best, mass


def store(blocks, best_in, mass_in, best_out, mass_out, state):
    if best_in is None:
        best_out[...] = jnp.full_like(best_out, APART)
        mass_out[...] = jnp.zeros_like(mass_out)
    else:
        best_out[...] = best_in[...]
        mass_out[...] = mass_in[...]
    for e in blocks:
        here = slice(e, e + 1)
        best, mass = settle(e, state)
        best_out[here, :] = jnp.maximum(best_out[here, :], best)
        mass_out[here, :] = mass_out[here, :] + mass


def early_kernel(b0l, b0h, b1l, b1h, b2l, b2h, best_out, mass_out, *state):
    b0, b1, b2 = (b0l, b0h), (b1l, b1h), (b2l, b2h)
    clear(state)
    for place, block in enumerate((b0, b1, b2)):
        spell(block, place, state)
    square(b0, b0, 0, 0, None, state, True)
    square(b1, b0, 1, 0, 0, state)
    square(b1, b2, 1, 2, 0, state)
    square(b2, b0, 2, 0, 1, state)
    store((0, 1, 2), None, None, best_out, mass_out, state)


def middle_kernel(
    b0l, b1l, b1h, b2l, b2h, b3l, b4l, low, high, best_in, mass_in, best_out, mass_out, *state
):
    b0, b1, b2, b3, b4 = (b0l, None), (b1l, b1h), (b2l, b2h), (b3l, None), (b4l, None)
    low, high = (low, None), (None, high)
    clear(state)
    for place, block in enumerate((b0, b1, b2, b4)):
        spell(block, place, state)
    square(b1, low, 1, 5, 0, state, parts=LOWS)
    square(b2, high, 2, 6, 1, state, parts=HIGHS)
    square(b1, high, 1, 6, 0, state, downs=LOWS, parts=HIGHS)
    square(b1, high, 1, 6, None, state, downs=HIGHS, parts=HIGHS)
    square(b2, low, 2, 5, 1, state, downs=HIGHS, parts=LOWS)
    square(b2, low, 2, 5, None, state, downs=LOWS, parts=LOWS)
    square(b0, b3, 0, 3, None, state, downs=LOWS, parts=LOWS)
    square(b1, b4, 1, 4, 0, state, parts=LOWS)
    square(b2, b3, 2, 3, 1, state, parts=LOWS)
    square(b4, b3, 3, 3, None, state, downs=LOWS, parts=LOWS)
    store((1, 2, 3, 4, 5, 6), best_in, mass_in, best_out, mass_out, state)


def late_kernel(
    b0h, b1l, b1h, b2l, b2h, b3l, b3h, b4l, b4h, low, high, best_in, mass_in, out, *state
):
    b0, b1, b2, b3, b4 = (None, b0h), (b1l, b1h), (b2l, b2h), (b3l, b3h), (b4l, b4h)
    low, high = (low, None), (None, high)
    clear(state)
    for place, block in enumerate((b0, b1, b2, b4)):
        spell(block, place, state)
    square(b0, b4, 0, 4, None, state, downs=HIGHS, parts=HIGHS)
    square(b1, b4, 1, 4, 0, state, parts=HIGHS)
    square(b2, b3, 2, 3, 1, state, parts=HIGHS)
    square(b4, b3, 3, 3, None, state, parts=HIGHS)
    square(b4, b3, 3, 3, None, state, downs=HIGHS, parts=LOWS)
    source_at = (iota((DEVICES, BLOCK), 0) + 1).astype(jnp.float32)
    line = iota((16, BLOCK), 0)
    back = []
    for e, block in enumerate((b0, b1, b2, b3, b4, low, high)):
        here = slice(e, e + 1)
        best, mass = jnp.maximum(best_in[here, :], -1.0), mass_in[here, :]
        if e in (1, 2, 3, 4):
            more, extra = settle(e, state)
            best = jnp.maximum(best, more)
            mass = mass + extra
        best = best + SHIFT
        names = names_of(block)
        if e == 5:
            names = jnp.where(iota(names.shape, 1) < LOW, names, 0.0)
        if e == 6:
            names = jnp.where(iota(names.shape, 1) >= LOW, names, 0.0)
        values = jnp.where((line & 1) == 0, best, mass)
        values = jnp.where((line >> 1).astype(jnp.float32) == names[2:3], values, 0.0)
        to = (source_at == names[1:2]).astype(jnp.bfloat16)
        back.append(joined(matmul(split(values), to, NT)))
    back.append(jnp.zeros((128 - 16 * len(back), DEVICES), jnp.float32))
    out[...] = jnp.concatenate(back, axis=0).T


def finish_kernel(arrived, places, best_out, mass_out):
    shape = (DEVICES, DEVICES)
    at, col = iota(shape, 0), iota(shape, 1)
    base, ay, az = at >> 4, (at >> 2) & 3, at & 3
    turned = (base & 1) == 1
    best = mass = None
    pieces = split(arrived[...].T)
    for e, (dy, dz) in enumerate(SPOTS):
        by = (ay + jnp.where(turned, dz, (-dy) & 3)) & 3
        bz = (az + jnp.where(turned, dy, (-dz) & 3)) & 3
        move = (col == base * MEMBERS + by * 4 + bz).astype(jnp.bfloat16)
        part = jnp.concatenate(
            [pieces[128 * p + 16 * e : 128 * p + 16 * e + 16] for p in range(3)], axis=0
        )
        moved = joined(matmul(part, move, NT))
        best = moved if best is None else jnp.maximum(best, moved)
        mass = moved if mass is None else mass + moved
    merged = jnp.where((iota((16, DEVICES), 0) & 1) == 0, best, mass)
    holder = (iota((DEVICES, ROWS), 0) == places[0:1, :]).astype(jnp.bfloat16)
    picked = joined(matmul(split(merged), holder, NN))
    line = iota((16, ROWS), 0)
    turn = places[1:2, :]
    best = jnp.sum(jnp.where(line == 2 * turn, picked, 0.0), axis=0, keepdims=True)
    best_out[...] = best - SHIFT
    mass = jnp.sum(jnp.where(line == 2 * turn + 1, picked, 0.0), axis=0, keepdims=True)
    mass_out[...] = jnp.log1p(mass)


def call(kernel, out_shape, scratch=(), flops=0, name=None):
    return pl.pallas_call(
        kernel,
        out_shape=out_shape,
        scratch_shapes=scratch,
        compiler_params=pltpu.CompilerParams(vmem_limit_bytes=VMEM_LIMIT),
        cost_estimate=pl.CostEstimate(flops=flops, bytes_accessed=8_000_000, transcendentals=0),
        name=name,
    )


def hop(dy, dz):
    pairs = []
    for g in range(GROUPS):
        up, along = (-dz, -dy) if g & 1 else (dy, dz)
        for y in range(4):
            for z in range(4):
                source = ((y + up) % 4) * 4 + (z + along) % 4
                pairs.append((g * MEMBERS + source, g * MEMBERS + y * 4 + z))
    return pairs


def from_spot(x, dy, dz):
    return lax.ppermute(x, AXES, hop(dy, dz))


def fast(embeddings, labels, cluster_slot):
    f32, bf16, i32 = jnp.float32, jnp.bfloat16, jnp.int32
    shape = jax.ShapeDtypeStruct
    spread, places = call(
        prelude_kernel,
        (shape((HELD, WIDE), bf16), shape((8, ROWS), i32)),
        flops=3_000_000_000,
        name="prelude",
    )(labels.reshape(1, ROWS), cluster_slot.reshape(1, ROWS), embeddings)
    arrived = lax.all_to_all(spread, AXES, split_axis=0, concat_axis=0, tiled=True)
    b0l, position, names = call(
        pack_low_kernel,
        (shape((LOW_SENT, FEAT), bf16), shape((8, HELD), i32), shape((8, HELD), f32)),
        flops=2_000_000_000,
        name="pack_low",
    )(arrived)
    b0h = call(
        pack_high_kernel, shape((HIGH_SENT, FEAT), bf16), flops=1_000_000_000, name="pack_high"
    )(arrived, b0l, position, names)
    b1l = from_spot(b0l, 1, 0)
    b2l = from_spot(b0l, 0, 1)
    b1h = from_spot(b0h, 1, 0)
    b2h = from_spot(b0h, 0, 1)
    high, b1l, b2l = lax.optimization_barrier((b0h, b1l, b2l))
    high = from_spot(high, 3, 0)
    b3l = from_spot(b1l, 1, 0)
    b4l = from_spot(b2l, 0, 1)
    low, b1h, b2h = lax.optimization_barrier((b0l, b1h, b2h))
    over = call(over_kernel, shape((8, 128), i32), flops=10_000_000, name="over")(arrived)
    b4h = from_spot(b2h, 0, 1)
    b3h = from_spot(b1h, 1, 0)
    low = from_spot(low, 0, 3)

    def state(places):
        return (
            pltpu.VMEM((7, 8, BLOCK), f32),
            pltpu.VMEM((7, 8, BLOCK), f32),
            pltpu.VMEM((2, BLOCK, 128), f32),
            pltpu.VMEM((2, BLOCK, 128), f32),
            pltpu.VMEM((places, BLOCK, 128), f32),
        )

    stats = (shape((8, BLOCK), f32), shape((8, BLOCK), f32))
    best, mass = call(
        early_kernel, stats, scratch=state(3), flops=6_000_000_000, name="early"
    )(b0l, b0h, b1l, b1h, b2l, b2h)
    best, mass = call(
        middle_kernel, stats, scratch=state(4), flops=1_500_000_000, name="middle"
    )(b0l, b1l, b1h, b2l, b2h, b3l, b4l, low, high, best, mass)
    message = call(
        late_kernel,
        shape((DEVICES, 128), f32),
        scratch=state(4),
        flops=3_000_000_000,
        name="late",
    )(b0h, b1l, b1h, b2l, b2h, b3l, b3h, b4l, b4h, low, high, best, mass)
    answer = lax.all_to_all(message, AXES, split_axis=0, concat_axis=0, tiled=True)
    best, mass = call(
        finish_kernel,
        (shape((1, ROWS), f32), shape((1, ROWS), f32)),
        flops=ROWS * ROWS * 128,
        name="finish",
    )(answer, places)
    return (best.reshape(ROWS), mass.reshape(ROWS)), jnp.max(over)


def general(embeddings, labels, cluster_slot):
    groups = lax.axis_size("grp")
    members = lax.axis_size("blk")
    row_count, feature_count = embeddings.shape
    capacity = row_count // 4
    held = groups * capacity
    widened = embeddings.astype(jnp.float32)
    units = (
        widened * lax.rsqrt(jnp.sum(widened * widened, axis=1, keepdims=True) + epsilon)
    ).astype(jnp.bfloat16)
    slot_ids = cluster_slot[labels]
    owner_group = slot_ids // (cluster_slot.shape[0] // groups)
    owner_onehot = (owner_group[:, None] == jnp.arange(groups, dtype=jnp.int32)[None, :]).astype(
        jnp.int32
    )
    earlier = jnp.cumsum(owner_onehot, axis=0) - owner_onehot
    send_place = owner_group * capacity + jnp.sum(earlier * owner_onehot, axis=1)
    outgoing = jnp.zeros((held, feature_count), jnp.bfloat16).at[send_place].set(units)
    outgoing_slots = jnp.full((held,), -1, jnp.int32).at[send_place].set(slot_ids)
    rows = lax.all_to_all(outgoing, "grp", split_axis=0, concat_axis=0, tiled=True)
    slots = lax.all_to_all(outgoing_slots, "grp", split_axis=0, concat_axis=0, tiled=True)
    ring = [(i, (i + 1) % members) for i in range(members)]
    local = jnp.arange(held, dtype=jnp.int32)
    place = lax.axis_index("blk")
    own_ids = place * held + local

    def step(turn, carry):
        key_rows, key_slots, best, mass = carry
        scores = jnp.einsum("qd,kd->qk", rows, key_rows, preferred_element_type=jnp.float32)
        matched = (slots[:, None] == key_slots[None, :]) & (key_slots[None, :] >= 0)
        owner = (place - turn) & (members - 1)
        matched = matched & (own_ids[:, None] != (owner * held + local)[None, :])
        best = jnp.maximum(best, jnp.max(jnp.where(matched, scores, -1.0), axis=1))
        mass = mass + jnp.sum(
            jnp.where(matched, jnp.exp(sharpness * (scores - 1.0)), 0.0), axis=1
        )
        key_rows = lax.ppermute(key_rows, "blk", ring)
        key_slots = lax.ppermute(key_slots, "blk", ring)
        return key_rows, key_slots, best, mass

    start = (
        rows,
        slots,
        jnp.full((held,), -1.0, jnp.float32),
        jnp.zeros((held,), jnp.float32),
    )
    _, _, best, mass = lax.fori_loop(0, members, step, start)
    best = lax.all_to_all(best, "grp", split_axis=0, concat_axis=0, tiled=True)
    mass = lax.all_to_all(mass, "grp", split_axis=0, concat_axis=0, tiled=True)
    return (best[send_place], jnp.log1p(mass[send_place]))


def body(embeddings, labels, cluster_slot):
    result, over = fast(embeddings, labels, cluster_slot)
    return lax.cond(
        over > 0, lambda: general(embeddings, labels, cluster_slot), lambda: result
    )


def solution(mesh):
    placed = (P(AXES, None), P(AXES), P())
    return jax.shard_map(
        body,
        mesh=mesh,
        in_specs=placed,
        out_specs=(P(AXES), P(AXES)),
        check_vma=False,
    )
```
